32 devices in a mesh: row: 8 (over z, x), col: 4 (over y, core).
Axes of the slice: x: 2, y: 2, z: 4, core: 2. Of those that a mesh axis runs over, the one named last changes fastest.
Arguments:
- tile_values: bfloat16 [8, 4, 360, 128, 128], P('row', 'col')
- tile_places: int32 [8, 4, 2, 360], P('row', 'col'), may hold values from 0 to 47, as said below
- tile_counts: int32 [8, 4], P('row', 'col'), may hold values from 90 to 360, as said below
- sketch: bfloat16 [24576, 512], P('col'), may hold values from -6 to 6
Outputs:
- range_basis: float32 [24576, 512], P(('row', 'col'))
- triangle: float32 [512, 512], replicated
The draws below stay inside these ranges and needn't reach their ends.
Inputs may be any that keep to these rules, and one draw needn't show every extreme that they name: `tile_places`: entry [r, c, 0, t] is the slot's tile row among the 24 tile rows of row block r and entry [r, c, 1, t] its tile column among the 48 tile columns of column block c; the 360 slots of one block pair name distinct positions, padded slots included. Slots t < tile_counts[r, c] hold the live tiles of block pair (r, c); later slots are padding and contribute nothing. Some block pair holds exactly 360 live tiles.
All inputs are finite; a program needn't handle non-finite values.
Results may differ from the reference program's by a relative error of at most 0.0003.
Values sent between devices are 32-bit elements; how exact they have to be, the bound alone decides.
No kernel may reach another device: no remote copies, remote signals or barrier semaphores. Data moves between devices by JAX's collectives and lax.ppermute only.
A program may use at most 192 MiB of HBM per device.

```python
import math
import jax
import jax.numpy as jnp
from jax import lax

TILE = 128
K = 512
TMAX = 360
ROW_BLOCKS = 8
COL_BLOCKS = 4
TROWS = 24
TCOLS = 48
NORDER = 24576


def draw_tile_values(key, part):
    keys = jax.random.split(key, 2)
    full_shape = (ROW_BLOCKS, COL_BLOCKS, TMAX, TILE, TILE)
    entries = jax.random.normal(keys[0], full_shape, jnp.float32)
    growth = 3.0
    row_spread = jnp.exp(jax.random.uniform(keys[1], (ROW_BLOCKS, COL_BLOCKS, TMAX, TILE, 1), jnp.float32, -1.15, 1.15))
    block_growth = growth ** (jnp.arange(ROW_BLOCKS, dtype=jnp.float32) / max(ROW_BLOCKS - 1, 1))
    fan_total = TILE * (COL_BLOCKS * TMAX // (2 * TROWS) + 1)
    values = entries * row_spread * (block_growth[:, None, None, None, None] / math.sqrt(fan_total))
    return values.astype(jnp.bfloat16)


def draw_tile_places(key, part):
    keys = jax.random.split(key, ROW_BLOCKS * COL_BLOCKS)

    def pick_slots(one_key):
        return jax.random.permutation(one_key, TROWS * TCOLS)[:TMAX].astype(jnp.int32)
    chosen = jax.vmap(pick_slots)(keys).reshape(ROW_BLOCKS, COL_BLOCKS, TMAX)
    return jnp.stack([chosen // TCOLS, chosen % TCOLS], axis=2).astype(jnp.int32)


def draw_tile_counts(key, part):
    keys = jax.random.split(key, 2)
    low_count = TMAX // 4
    span_count = TMAX - low_count
    raw_draw = jax.random.randint(keys[0], (ROW_BLOCKS * COL_BLOCKS,), 0, span_count + 1, dtype=jnp.int32)
    counted = low_count + raw_draw * raw_draw // span_count
    busiest = jax.random.randint(keys[1], (), 0, ROW_BLOCKS * COL_BLOCKS, dtype=jnp.int32)
    counted = counted.at[busiest].set(TMAX)
    return counted.reshape(ROW_BLOCKS, COL_BLOCKS).astype(jnp.int32)


def shard_levels(own_key, dims, shards, least, largest):
    level, own = 1.0, jax.random.fold_in(own_key, 6)
    for dim, shards_of in shards:
        steps = jnp.exp(jax.random.uniform(jax.random.fold_in(own, dim), (shards_of,), jnp.float32, least / len(shards), largest / len(shards)))
        level = level * jnp.repeat(steps, dims[dim] // shards_of).reshape([-1 if axis == dim else 1 for axis in range(len(dims))])
    return level


def bell_draw(rng, extent, scale, reach, pieces=(), held_as=jnp.bfloat16):
    gain = shard_levels(rng, extent, pieces, -0.22, 0.18) if pieces else 1.0
    result = jax.random.normal(rng, extent, jnp.float32) * scale * gain
    return jnp.minimum(jnp.maximum(result, -reach), reach).astype(held_as)


def setup_inputs(seed: int = 0) -> dict:
    streams_of = jax.random.split(jax.random.key(seed), 5)
    return {
        "tile_values": draw_tile_values(jax.random.fold_in(streams_of[4], 71), 0),
        "tile_places": draw_tile_places(jax.random.fold_in(streams_of[4], 71), 0),
        "tile_counts": draw_tile_counts(jax.random.fold_in(streams_of[4], 71), 0),
        "sketch": bell_draw(streams_of[3], (NORDER, K), 1.0, 6.0, ((0, 4),)),
    }


def reference(tile_values, tile_places, tile_counts, sketch):
    panels = sketch.reshape(COL_BLOCKS, TCOLS, TILE, K)

    def row_block(block_row):

        def add_column(partial_value, block_col):
            tile_stack = tile_values[block_row, block_col]
            places = tile_places[block_row, block_col]
            live_mask = jnp.arange(TMAX, dtype=jnp.int32) < tile_counts[block_row, block_col]
            picked = panels[block_col][places[1]]
            products = jnp.einsum('tab,tbk->tak', tile_stack.astype(jnp.float32), picked.astype(jnp.float32), precision=lax.Precision.HIGHEST)
            products = jnp.where(live_mask[:, None, None], products, jnp.zeros_like(products))
            return (partial_value + jax.ops.segment_sum(products, places[0], num_segments=TROWS), None)
        partial_value, unused = lax.scan(add_column, jnp.zeros((TROWS, TILE, K), jnp.float32), jnp.arange(COL_BLOCKS, dtype=jnp.int32))
        return partial_value.reshape(TROWS * TILE, K)
    sketched = lax.map(row_block, jnp.arange(ROW_BLOCKS, dtype=jnp.int32)).reshape(NORDER, K)
    gram = jnp.dot(sketched.T.astype(jnp.float32), sketched.astype(jnp.float32), precision=lax.Precision.HIGHEST, preferred_element_type=jnp.float32)
    lower = jnp.linalg.cholesky(gram)
    order_scale = jnp.sqrt(jnp.float32(NORDER))
    basis_t = jax.scipy.linalg.solve_triangular(lower, sketched.T, lower=True)
    return (basis_t.T * order_scale, lower.T / order_scale)
```

```python
import functools
import math

import jax
import jax.numpy as jnp
from jax import lax
from jax.experimental import pallas as pl
from jax.experimental.pallas import tpu as pltpu
from jax.sharding import PartitionSpec as P

BF16 = jnp.bfloat16
F32 = jnp.float32
PAIR = 2
TURN = 8
CHUNKS = 3
BLOCK = 128
LIMIT = 56 << 20
SMEM = pl.BlockSpec(memory_space=pltpu.SMEM)
VMEM = pl.BlockSpec(memory_space=pltpu.VMEM)
ANY = pl.BlockSpec(memory_space=pl.ANY)
PARAMS = pltpu.CompilerParams(vmem_limit_bytes=LIMIT)


def halves(x):
    high = x.astype(BF16)
    return high, (x - high.astype(F32)).astype(BF16)


def tile_kernel(resident, groups, chunks, meta, places, tiles, panels, *refs):
    outs = refs[: 2 * chunks]
    acc, tile_buf, panel_buf, key, fill, slot, column, target, sems = refs[2 * chunks :]
    slots = tiles.shape[0]
    blocks = acc.shape[0]
    per_owner = blocks // 2
    tile_copy = pltpu.make_async_copy(tiles, tile_buf.at[pl.ds(0, slots)], sems.at[0])
    tile_copy.start()
    if resident:
        panel_copy = pltpu.make_async_copy(panels, panel_buf, sems.at[1])
        panel_copy.start()
    live, own, flip = meta[0], meta[1], meta[2]

    def clear(k, carry):
        fill[k] = 0
        return carry

    lax.fori_loop(0, blocks + 1, clear, 0)

    def name_row(r, carry):
        owner = r // per_owner
        inside = r % per_owner
        base = jnp.where((owner & 1) == (own & 1), per_owner, 0)
        wanted = (owner >> 1) == ((own >> 1) ^ flip)
        key[r] = jnp.where(wanted, base + inside, blocks)
        return carry

    lax.fori_loop(0, key.shape[0], name_row, 0)

    def count(t, carry):
        k = key[places[0, t]]
        fill[k] = fill[k] + 1
        return carry

    lax.fori_loop(0, live, count, 0)

    def prefix(k, total):
        size = (fill[k] + PAIR - 1) // PAIR * PAIR
        fill[k] = total
        return total + size

    total = lax.fori_loop(0, blocks, prefix, 0)
    turns = (total + PAIR * TURN - 1) // (PAIR * TURN)
    fill[blocks] = groups

    def blank(p, carry):
        slot[p] = slots
        column[p] = 0
        target[p // PAIR] = 0
        return carry

    lax.fori_loop(0, turns * PAIR * TURN, blank, 0)

    def put(t, carry):
        k = key[places[0, t]]
        p = fill[k]
        fill[k] = p + 1
        slot[p] = t
        column[p] = places[1, t]
        target[p // PAIR] = k
        return carry

    lax.fori_loop(0, live, put, 0)
    acc[...] = jnp.zeros_like(acc)
    tile_buf[slots] = jnp.zeros_like(tile_buf[slots])
    tile_copy.wait()
    if resident:
        panel_copy.wait()

    def turn(g, carry):
        first = g * (PAIR * TURN)
        if not resident:
            copies = [
                pltpu.make_async_copy(
                    panels.at[column[first + i]], panel_buf.at[i], sems.at[1 + i]
                )
                for i in range(PAIR * TURN)
            ]
            for copy in copies:
                copy.start()
            for copy in copies:
                copy.wait()
        for i in range(TURN):
            at = first + i * PAIR
            left = jnp.concatenate([tile_buf[slot[at + j]] for j in range(PAIR)], axis=1)
            right = jnp.concatenate(
                [
                    panel_buf[column[at + j] if resident else i * PAIR + j]
                    for j in range(PAIR)
                ],
                axis=0,
            )
            k = target[g * TURN + i]
            acc[k] += jnp.dot(left, right, preferred_element_type=F32)
        return carry

    lax.fori_loop(0, turns, turn, 0)
    size = per_owner // chunks
    copies = [
        pltpu.make_async_copy(acc.at[pl.ds(n * size, size)], outs[n], sems.at[n])
        for n in range(2 * chunks)
    ]
    for copy in copies:
        copy.start()
    for copy in copies:
        copy.wait()


def tile_products(meta, places, tiles, panels, tile_rows, owners, chunks):
    slots, size, _ = tiles.shape
    width = panels.shape[2]
    blocks = tile_rows // owners * 2
    step = PAIR * TURN
    groups = (slots + blocks * (PAIR - 1) + step - 1) // step * step
    resident = panels.size * 2 <= 16 << 20
    piece = jax.ShapeDtypeStruct((blocks // 2 // chunks, size, width), F32)
    return pl.pallas_call(
        functools.partial(tile_kernel, resident, groups, chunks),
        out_shape=[piece] * (2 * chunks),
        in_specs=[SMEM, SMEM, ANY, ANY],
        out_specs=[ANY] * (2 * chunks),
        scratch_shapes=[
            pltpu.VMEM((blocks, size, width), F32),
            pltpu.VMEM((slots + 1, size, size), BF16),
            pltpu.VMEM((panels.shape[0] if resident else step, size, width), BF16),
            pltpu.SMEM((tile_rows,), jnp.int32),
            pltpu.SMEM((blocks + 1,), jnp.int32),
            pltpu.SMEM((groups + slots,), jnp.int32),
            pltpu.SMEM((groups + slots,), jnp.int32),
            pltpu.SMEM(((groups + slots) // PAIR + 1,), jnp.int32),
            pltpu.SemaphoreType.DMA((max(2, 2 * chunks, 1 if resident else 1 + step),)),
        ],
        compiler_params=PARAMS,
        cost_estimate=pl.CostEstimate(
            flops=slots * size * size * width,
            bytes_accessed=tiles.size * 2 + panels.size * 2,
            transcendentals=0,
        ),
    )(meta, places, tiles, panels)


def block_list(order):
    return [(i, j) for i in range(order) for j in range(i + 1)]


def gram_kernel(last, meta, *refs):
    if last:
        keep, core, across, *earlier, rows, mine, other, acc = refs
    else:
        keep, core, across, rows, acc = refs
    total = (keep[...] + core[...]) + across[...]
    total = total.reshape(rows.shape)
    rows[...] = total
    high, low = halves(total)
    left = jnp.concatenate([high, high, low], axis=0)
    right = jnp.concatenate([high, low, high], axis=0)
    order = rows.shape[1] // BLOCK
    for i in range(order):
        strip = lax.dot_general(
            left[:, i * BLOCK : (i + 1) * BLOCK],
            right[:, : (i + 1) * BLOCK],
            (((0,), (0,)), ((), ())),
            preferred_element_type=F32,
        )
        for j in range(i + 1):
            n = i * (i + 1) // 2 + j
            part = strip[:, j * BLOCK : (j + 1) * BLOCK]
            if last:
                for gram in earlier:
                    part = part + gram[n]
            acc[n] = part
    if last:
        core_bit = meta[1] & 1
        half = acc.shape[0] // 2
        mine[...] = acc[pl.ds(core_bit * half, half)]
        other[...] = acc[pl.ds((1 - core_bit) * half, half)]


def gram_chunk(meta, keep, core, across, earlier, last):
    width = keep.shape[2]
    rows = keep.shape[0] * keep.shape[1]
    number = len(block_list(width // BLOCK))
    whole = jax.ShapeDtypeStruct((number, BLOCK, BLOCK), F32)
    half = jax.ShapeDtypeStruct((number // 2, BLOCK, BLOCK), F32)
    row_shape = jax.ShapeDtypeStruct((rows, width), F32)
    args = [meta, keep, core, across] + (list(earlier) if last else [])
    outs = [row_shape] + ([half, half] if last else [whole])
    return pl.pallas_call(
        functools.partial(gram_kernel, last),
        out_shape=outs,
        in_specs=[SMEM] + [VMEM] * (len(args) - 1),
        out_specs=[VMEM] * len(outs),
        scratch_shapes=[pltpu.VMEM(whole.shape, F32)] if last else [],
        compiler_params=PARAMS,
        cost_estimate=pl.CostEstimate(
            flops=4 * rows * width * width, bytes_accessed=rows * width * 16, transcendentals=0
        ),
    )(*args)


def pack_kernel(meta, mine, theirs, *refs):
    outs, total = refs[:-1], refs[-1]
    total[...] = mine[...].reshape(total.shape) + theirs[...].reshape(total.shape)
    me = meta[3]
    for d, out in enumerate(outs):
        out[...] = total[me ^ d]


def pack(meta, mine, theirs, pieces):
    size = mine.shape[0] * mine.shape[1] // pieces
    shape = (size, mine.shape[2])
    return pl.pallas_call(
        pack_kernel,
        out_shape=[jax.ShapeDtypeStruct(shape, F32)] * pieces,
        in_specs=[SMEM, VMEM, VMEM],
        out_specs=[VMEM] * pieces,
        scratch_shapes=[pltpu.VMEM((pieces, *shape), F32)],
        compiler_params=PARAMS,
    )(meta, mine, theirs)


def unpack_kernel(meta, *refs):
    out = refs[-1]
    me = meta[3]
    for d, piece in enumerate(refs[:-1]):
        out[me ^ d] = piece[...]


def unpack(meta, pieces):
    return pl.pallas_call(
        unpack_kernel,
        out_shape=jax.ShapeDtypeStruct((len(pieces), *pieces[0].shape), F32),
        in_specs=[SMEM] + [VMEM] * len(pieces),
        out_specs=VMEM,
        compiler_params=PARAMS,
    )(meta, *pieces)


def swapped(x, row_flip, col_flip):
    rows, cols = lax.axis_size("row"), lax.axis_size("col")
    if not row_flip:
        return lax.ppermute(x, "col", [(c, c ^ col_flip) for c in range(cols)])
    if not col_flip:
        return lax.ppermute(x, "row", [(r, r ^ row_flip) for r in range(rows)])
    route = [
        (r * cols + c, (r ^ row_flip) * cols + (c ^ col_flip))
        for r in range(rows)
        for c in range(cols)
    ]
    return lax.ppermute(x, ("row", "col"), route)


FLIPS = ((1, 0), (0, 2), (1, 2))


def gram_sum(meta, mine, other):
    theirs = swapped(other, 0, 1)
    own, *sends = pack(meta, mine, theirs, 4)
    got = [swapped(x, *flip) for x, flip in zip(sends, FLIPS)]
    piece = (own + got[0]) + (got[1] + got[2])
    bits = lax.axis_size("row").bit_length() - 1
    bit = 1
    while bit < bits:
        if bit + 1 < bits:
            a, b = 1 << bit, 2 << bit
            got = [swapped(piece, flip, 0) for flip in (a, b, a | b)]
            piece = (piece + got[0]) + (got[1] + got[2])
            bit += 2
        else:
            piece = piece + swapped(piece, 1 << bit, 0)
            bit += 1
    got = [swapped(piece, *flip) for flip in FLIPS]
    half = unpack(meta, [piece, *got])
    return half, swapped(half, 0, 1)


def against(left, right_rows):
    lh, ll = left
    rh, rl = right_rows
    return lax.dot_general(
        jnp.concatenate([lh, lh, ll], axis=1),
        jnp.concatenate([rh, rl, rh], axis=1),
        (((1,), (1,)), ((), ())),
        preferred_element_type=F32,
    )


def times(left, right):
    lh, ll = left
    rh, rl = right
    return jnp.dot(
        jnp.concatenate([lh, lh, ll], axis=1),
        jnp.concatenate([rh, rl, rh], axis=0),
        preferred_element_type=F32,
    )


def factor_kernel(chunks, scale, rounds, meta, mine, theirs, *refs):
    rows = refs[:chunks]
    basis, triangle, gram_out, flag, blocks, gram, w, wh, wl, gh, gl, yh, yl, ph = refs[chunks:]
    size = gram.shape[0]
    order = size // BLOCK
    core_bit = meta[1] & 1
    half = blocks.shape[0] // 2
    blocks[pl.ds(core_bit * half, half)] = mine[...].reshape(half, BLOCK, BLOCK)
    blocks[pl.ds((1 - core_bit) * half, half)] = theirs[...].reshape(half, BLOCK, BLOCK)
    at = [slice(i * BLOCK, (i + 1) * BLOCK) for i in range(order)]
    for n, (i, j) in enumerate(block_list(order)):
        if i == j:
            gram[at[i], at[j]] = blocks[n]
        else:
            gram[at[i], at[j]] = blocks[n]
            gram[at[j], at[i]] = blocks[n].T
    high, low = halves(gram[...])
    gh[...] = high
    gl[...] = low
    gram_out[...] = gram[...]

    def index(i):
        shape = (BLOCK, size)
        return (
            lax.broadcasted_iota(jnp.int32, shape, 0) + i * BLOCK,
            lax.broadcasted_iota(jnp.int32, shape, 1),
        )

    def phi(error, i):
        r, c = index(i)
        r, c = r[:, : error.shape[1]], c[:, : error.shape[1]]
        return jnp.where(r > c, error, jnp.where(r == c, 0.5 * error, 0.0))

    row_scale, col_scale = [], []
    for i in range(order):
        block = gram[at[i], at[i]]
        r, c = index(0)
        diagonal = jnp.where(r[:, :BLOCK] == c[:, :BLOCK], block, 0.0)
        row_scale.append(lax.rsqrt(jnp.sum(diagonal, axis=1, keepdims=True)))
        col_scale.append(lax.rsqrt(jnp.sum(diagonal, axis=0, keepdims=True)))
    col_scale = jnp.concatenate(col_scale, axis=1)
    for i in range(order):
        r, c = index(i)
        same = jnp.where(r == c, 1.0, 0.0)
        error = gram[at[i], :] * row_scale[i] * col_scale - same
        w[at[i], :] = (same - phi(error, i)) * col_scale

    def split_w():
        for i in range(order):
            high, low = halves(w[at[i], :])
            wh[at[i], :] = high
            wl[at[i], :] = low

    def step(exact):
        split_w()
        for i in range(order):
            if exact:
                y = against((gh[at[i], :], gl[at[i], :]), (wh[...], wl[...]))
            else:
                y = lax.dot_general(
                    gh[at[i], :], wh[...], (((1,), (1,)), ((), ())), preferred_element_type=F32
                )
            high, low = halves(y)
            yh[at[i], :] = high
            yl[at[i], :] = low
        norm = jnp.zeros((1, 1), F32)
        for i in range(order):
            k = (i + 1) * BLOCK
            if exact:
                m = times((wh[at[i], :k], wl[at[i], :k]), (yh[:k, :k], yl[:k, :k]))
            else:
                m = jnp.dot(wh[at[i], :k], yh[:k, :k], preferred_element_type=F32)
            r, c = index(i)
            p = phi(m - jnp.where(r[:, :k] == c[:, :k], 1.0, 0.0), i)
            ph[at[i], :k] = p.astype(BF16)
            norm = norm + jnp.sum(p * p, keepdims=True)
        for i in range(order):
            k = (i + 1) * BLOCK
            w[at[i], :k] -= jnp.dot(ph[at[i], :k], wh[:k, :k], preferred_element_type=F32)
        return jnp.sum(norm)

    step(False)

    def not_done(state):
        count, norm = state
        return jnp.logical_and(count < rounds, jnp.logical_not(norm < 2.5e-5))

    def again(state):
        count, _ = state
        return count + 1, step(True)

    _, norm = lax.while_loop(not_done, again, (jnp.int32(0), jnp.float32(1.0)))
    flag[0] = jnp.where(norm < 2.5e-5, 1, 0).astype(jnp.int32)
    split_w()
    for i in range(order):
        k = (i + 1) * BLOCK
        upper = times((wh[at[i], :k], wl[at[i], :k]), (gh[:k, :], gl[:k, :]))
        r, c = index(i)
        triangle[at[i], :] = jnp.where(r <= c, upper, 0.0) * (1.0 / scale)
    first = 0
    for part in rows:
        size = part.shape[0]
        out = against(halves(part[...]), (wh[...], wl[...]))
        basis[pl.ds(first, size), :] = out * scale
        first += size


def factor(meta, mine, theirs, rows, scale):
    width = rows[0].shape[1]
    square = (width, width)
    local = sum(part.shape[0] for part in rows)
    number = len(block_list(width // BLOCK))
    return pl.pallas_call(
        functools.partial(factor_kernel, len(rows), scale, 12),
        out_shape=[
            jax.ShapeDtypeStruct((local, width), F32),
            jax.ShapeDtypeStruct(square, F32),
            jax.ShapeDtypeStruct(square, F32),
            jax.ShapeDtypeStruct((1,), jnp.int32),
        ],
        in_specs=[SMEM] + [VMEM] * (2 + len(rows)),
        out_specs=[VMEM, VMEM, VMEM, SMEM],
        scratch_shapes=[
            pltpu.VMEM((number, BLOCK, BLOCK), F32),
            pltpu.VMEM(square, F32),
            pltpu.VMEM(square, F32),
        ]
        + [pltpu.VMEM(square, BF16)] * 7,
        compiler_params=PARAMS,
    )(meta, mine, theirs, *rows)


def direct(gram, rows, scale):
    lower = jnp.linalg.cholesky(gram)
    own_rows = jnp.concatenate(rows, axis=0)
    basis = jax.scipy.linalg.solve_triangular(lower, own_rows.T, lower=True).T * scale
    return basis, lower.T / scale


def body(tile_values, tile_places, tile_counts, sketch):
    tiles = tile_values[0, 0]
    size = tiles.shape[1]
    width = sketch.shape[1]
    row_devices = lax.axis_size("row")
    col_devices = lax.axis_size("col")
    local_rows = sketch.shape[0] // row_devices
    tile_rows = local_rows * col_devices // size
    panels = sketch.reshape(-1, size, width)
    places = tile_places[0, 0]
    row, col = lax.axis_index("row"), lax.axis_index("col")
    piece = (row & 1) | (col & 2)
    scale = math.sqrt(local_rows * row_devices * col_devices)

    def meta_of(flip):
        return jnp.stack([tile_counts[0, 0], col, jnp.int32(flip), piece]).astype(jnp.int32)

    meta = meta_of(0)
    chunks = math.gcd(CHUNKS, tile_rows // col_devices)
    far = tile_products(meta_of(1), places, tiles, panels, tile_rows, col_devices, chunks)
    near = tile_products(meta, places, tiles, panels, tile_rows, col_devices, chunks)
    across = []
    for n in range(chunks):
        own = far[chunks + n] + swapped(far[n], 0, 1)
        across.append(swapped(own, 0, 2))
    rows, grams = [], []
    for n in range(chunks):
        last = n == chunks - 1
        out = gram_chunk(
            meta, near[chunks + n], swapped(near[n], 0, 1), across[n], grams, last
        )
        rows.append(out[0])
        if last:
            mine, other = out[1:]
        else:
            grams.append(out[1])
    mine, theirs = gram_sum(meta, mine, other)
    basis, triangle, gram, flag = factor(meta, mine, theirs, rows, scale)
    return lax.cond(
        flag[0] == 1,
        lambda: (basis, triangle),
        lambda: direct(gram, rows, scale),
    )


def solution(mesh):
    in_specs = (
        P("row", "col", None, None, None),
        P("row", "col", None, None),
        P("row", "col"),
        P("col", None),
    )
    out_specs = (P(("row", "col"), None), P())
    return jax.shard_map(body, mesh=mesh, in_specs=in_specs, out_specs=out_specs, check_vma=False)
```

```python
import functools
import math

import jax
import jax.numpy as jnp
from jax import lax
from jax.experimental import pallas as pl
from jax.experimental.pallas import tpu as pltpu
from jax.sharding import PartitionSpec as P

BF16 = jnp.bfloat16
F32 = jnp.float32
PAIR = 2
TURN = 8
CHUNKS = 3
BLOCK = 128
SMEM = pl.BlockSpec(memory_space=pltpu.SMEM)
VMEM = pl.BlockSpec(memory_space=pltpu.VMEM)
ANY = pl.BlockSpec(memory_space=pl.ANY)


def params(size):
    return pltpu.CompilerParams(vmem_limit_bytes=size)


def halves(x):
    high = x.astype(BF16)
    return high, (x - high.astype(F32)).astype(BF16)


def tile_kernel(resident, span, chunks, flip, stride, counts, places, tiles, panels, *refs):
    outs = refs[: 2 * chunks]
    refs = refs[2 * chunks :]
    acc, tile_buf, panel_buf, key, fill, slot, column, first_of, key_of = refs[:9]
    tile_sem, panel_sem, out_sem = refs[9:]
    slots = tiles.shape[0]
    blocks = acc.shape[0]
    per_owner = key.shape[0] // lax.axis_size("col")
    here = blocks // 2
    bulk_copy = pltpu.make_async_copy(tiles, tile_buf.at[pl.ds(0, slots)], tile_sem.at[0])
    bulk_copy.start()
    if resident:
        panel_copy = pltpu.make_async_copy(panels, panel_buf, panel_sem.at[0])
        panel_copy.start()
    live = counts[0, 0]
    own = lax.axis_index("col")

    for owner in range(key.shape[0] // per_owner):
        base = jnp.where((owner & 1) == (own & 1), here, 0)
        wanted = (owner >> 1) == ((own >> 1) ^ flip)
        for inside in range(per_owner):
            name = jnp.where(wanted, base + inside - span[0], blocks)
            key[owner * per_owner + inside] = name if span[0] <= inside < span[1] else blocks
    for k in range(blocks + 1):
        fill[k] = k * stride

    unroll = math.gcd(slots, 8)

    def put(g, carry):
        for i in range(unroll):
            t = g * unroll + i
            k = jnp.where(t < live, key[places[0, t]], blocks)
            p = fill[k]
            fill[k] = p + 1
            slot[p] = t
            column[p] = places[1, t]
        return carry

    lax.fori_loop(0, (live + unroll - 1) // unroll, put, 0)

    empty = blocks * stride + slots
    for i in range(PAIR):
        slot[empty + i] = slots
        column[empty + i] = 0
    number, bounds = 0, [0]
    for k in range(blocks):
        size = fill[k] - k * stride
        for i in range(PAIR - 1):
            slot[fill[k] + i] = slots
            column[fill[k] + i] = 0

        def add_pair(j, at, k=k):
            first_of[at + j] = k * stride + j * PAIR
            key_of[at + j] = k
            return at

        pairs = (size + PAIR - 1) // PAIR
        lax.fori_loop(0, pairs, add_pair, number)
        number += pairs
        if (k + 1) % here == 0:
            for i in range(TURN - 1):
                first_of[number + i] = empty
                key_of[number + i] = k
            number = (number + TURN - 1) // TURN * TURN
            bounds.append(number // TURN)
    acc[...] = jnp.zeros_like(acc)
    tile_buf[slots] = jnp.zeros_like(tile_buf[slots])
    bulk_copy.wait()
    if resident:
        panel_copy.wait()

    def turn(g, carry):
        firsts = [first_of[g * TURN + i] for i in range(TURN)]
        if not resident:
            copies = [
                pltpu.make_async_copy(
                    panels.at[column[firsts[i] + j]],
                    panel_buf.at[i * PAIR + j],
                    panel_sem.at[i * PAIR + j],
                )
                for i in range(TURN)
                for j in range(PAIR)
            ]
            for copy in copies:
                copy.start()
            for copy in copies:
                copy.wait()
        for i, at in enumerate(firsts):
            left = jnp.concatenate([tile_buf[slot[at + j]] for j in range(PAIR)], axis=1)
            right = jnp.concatenate(
                [
                    panel_buf[column[at + j] if resident else i * PAIR + j]
                    for j in range(PAIR)
                ],
                axis=0,
            )
            acc[key_of[g * TURN + i]] += jnp.dot(left, right, preferred_element_type=F32)
        return carry

    size = here // chunks
    copies = []
    for half in range(2):
        lax.fori_loop(bounds[half], bounds[half + 1], turn, 0)
        for n in range(half * chunks, (half + 1) * chunks):
            copy = pltpu.make_async_copy(acc.at[pl.ds(n * size, size)], outs[n], out_sem.at[n])
            copy.start()
            copies.append(copy)
    for copy in copies:
        copy.wait()


def tile_products(counts, places, tiles, panels, tile_rows, span, chunks, flip, limit):
    slots, size, _ = tiles.shape
    width = panels.shape[2]
    blocks = (span[1] - span[0]) * 2
    stride = (min(slots, panels.shape[0]) // PAIR + 1) * PAIR
    entries = blocks * stride + slots + PAIR
    pairs = blocks * stride // PAIR + 2 * TURN
    resident = panels.size * 2 <= 16 << 20
    panel_shape = (panels.shape[0] if resident else PAIR * TURN, size, width)
    used = blocks * size * width * 4 + (slots + 1) * size * size * 2 + math.prod(panel_shape) * 2
    piece = jax.ShapeDtypeStruct((blocks // 2 // chunks, size, width), F32)
    return pl.pallas_call(
        functools.partial(tile_kernel, resident, span, chunks, flip, stride),
        out_shape=[piece] * (2 * chunks),
        in_specs=[SMEM, SMEM, ANY, ANY],
        out_specs=[ANY] * (2 * chunks),
        scratch_shapes=[
            pltpu.VMEM((blocks, size, width), F32),
            pltpu.VMEM((slots + 1, size, size), BF16),
            pltpu.VMEM(panel_shape, BF16),
            pltpu.SMEM((tile_rows,), jnp.int32),
            pltpu.SMEM((blocks + 1,), jnp.int32),
            pltpu.SMEM((entries,), jnp.int32),
            pltpu.SMEM((entries,), jnp.int32),
            pltpu.SMEM((pairs,), jnp.int32),
            pltpu.SMEM((pairs,), jnp.int32),
            pltpu.SemaphoreType.DMA((1,)),
            pltpu.SemaphoreType.DMA((1 if resident else PAIR * TURN,)),
            pltpu.SemaphoreType.DMA((2 * chunks,)),
        ],
        compiler_params=params(max(limit, used + (6 << 20))),
        cost_estimate=pl.CostEstimate(
            flops=slots * size * size * width,
            bytes_accessed=tiles.size + panels.size * 2,
            transcendentals=0,
        ),
    )(counts, places, tiles, panels)


def block_list(order):
    return [(i, j) for i in range(order) for j in range(i + 1)]


def gram_kernel(last, *refs):
    if last:
        keep, core, across, *earlier, rows, own, send, acc = refs
    else:
        keep, core, across, rows, acc = refs
    total = (keep[...] + core[...]) + across[...]
    total = total.reshape(rows.shape)
    rows[...] = total
    high, low = halves(total)
    left = jnp.concatenate([high, high, low], axis=0)
    right = jnp.concatenate([high, low, high], axis=0)
    order = rows.shape[1] // BLOCK
    for i in range(order):
        strip = lax.dot_general(
            left[:, i * BLOCK : (i + 1) * BLOCK],
            right[:, : (i + 1) * BLOCK],
            (((0,), (0,)), ((), ())),
            preferred_element_type=F32,
        )
        for j in range(i + 1):
            at = pl.ds((i * (i + 1) // 2 + j) * BLOCK, BLOCK)
            part = strip[:, j * BLOCK : (j + 1) * BLOCK]
            if last:
                for gram in earlier:
                    part = part + gram[at]
            acc[at] = part
    if last:
        core_bit, me = place()
        size = own.shape[1]
        half = acc.shape[0] // 2
        for d in range(own.shape[0]):
            at = (me ^ d) * size
            own[d] = acc[pl.ds(pl.multiple_of(core_bit * half + at, 8), size)]
            send[d] = acc[pl.ds(pl.multiple_of((1 - core_bit) * half + at, 8), size)]


def place():
    row, col = lax.axis_index("row"), lax.axis_index("col")
    return col & 1, (row & 1) | (col & 2)


def gram_chunk(keep, core, across, earlier, last):
    width = keep.shape[2]
    rows = keep.shape[0] * keep.shape[1]
    number = len(block_list(width // BLOCK)) * BLOCK
    whole = jax.ShapeDtypeStruct((number, BLOCK), F32)
    pieces = jax.ShapeDtypeStruct((4, number // 8, BLOCK), F32)
    row_shape = jax.ShapeDtypeStruct((rows, width), F32)
    args = [keep, core, across] + (list(earlier) if last else [])
    outs = [row_shape] + ([pieces, pieces] if last else [whole])
    return pl.pallas_call(
        functools.partial(gram_kernel, last),
        out_shape=outs,
        in_specs=[VMEM] * len(args),
        out_specs=[VMEM] * len(outs),
        scratch_shapes=[pltpu.VMEM(whole.shape, F32)] if last else [],
        compiler_params=params(16 << 20),
        cost_estimate=pl.CostEstimate(
            flops=4 * rows * width * width, bytes_accessed=rows * width * 16, transcendentals=0
        ),
    )(*args)


def swapped(x, row_flip, col_flip):
    rows, cols = lax.axis_size("row"), lax.axis_size("col")
    if not row_flip:
        return lax.ppermute(x, "col", [(c, c ^ col_flip) for c in range(cols)])
    if not col_flip:
        return lax.ppermute(x, "row", [(r, r ^ row_flip) for r in range(rows)])
    route = [
        (r * cols + c, (r ^ row_flip) * cols + (c ^ col_flip))
        for r in range(rows)
        for c in range(cols)
    ]
    return lax.ppermute(x, ("row", "col"), route)


FLIPS = ((1, 0), (0, 2), (1, 2))


def gram_sum(own, send):
    theirs = swapped(send, 0, 1)
    part = [own[d] + theirs[d] for d in range(4)]
    got = [swapped(x, *flip) for x, flip in zip(part[1:], FLIPS)]
    piece = (part[0] + got[0]) + (got[1] + got[2])
    bits = lax.axis_size("row").bit_length() - 1
    bit = 1
    while bit < bits:
        if bit + 1 < bits:
            a, b = 1 << bit, 2 << bit
            got = [swapped(piece, flip, 0) for flip in (a, b, a | b)]
            piece = (piece + got[0]) + (got[1] + got[2])
            bit += 2
        else:
            piece = piece + swapped(piece, 1 << bit, 0)
            bit += 1
    mine = [piece] + [swapped(piece, *flip) for flip in FLIPS]
    return mine, [swapped(x, 0, 1) for x in mine]


def against(left, right_rows):
    lh, ll = left
    rh, rl = right_rows
    return lax.dot_general(
        jnp.concatenate([lh, lh, ll], axis=1),
        jnp.concatenate([rh, rl, rh], axis=1),
        (((1,), (1,)), ((), ())),
        preferred_element_type=F32,
    )


def times(left, right):
    lh, ll = left
    rh, rl = right
    return jnp.dot(
        jnp.concatenate([lh, lh, ll], axis=1),
        jnp.concatenate([rh, rl, rh], axis=0),
        preferred_element_type=F32,
    )


def factor_kernel(chunks, scale, rounds, *refs):
    pieces, rows = refs[:8], refs[8 : 8 + chunks]
    basis, triangle, gram_out, flag = refs[8 + chunks : 12 + chunks]
    blocks, gram, w, wh, wl, gh, gl, yh, yl, ph = refs[12 + chunks :]
    size = gram.shape[0]
    order = size // BLOCK
    core_bit, me = place()
    half = blocks.shape[0] // 2
    for n, piece in enumerate(pieces):
        at = (core_bit ^ (n // 4)) * half + (me ^ (n % 4)) * piece.shape[0]
        blocks[pl.ds(pl.multiple_of(at, 8), piece.shape[0])] = piece[...]
    at = [slice(i * BLOCK, (i + 1) * BLOCK) for i in range(order)]
    for n, (i, j) in enumerate(block_list(order)):
        block = blocks[n * BLOCK : (n + 1) * BLOCK]
        gram[at[i], at[j]] = block
        if i != j:
            gram[at[j], at[i]] = block.T
    high, low = halves(gram[...])
    gh[...] = high
    gl[...] = low
    gram_out[...] = gram[...]

    def index(i):
        shape = (BLOCK, size)
        return (
            lax.broadcasted_iota(jnp.int32, shape, 0) + i * BLOCK,
            lax.broadcasted_iota(jnp.int32, shape, 1),
        )

    def phi(error, i):
        r, c = index(i)
        r, c = r[:, : error.shape[1]], c[:, : error.shape[1]]
        return jnp.where(r > c, error, jnp.where(r == c, 0.5 * error, 0.0))

    row_scale, col_scale = [], []
    for i in range(order):
        block = gram[at[i], at[i]]
        r, c = index(0)
        diagonal = jnp.where(r[:, :BLOCK] == c[:, :BLOCK], block, 0.0)
        row_scale.append(lax.rsqrt(jnp.sum(diagonal, axis=1, keepdims=True)))
        col_scale.append(lax.rsqrt(jnp.sum(diagonal, axis=0, keepdims=True)))
    col_scale = jnp.concatenate(col_scale, axis=1)
    for i in range(order):
        r, c = index(i)
        same = jnp.where(r == c, 1.0, 0.0)
        error = gram[at[i], :] * row_scale[i] * col_scale - same
        w[at[i], :] = (same - phi(error, i)) * col_scale

    def split_w():
        for i in range(order):
            high, low = halves(w[at[i], :])
            wh[at[i], :] = high
            wl[at[i], :] = low

    def step(exact):
        split_w()
        for i in range(order):
            if exact:
                y = against((gh[at[i], :], gl[at[i], :]), (wh[...], wl[...]))
            else:
                y = lax.dot_general(
                    gh[at[i], :], wh[...], (((1,), (1,)), ((), ())), preferred_element_type=F32
                )
            high, low = halves(y)
            yh[at[i], :] = high
            yl[at[i], :] = low
        norm = jnp.zeros((1, 1), F32)
        for i in range(order):
            k = (i + 1) * BLOCK
            if exact:
                m = times((wh[at[i], :k], wl[at[i], :k]), (yh[:k, :k], yl[:k, :k]))
            else:
                m = jnp.dot(wh[at[i], :k], yh[:k, :k], preferred_element_type=F32)
            r, c = index(i)
            p = phi(m - jnp.where(r[:, :k] == c[:, :k], 1.0, 0.0), i)
            ph[at[i], :k] = p.astype(BF16)
            norm = norm + jnp.sum(p * p, keepdims=True)
        for i in range(order):
            k = (i + 1) * BLOCK
            w[at[i], :k] -= jnp.dot(ph[at[i], :k], wh[:k, :k], preferred_element_type=F32)
        return jnp.sum(norm)

    step(False)

    def not_done(state):
        count, norm = state
        return jnp.logical_and(count < rounds, jnp.logical_not(norm < 2.5e-5))

    def again(state):
        count, _ = state
        return count + 1, step(True)

    _, norm = lax.while_loop(not_done, again, (jnp.int32(0), jnp.float32(1.0)))
    flag[0] = jnp.where(norm < 2.5e-5, 1, 0).astype(jnp.int32)
    split_w()
    for i in range(order):
        k = (i + 1) * BLOCK
        upper = times((wh[at[i], :k], wl[at[i], :k]), (gh[:k, :], gl[:k, :]))
        r, c = index(i)
        triangle[at[i], :] = jnp.where(r <= c, upper, 0.0) * (1.0 / scale)
    first = 0
    for part in rows:
        size = part.shape[0]
        out = against(halves(part[...]), (wh[...], wl[...]))
        basis[pl.ds(first, size), :] = out * scale
        first += size


def factor(pieces, rows, scale):
    width = rows[0].shape[1]
    square = (width, width)
    local = sum(part.shape[0] for part in rows)
    number = len(block_list(width // BLOCK))
    return pl.pallas_call(
        functools.partial(factor_kernel, len(rows), scale, 12),
        out_shape=[
            jax.ShapeDtypeStruct((local, width), F32),
            jax.ShapeDtypeStruct(square, F32),
            jax.ShapeDtypeStruct(square, F32),
            jax.ShapeDtypeStruct((1,), jnp.int32),
        ],
        in_specs=[VMEM] * (8 + len(rows)),
        out_specs=[VMEM, VMEM, VMEM, SMEM],
        scratch_shapes=[
            pltpu.VMEM((number * BLOCK, BLOCK), F32),
            pltpu.VMEM(square, F32),
            pltpu.VMEM(square, F32),
        ]
        + [pltpu.VMEM(square, BF16)] * 7,
        compiler_params=params(24 << 20),
    )(*pieces, *rows)


def direct(gram, rows, scale):
    lower = jnp.linalg.cholesky(gram)
    own_rows = jnp.concatenate(rows, axis=0)
    basis = jax.scipy.linalg.solve_triangular(lower, own_rows.T, lower=True).T * scale
    return basis, lower.T / scale


def body(tile_values, tile_places, tile_counts, sketch):
    tiles = tile_values[0, 0]
    size = tiles.shape[1]
    width = sketch.shape[1]
    row_devices = lax.axis_size("row")
    col_devices = lax.axis_size("col")
    local_rows = sketch.shape[0] // row_devices
    tile_rows = local_rows * col_devices // size
    panels = sketch.reshape(-1, size, width)
    places = tile_places[0, 0]
    scale = math.sqrt(local_rows * row_devices * col_devices)
    per_owner = tile_rows // col_devices
    chunks = math.gcd(CHUNKS, per_owner)

    def products(first, last, flip, limit):
        span = (first * per_owner // chunks, last * per_owner // chunks)
        out = tile_products(
            tile_counts, places, tiles, panels, tile_rows, span, last - first, flip, limit
        )
        return out[: last - first], out[last - first :]

    across = []
    for first, last in ((0, 1), (1, chunks))[: min(2, chunks)]:
        send, keep = products(first, last, 1, 56 << 20)
        own = [k + swapped(x, 0, 1) for k, x in zip(keep, send)]
        places, *own = lax.optimization_barrier((places, *own))
        across += [swapped(x, 0, 2) for x in own]
    send, keep = products(0, chunks, 0, 0)
    rows, grams = [], []
    for n in range(chunks):
        last = n == chunks - 1
        out = gram_chunk(keep[n], swapped(send[n], 0, 1), across[n], grams, last)
        rows.append(out[0])
        grams.append(out[1])
    mine, theirs = gram_sum(*out[1:])
    basis, triangle, gram, flag = factor(mine + theirs, rows, scale)
    return lax.cond(
        flag[0] == 1,
        lambda: (basis, triangle),
        lambda: direct(gram, rows, scale),
    )


def solution(mesh):
    in_specs = (
        P("row", "col", None, None, None),
        P("row", "col", None, None),
        P("row", "col"),
        P("col", None),
    )
    out_specs = (P(("row", "col"), None), P())
    return jax.shard_map(body, mesh=mesh, in_specs=in_specs, out_specs=out_specs, check_vma=False)
```

```python
import functools
import math

import jax
import jax.numpy as jnp
from jax import lax
from jax.experimental import pallas as pl
from jax.experimental.pallas import tpu as pltpu
from jax.sharding import PartitionSpec as P

BF16 = jnp.bfloat16
F32 = jnp.float32
PAIR = 2
TURN = 12
PARTS = 2
BLOCK = 128
SMEM = pl.BlockSpec(memory_space=pltpu.SMEM)
VMEM = pl.BlockSpec(memory_space=pltpu.VMEM)
ANY = pl.BlockSpec(memory_space=pl.ANY)

def params(size):
    return pltpu.CompilerParams(vmem_limit_bytes=size)


def halves(x):
    high = x.astype(BF16)
    return high, (x - high.astype(F32)).astype(BF16)


def tile_kernel(resident, flip, stride, counts, places, tiles, panels, *refs):
    outs, refs = refs[:-13], refs[-13:]
    tile_buf, panel_buf, live_of, place_of, key, fill, slot, column, first_of, key_of = refs[:10]
    acc, load_sem, panel_sem = refs[10:]
    slots = tiles.shape[0]
    blocks = acc.shape[0]
    per_owner = blocks // 2
    index_loads = [
        pltpu.make_async_copy(counts, live_of, load_sem.at[0]),
        pltpu.make_async_copy(places, place_of, load_sem.at[1]),
    ]
    panel_loads = [pltpu.make_async_copy(panels, panel_buf, panel_sem.at[0])] if resident else []
    cuts = [slots * n // PARTS for n in range(PARTS + 1)]
    tile_loads = [
        pltpu.make_async_copy(
            tiles.at[pl.ds(a, b - a)], tile_buf.at[pl.ds(a, b - a)], load_sem.at[2 + n]
        )
        for n, (a, b) in enumerate(zip(cuts, cuts[1:]))
    ]
    for load in index_loads + panel_loads + tile_loads:
        load.start()
    own = lax.axis_index("col")

    for owner in range(key.shape[0] // per_owner):
        base = jnp.where((owner & 1) == (own & 1), per_owner, 0)
        wanted = (owner >> 1) == ((own >> 1) ^ flip)
        for inside in range(per_owner):
            key[owner * per_owner + inside] = jnp.where(wanted, base + inside, blocks)
    lists = PARTS * blocks
    for k in range(lists + 1):
        fill[k] = k * stride
    for load in index_loads:
        load.wait()
    live = live_of[0, 0]

    unroll = math.gcd(slots, 8)

    def put(g, carry):
        for i in range(unroll):
            t = g * unroll + i
            part = sum(jnp.where(t >= cut, blocks, 0) for cut in cuts[1:-1])
            row = key[place_of[0, t]]
            k = jnp.where(jnp.logical_and(t < live, row < blocks), part + row, lists)
            p = fill[k]
            fill[k] = p + 1
            slot[p] = t
            column[p] = place_of[1, t]
        return carry

    lax.fori_loop(0, (live + unroll - 1) // unroll, put, 0)

    empty = lists * stride + slots
    for i in range(PAIR):
        slot[empty + i] = slots
        column[empty + i] = 0
    number, bounds = 0, [0]
    for k in range(lists):
        size = fill[k] - k * stride
        for i in range(PAIR - 1):
            slot[fill[k] + i] = slots
            column[fill[k] + i] = 0

        def add_pair(j, at, k=k):
            first_of[at + j] = k * stride + j * PAIR
            key_of[at + j] = k % blocks
            return at

        pairs = (size + PAIR - 1) // PAIR
        lax.fori_loop(0, pairs, add_pair, number)
        number += pairs
        if (k + 1) % blocks == 0:
            for i in range(TURN - 1):
                first_of[number + i] = empty
                key_of[number + i] = 0
            number = (number + TURN - 1) // TURN * TURN
            bounds.append(number // TURN)
    acc[...] = jnp.zeros_like(acc)
    tile_buf[slots] = jnp.zeros_like(tile_buf[slots])
    for load in panel_loads:
        load.wait()

    def turn(g, carry):
        firsts = [first_of[g * TURN + i] for i in range(TURN)]
        if not resident:
            copies = [
                pltpu.make_async_copy(
                    panels.at[column[firsts[i] + j]],
                    panel_buf.at[i * PAIR + j],
                    panel_sem.at[i * PAIR + j],
                )
                for i in range(TURN)
                for j in range(PAIR)
            ]
            for copy in copies:
                copy.start()
            for copy in copies:
                copy.wait()
        for i, at in enumerate(firsts):
            left = jnp.concatenate([tile_buf[slot[at + j]] for j in range(PAIR)], axis=1)
            right = jnp.concatenate(
                [
                    panel_buf[column[at + j] if resident else i * PAIR + j]
                    for j in range(PAIR)
                ],
                axis=0,
            )
            acc[key_of[g * TURN + i]] += jnp.dot(left, right, preferred_element_type=F32)
        return carry

    for n, load in enumerate(tile_loads):
        load.wait()
        lax.fori_loop(bounds[n], bounds[n + 1], turn, 0)
    first = 0
    for out in outs:
        out[...] = acc[first : first + out.shape[0]]
        first += out.shape[0]


def tile_products(counts, places, tiles, panels, tile_rows, sizes, flip):
    slots, size, _ = tiles.shape
    width = panels.shape[2]
    blocks = 2 * sum(sizes)
    stride = (min(slots, panels.shape[0]) // PAIR + 1) * PAIR
    lists = PARTS * blocks
    entries = lists * stride + slots + PAIR
    pairs = lists * stride // PAIR + TURN * (PARTS + 1)
    resident = panels.size * 2 <= 16 << 20
    panel_shape = (panels.shape[0] if resident else PAIR * TURN, size, width)
    return pl.pallas_call(
        functools.partial(tile_kernel, resident, flip, stride),
        out_shape=[jax.ShapeDtypeStruct((n, size, width), F32) for n in (*sizes, *sizes)],
        in_specs=[ANY] * 4,
        out_specs=[VMEM] * (2 * len(sizes)),
        scratch_shapes=[
            pltpu.VMEM((slots + 1, size, size), BF16),
            pltpu.VMEM(panel_shape, BF16),
            pltpu.SMEM((1, 1), jnp.int32),
            pltpu.SMEM((2, slots), jnp.int32),
            pltpu.SMEM((tile_rows,), jnp.int32),
            pltpu.SMEM((lists + 1,), jnp.int32),
            pltpu.SMEM((entries,), jnp.int32),
            pltpu.SMEM((entries,), jnp.int32),
            pltpu.SMEM((pairs,), jnp.int32),
            pltpu.SMEM((pairs,), jnp.int32),
            pltpu.VMEM((blocks, size, width), F32),
            pltpu.SemaphoreType.DMA((2 + PARTS,)),
            pltpu.SemaphoreType.DMA((1 if resident else PAIR * TURN,)),
        ],
        compiler_params=params(50 << 20),
    )(counts, places, tiles, panels)


def block_list(order):
    return [(i, j) for i in range(order) for j in range(i + 1)]


def gram_kernel(last, *refs):
    if last:
        keep, core, across, *earlier, rows, own, send, acc = refs
    else:
        keep, core, across, rows, acc = refs
    total = (keep[...] + core[...]) + across[...]
    total = total.reshape(rows.shape)
    rows[...] = total
    high, low = halves(total)
    left = jnp.concatenate([high, high, low], axis=0)
    right = jnp.concatenate([high, low, high], axis=0)
    order = rows.shape[1] // BLOCK
    for i in range(order):
        strip = lax.dot_general(
            left[:, i * BLOCK : (i + 1) * BLOCK],
            right[:, : (i + 1) * BLOCK],
            (((0,), (0,)), ((), ())),
            preferred_element_type=F32,
        )
        for j in range(i + 1):
            at = pl.ds((i * (i + 1) // 2 + j) * BLOCK, BLOCK)
            part = strip[:, j * BLOCK : (j + 1) * BLOCK]
            if last:
                for gram in earlier:
                    part = part + gram[at]
            acc[at] = part
    if last:
        core_bit, me = place()
        size = own.shape[1]
        half = acc.shape[0] // 2
        for d in range(own.shape[0]):
            at = (me ^ d) * size
            own[d] = acc[pl.ds(pl.multiple_of(core_bit * half + at, 8), size)]
            send[d] = acc[pl.ds(pl.multiple_of((1 - core_bit) * half + at, 8), size)]


def place():
    row, col = lax.axis_index("row"), lax.axis_index("col")
    return col & 1, (row & 1) | (col & 2)


def gram_chunk(keep, core, across, earlier, last):
    width = keep.shape[2]
    rows = keep.shape[0] * keep.shape[1]
    number = len(block_list(width // BLOCK)) * BLOCK
    whole = jax.ShapeDtypeStruct((number, BLOCK), F32)
    pieces = jax.ShapeDtypeStruct((4, number // 8, BLOCK), F32)
    row_shape = jax.ShapeDtypeStruct((rows, width), F32)
    args = [keep, core, across] + (list(earlier) if last else [])
    outs = [row_shape] + ([pieces, pieces] if last else [whole])
    return pl.pallas_call(
        functools.partial(gram_kernel, last),
        out_shape=outs,
        in_specs=[VMEM] * len(args),
        out_specs=[VMEM] * len(outs),
        scratch_shapes=[pltpu.VMEM(whole.shape, F32)] if last else [],
        compiler_params=params(16 << 20),
    )(*args)


def swapped(x, row_flip, col_flip):
    rows, cols = lax.axis_size("row"), lax.axis_size("col")
    if not row_flip:
        return lax.ppermute(x, "col", [(c, c ^ col_flip) for c in range(cols)])
    if not col_flip:
        return lax.ppermute(x, "row", [(r, r ^ row_flip) for r in range(rows)])
    route = [
        (r * cols + c, (r ^ row_flip) * cols + (c ^ col_flip))
        for r in range(rows)
        for c in range(cols)
    ]
    return lax.ppermute(x, ("row", "col"), route)


FLIPS = ((1, 0), (0, 2), (1, 2))


def gram_sum(own, send):
    theirs = swapped(send, 0, 1)
    part = [own[d] + theirs[d] for d in range(4)]
    got = [swapped(x, *flip) for x, flip in zip(part[1:], FLIPS)]
    piece = (part[0] + got[0]) + (got[1] + got[2])
    bits = lax.axis_size("row").bit_length() - 1
    bit = 1
    while bit < bits:
        if bit + 1 < bits:
            a, b = 1 << bit, 2 << bit
            got = [swapped(piece, flip, 0) for flip in (a, b, a | b)]
            piece = (piece + got[0]) + (got[1] + got[2])
            bit += 2
        else:
            piece = piece + swapped(piece, 1 << bit, 0)
            bit += 1
    mine = [piece] + [swapped(piece, *flip) for flip in FLIPS]
    return mine, [swapped(x, 0, 1) for x in mine]


def against(left, right_rows):
    lh, ll = left
    rh, rl = right_rows
    return lax.dot_general(
        jnp.concatenate([lh, lh, ll], axis=1),
        jnp.concatenate([rh, rl, rh], axis=1),
        (((1,), (1,)), ((), ())),
        preferred_element_type=F32,
    )


def times(left, right):
    lh, ll = left
    rh, rl = right
    return jnp.dot(
        jnp.concatenate([lh, lh, ll], axis=1),
        jnp.concatenate([rh, rl, rh], axis=0),
        preferred_element_type=F32,
    )


def factor_kernel(chunks, scale, rounds, *refs):
    pieces, rows = refs[:8], refs[8 : 8 + chunks]
    basis, triangle, gram_out, flag = refs[8 + chunks : 12 + chunks]
    blocks, gram, w, wh, wl, gh, gl, yh, yl, ph = refs[12 + chunks :]
    size = gram.shape[0]
    order = size // BLOCK
    core_bit, me = place()
    half = blocks.shape[0] // 2
    for n, piece in enumerate(pieces):
        at = (core_bit ^ (n // 4)) * half + (me ^ (n % 4)) * piece.shape[0]
        blocks[pl.ds(pl.multiple_of(at, 8), piece.shape[0])] = piece[...]
    at = [slice(i * BLOCK, (i + 1) * BLOCK) for i in range(order)]
    for n, (i, j) in enumerate(block_list(order)):
        block = blocks[n * BLOCK : (n + 1) * BLOCK]
        gram[at[i], at[j]] = block
        if i != j:
            gram[at[j], at[i]] = block.T
    high, low = halves(gram[...])
    gh[...] = high
    gl[...] = low
    gram_out[...] = gram[...]

    def index(i):
        shape = (BLOCK, size)
        return (
            lax.broadcasted_iota(jnp.int32, shape, 0) + i * BLOCK,
            lax.broadcasted_iota(jnp.int32, shape, 1),
        )

    def phi(error, i):
        r, c = index(i)
        r, c = r[:, : error.shape[1]], c[:, : error.shape[1]]
        return jnp.where(r > c, error, jnp.where(r == c, 0.5 * error, 0.0))

    row_scale, col_scale = [], []
    for i in range(order):
        block = gram[at[i], at[i]]
        r, c = index(0)
        diagonal = jnp.where(r[:, :BLOCK] == c[:, :BLOCK], block, 0.0)
        row_scale.append(lax.rsqrt(jnp.sum(diagonal, axis=1, keepdims=True)))
        col_scale.append(lax.rsqrt(jnp.sum(diagonal, axis=0, keepdims=True)))
    col_scale = jnp.concatenate(col_scale, axis=1)
    for i in range(order):
        r, c = index(i)
        same = jnp.where(r == c, 1.0, 0.0)
        error = gram[at[i], :] * row_scale[i] * col_scale - same
        w[at[i], :] = (same - phi(error, i)) * col_scale

    def split_w():
        for i in range(order):
            high, low = halves(w[at[i], :])
            wh[at[i], :] = high
            wl[at[i], :] = low

    def step(exact):
        split_w()
        for i in range(order):
            if exact:
                y = against((gh[at[i], :], gl[at[i], :]), (wh[...], wl[...]))
            else:
                y = lax.dot_general(
                    gh[at[i], :], wh[...], (((1,), (1,)), ((), ())), preferred_element_type=F32
                )
            high, low = halves(y)
            yh[at[i], :] = high
            yl[at[i], :] = low
        norm = jnp.zeros((1, 1), F32)
        for i in range(order):
            k = (i + 1) * BLOCK
            if exact:
                m = times((wh[at[i], :k], wl[at[i], :k]), (yh[:k, :k], yl[:k, :k]))
            else:
                m = jnp.dot(wh[at[i], :k], yh[:k, :k], preferred_element_type=F32)
            r, c = index(i)
            p = phi(m - jnp.where(r[:, :k] == c[:, :k], 1.0, 0.0), i)
            ph[at[i], :k] = p.astype(BF16)
            norm = norm + jnp.sum(p * p, keepdims=True)
        for i in range(order):
            k = (i + 1) * BLOCK
            w[at[i], :k] -= jnp.dot(ph[at[i], :k], wh[:k, :k], preferred_element_type=F32)
        return jnp.sum(norm)

    step(False)

    def not_done(state):
        count, norm = state
        return jnp.logical_and(count < rounds, jnp.logical_not(norm < 2.5e-5))

    def again(state):
        count, _ = state
        return count + 1, step(True)

    _, norm = lax.while_loop(not_done, again, (jnp.int32(0), jnp.float32(1.0)))
    flag[0] = jnp.where(norm < 2.5e-5, 1, 0).astype(jnp.int32)
    split_w()
    for i in range(order):
        k = (i + 1) * BLOCK
        upper = times((wh[at[i], :k], wl[at[i], :k]), (gh[:k, :], gl[:k, :]))
        r, c = index(i)
        triangle[at[i], :] = jnp.where(r <= c, upper, 0.0) * (1.0 / scale)
    first = 0
    for part in rows:
        size = part.shape[0]
        out = against(halves(part[...]), (wh[...], wl[...]))
        basis[pl.ds(first, size), :] = out * scale
        first += size


def factor(pieces, rows, scale):
    width = rows[0].shape[1]
    square = (width, width)
    local = sum(part.shape[0] for part in rows)
    number = len(block_list(width // BLOCK))
    return pl.pallas_call(
        functools.partial(factor_kernel, len(rows), scale, 12),
        out_shape=[
            jax.ShapeDtypeStruct((local, width), F32),
            jax.ShapeDtypeStruct(square, F32),
            jax.ShapeDtypeStruct(square, F32),
            jax.ShapeDtypeStruct((1,), jnp.int32),
        ],
        in_specs=[VMEM] * (8 + len(rows)),
        out_specs=[VMEM, VMEM, VMEM, SMEM],
        scratch_shapes=[
            pltpu.VMEM((number * BLOCK, BLOCK), F32),
            pltpu.VMEM(square, F32),
            pltpu.VMEM(square, F32),
        ]
        + [pltpu.VMEM(square, BF16)] * 7,
        compiler_params=params(24 << 20),
    )(*pieces, *rows)


def direct(gram, rows, scale):
    lower = jnp.linalg.cholesky(gram)
    own_rows = jnp.concatenate(rows, axis=0)
    basis = jax.scipy.linalg.solve_triangular(lower, own_rows.T, lower=True).T * scale
    return basis, lower.T / scale


def body(tile_values, tile_places, tile_counts, sketch):
    tiles = tile_values[0, 0]
    size = tiles.shape[1]
    width = sketch.shape[1]
    row_devices = lax.axis_size("row")
    col_devices = lax.axis_size("col")
    local_rows = sketch.shape[0] // row_devices
    tile_rows = local_rows * col_devices // size
    panels = sketch.reshape(-1, size, width)
    places = tile_places[0, 0]
    scale = math.sqrt(local_rows * row_devices * col_devices)
    per_owner = tile_rows // col_devices
    first = max(1, per_owner // 3)
    sizes = (first, per_owner - first) if per_owner > first else (first,)
    chunks = len(sizes)

    def products(flip):
        out = tile_products(tile_counts, places, tiles, panels, tile_rows, sizes, flip)
        return out[:chunks], out[chunks:]

    send, keep = products(1)
    across = [swapped(k + swapped(x, 0, 1), 0, 2) for k, x in zip(keep, send)]
    send, keep = products(0)
    send, keep, across[0] = lax.optimization_barrier((send, keep, across[0]))
    rows, grams = [], []
    for n in range(chunks):
        out = gram_chunk(keep[n], swapped(send[n], 0, 1), across[n], grams, n == chunks - 1)
        rows.append(out[0])
        grams.append(out[1])
    mine, theirs = gram_sum(*out[1:])
    basis, triangle, gram, flag = factor(mine + theirs, rows, scale)
    return lax.cond(
        flag[0] == 1,
        lambda: (basis, triangle),
        lambda: direct(gram, rows, scale),
    )


def solution(mesh):
    in_specs = (
        P("row", "col", None, None, None),
        P("row", "col", None, None),
        P("row", "col"),
        P("col", None),
    )
    out_specs = (P(("row", "col"), None), P())
    return jax.shard_map(body, mesh=mesh, in_specs=in_specs, out_specs=out_specs, check_vma=False)
```

```python
import functools
import math

import jax
import jax.numpy as jnp
from jax import lax
from jax.experimental import pallas as pl
from jax.experimental.pallas import tpu as pltpu
from jax.sharding import PartitionSpec as P

BF16 = jnp.bfloat16
F32 = jnp.float32
PAIR = 2
TURN = 12
PARTS = 2
BLOCK = 128
SMALL = 0.01
SMEM = pl.BlockSpec(memory_space=pltpu.SMEM)
VMEM = pl.BlockSpec(memory_space=pltpu.VMEM)
HBM = pl.BlockSpec(memory_space=pltpu.HBM)

def in_hbm(x):
    return pltpu.with_memory_space_constraint(x, pltpu.HBM)


def params(size):
    return pltpu.CompilerParams(vmem_limit_bytes=size)


def halves(x):
    high = x.astype(BF16)
    return high, (x - high.astype(F32)).astype(BF16)


def tile_kernel(resident, flip, stride, counts, places, tiles, panels, *refs):
    outs, refs = refs[:-12], refs[-12:]
    tile_buf, panel_buf, place_of, key, fill, slot, column, first_of, key_of = refs[:9]
    acc, load_sem, panel_sem = refs[9:]
    slots = tiles.shape[0]
    blocks = acc.shape[0]
    per_owner = blocks // 2
    place_load = pltpu.make_async_copy(places, place_of, load_sem.at[0])
    panel_loads = [pltpu.make_async_copy(panels, panel_buf, panel_sem.at[0])] if resident else []
    cuts = [slots * n // PARTS for n in range(PARTS + 1)]
    tile_loads = [
        pltpu.make_async_copy(
            tiles.at[pl.ds(a, b - a)], tile_buf.at[pl.ds(a, b - a)], load_sem.at[1 + n]
        )
        for n, (a, b) in enumerate(zip(cuts, cuts[1:]))
    ]
    for load in [place_load] + panel_loads + tile_loads:
        load.start()
    own = lax.axis_index("col")

    for owner in range(key.shape[0] // per_owner):
        base = jnp.where((owner & 1) == (own & 1), per_owner, 0)
        wanted = (owner >> 1) == ((own >> 1) ^ flip)
        for inside in range(per_owner):
            key[owner * per_owner + inside] = jnp.where(wanted, base + inside, blocks)
    lists = PARTS * blocks
    for k in range(lists + 1):
        fill[k] = k * stride
    place_load.wait()
    live = counts[0, 0]

    unroll = math.gcd(slots, 8)

    def put(g, carry):
        for i in range(unroll):
            t = g * unroll + i
            part = sum(jnp.where(t >= cut, blocks, 0) for cut in cuts[1:-1])
            row = key[place_of[0, t]]
            k = jnp.where(jnp.logical_and(t < live, row < blocks), part + row, lists)
            p = fill[k]
            fill[k] = p + 1
            slot[p] = t
            column[p] = place_of[1, t]
        return carry

    lax.fori_loop(0, (live + unroll - 1) // unroll, put, 0)

    empty = lists * stride + slots
    for i in range(PAIR):
        slot[empty + i] = slots
        column[empty + i] = 0
    number, bounds = 0, [0]
    for k in range(lists):
        size = fill[k] - k * stride
        for i in range(PAIR - 1):
            slot[fill[k] + i] = slots
            column[fill[k] + i] = 0

        def add_pair(j, at, k=k):
            first_of[at + j] = k * stride + j * PAIR
            key_of[at + j] = k % blocks
            return at

        pairs = (size + PAIR - 1) // PAIR
        lax.fori_loop(0, pairs, add_pair, number)
        number += pairs
        if (k + 1) % blocks == 0:
            for i in range(TURN - 1):
                first_of[number + i] = empty
                key_of[number + i] = 0
            number = (number + TURN - 1) // TURN * TURN
            bounds.append(number // TURN)
    acc[...] = jnp.zeros_like(acc)
    tile_buf[slots] = jnp.zeros_like(tile_buf[slots])
    for load in panel_loads:
        load.wait()

    def turn(g, carry):
        firsts = [first_of[g * TURN + i] for i in range(TURN)]
        if not resident:
            copies = [
                pltpu.make_async_copy(
                    panels.at[column[firsts[i] + j]],
                    panel_buf.at[i * PAIR + j],
                    panel_sem.at[i * PAIR + j],
                )
                for i in range(TURN)
                for j in range(PAIR)
            ]
            for copy in copies:
                copy.start()
            for copy in copies:
                copy.wait()
        for i, at in enumerate(firsts):
            left = jnp.concatenate([tile_buf[slot[at + j]] for j in range(PAIR)], axis=1)
            right = jnp.concatenate(
                [
                    panel_buf[column[at + j] if resident else i * PAIR + j]
                    for j in range(PAIR)
                ],
                axis=0,
            )
            acc[key_of[g * TURN + i]] += jnp.dot(left, right, preferred_element_type=F32)
        return carry

    for n, load in enumerate(tile_loads):
        load.wait()
        lax.fori_loop(bounds[n], bounds[n + 1], turn, 0)
    first = 0
    for out in outs:
        out[...] = acc[first : first + out.shape[0]]
        first += out.shape[0]


def tile_products(counts, places, tiles, panels, tile_rows, sizes, flip):
    slots, size, _ = tiles.shape
    width = panels.shape[2]
    blocks = 2 * sum(sizes)
    stride = (min(slots, panels.shape[0]) // PAIR + 1) * PAIR
    lists = PARTS * blocks
    entries = lists * stride + slots + PAIR
    pairs = lists * stride // PAIR + TURN * (PARTS + 1)
    resident = panels.size * 2 <= 16 << 20
    panel_shape = (panels.shape[0] if resident else PAIR * TURN, size, width)
    return pl.pallas_call(
        functools.partial(tile_kernel, resident, flip, stride),
        out_shape=[jax.ShapeDtypeStruct((n, size, width), F32) for n in (*sizes, *sizes)],
        in_specs=[SMEM, HBM, HBM, HBM],
        out_specs=[VMEM] * (2 * len(sizes)),
        scratch_shapes=[
            pltpu.VMEM((slots + 1, size, size), BF16),
            pltpu.VMEM(panel_shape, BF16),
            pltpu.SMEM((2, slots), jnp.int32),
            pltpu.SMEM((tile_rows,), jnp.int32),
            pltpu.SMEM((lists + 1,), jnp.int32),
            pltpu.SMEM((entries,), jnp.int32),
            pltpu.SMEM((entries,), jnp.int32),
            pltpu.SMEM((pairs,), jnp.int32),
            pltpu.SMEM((pairs,), jnp.int32),
            pltpu.VMEM((blocks, size, width), F32),
            pltpu.SemaphoreType.DMA((1 + PARTS,)),
            pltpu.SemaphoreType.DMA((1 if resident else PAIR * TURN,)),
        ],
        compiler_params=params(50 << 20),
    )(counts, in_hbm(places), tiles, panels)


def block_list(order):
    return [(i, j) for i in range(order) for j in range(i + 1)]


def gram_kernel(last, *refs):
    if last:
        keep, core, across, *earlier, rows, own, send, acc = refs
    else:
        keep, core, across, rows, acc = refs
    total = (keep[...] + core[...]) + across[...]
    total = total.reshape(rows.shape)
    rows[...] = total
    high, low = halves(total)
    left = jnp.concatenate([high, high, low], axis=0)
    right = jnp.concatenate([high, low, high], axis=0)
    order = rows.shape[1] // BLOCK
    for i in range(order):
        strip = lax.dot_general(
            left[:, i * BLOCK : (i + 1) * BLOCK],
            right[:, : (i + 1) * BLOCK],
            (((0,), (0,)), ((), ())),
            preferred_element_type=F32,
        )
        for j in range(i + 1):
            at = pl.ds((i * (i + 1) // 2 + j) * BLOCK, BLOCK)
            part = strip[:, j * BLOCK : (j + 1) * BLOCK]
            if last:
                for gram in earlier:
                    part = part + gram[at]
            acc[at] = part
    if last:
        core_bit, me = place()
        size = own.shape[1]
        half = acc.shape[0] // 2
        for d in range(own.shape[0]):
            at = (me ^ d) * size
            own[d] = acc[pl.ds(pl.multiple_of(core_bit * half + at, 8), size)]
            send[d] = acc[pl.ds(pl.multiple_of((1 - core_bit) * half + at, 8), size)]


def place():
    row, col = lax.axis_index("row"), lax.axis_index("col")
    return col & 1, (row & 1) | (col & 2)


def gram_chunk(keep, core, across, earlier, last):
    width = keep.shape[2]
    rows = keep.shape[0] * keep.shape[1]
    number = len(block_list(width // BLOCK)) * BLOCK
    whole = jax.ShapeDtypeStruct((number, BLOCK), F32)
    pieces = jax.ShapeDtypeStruct((4, number // 8, BLOCK), F32)
    row_shape = jax.ShapeDtypeStruct((rows, width), F32)
    args = [keep, core, across] + (list(earlier) if last else [])
    outs = [row_shape] + ([pieces, pieces] if last else [whole])
    return pl.pallas_call(
        functools.partial(gram_kernel, last),
        out_shape=outs,
        in_specs=[VMEM] * len(args),
        out_specs=[VMEM] * len(outs),
        scratch_shapes=[pltpu.VMEM(whole.shape, F32)] if last else [],
        compiler_params=params(16 << 20),
    )(*args)


def swapped(x, row_flip, col_flip):
    rows, cols = lax.axis_size("row"), lax.axis_size("col")
    if not row_flip:
        return lax.ppermute(x, "col", [(c, c ^ col_flip) for c in range(cols)])
    if not col_flip:
        return lax.ppermute(x, "row", [(r, r ^ row_flip) for r in range(rows)])
    route = [
        (r * cols + c, (r ^ row_flip) * cols + (c ^ col_flip))
        for r in range(rows)
        for c in range(cols)
    ]
    return lax.ppermute(x, ("row", "col"), route)


FLIPS = ((1, 0), (0, 2), (1, 2))


def gram_sum(own, send):
    theirs = swapped(send, 0, 1)
    part = [own[d] + theirs[d] for d in range(4)]
    got = [swapped(x, *flip) for x, flip in zip(part[1:], FLIPS)]
    piece = (part[0] + got[0]) + (got[1] + got[2])
    bits = lax.axis_size("row").bit_length() - 1
    bit = 1
    while bit < bits:
        if bit + 1 < bits:
            a, b = 1 << bit, 2 << bit
            got = [swapped(piece, flip, 0) for flip in (a, b, a | b)]
            piece = (piece + got[0]) + (got[1] + got[2])
            bit += 2
        else:
            piece = piece + swapped(piece, 1 << bit, 0)
            bit += 1
    mine = [piece] + [swapped(piece, *flip) for flip in FLIPS]
    return mine, [swapped(x, 0, 1) for x in mine]


def against(left, right_rows):
    lh, ll = left
    rh, rl = right_rows
    return lax.dot_general(
        jnp.concatenate([lh, lh, ll], axis=1),
        jnp.concatenate([rh, rl, rh], axis=1),
        (((1,), (1,)), ((), ())),
        preferred_element_type=F32,
    )


def times(left, right):
    lh, ll = left
    rh, rl = right
    return jnp.dot(
        jnp.concatenate([lh, lh, ll], axis=1),
        jnp.concatenate([rh, rl, rh], axis=0),
        preferred_element_type=F32,
    )


def factor_kernel(chunks, scale, rounds, *refs):
    pieces, rows = refs[:8], refs[8 : 8 + chunks]
    basis_out, triangle_out, gram, flag = refs[8 + chunks : 12 + chunks]
    blocks, half_mask, half_eye, w, basis, triangle, out_sem = refs[12 + chunks : 19 + chunks]
    wb, gh, gl, yh, yl, ph, dh, dl = refs[19 + chunks :]
    size = gram.shape[0]
    order = size // BLOCK
    core_bit, me = place()
    half = blocks.shape[0] // 2
    for n, piece in enumerate(pieces):
        at = (core_bit ^ (n // 4)) * half + (me ^ (n % 4)) * piece.shape[0]
        blocks[pl.ds(pl.multiple_of(at, 8), piece.shape[0])] = piece[...]
    at = [slice(i * BLOCK, (i + 1) * BLOCK) for i in range(order)]

    r = lax.broadcasted_iota(jnp.int32, (BLOCK, BLOCK), 0)
    c = lax.broadcasted_iota(jnp.int32, (BLOCK, BLOCK), 1)
    row_scale, col_scale = [], []
    for i in range(order):
        n = i * (i + 1) // 2 + i
        diagonal = jnp.where(r == c, blocks[n * BLOCK : (n + 1) * BLOCK], 0.0)
        row_scale.append(lax.rsqrt(jnp.sum(diagonal, axis=1, keepdims=True)))
        col_scale.append(lax.rsqrt(jnp.sum(diagonal, axis=0, keepdims=True)))
    for n, (i, j) in enumerate(block_list(order)):
        block = blocks[n * BLOCK : (n + 1) * BLOCK]
        first = -(block * row_scale[i] * col_scale[j])
        if i == j:
            first = jnp.where(r > c, first, jnp.where(r == c, 1.0, 0.0))
        wb[at[i], at[j]] = (first * col_scale[j]).astype(BF16)
        for p, q, x in [(i, j, block)] + ([(j, i, block.T)] if i != j else []):
            gram[at[p], at[q]] = x
            gh[at[p], at[q]], gl[at[p], at[q]] = halves(x)
        if i != j:
            wb[at[j], at[i]] = jnp.zeros((BLOCK, BLOCK), BF16)

    wide = size // 2
    top, low = slice(0, wide), slice(wide, size)
    r = lax.broadcasted_iota(jnp.int32, (wide, wide), 0)
    c = lax.broadcasted_iota(jnp.int32, (wide, wide), 1)
    half_mask[...] = jnp.where(r > c, 1.0, jnp.where(r == c, 0.5, 0.0))
    half_eye[...] = jnp.where(r == c, 0.5, 0.0)
    for ref in (ph, dh, dl):
        ref[top, low] = jnp.zeros((wide, wide), BF16)

    def dot(left, right):
        return jnp.dot(left, right, preferred_element_type=F32)

    def dot_rows(left, right):
        return lax.dot_general(left, right, (((1,), (1,)), ((), ())), preferred_element_type=F32)

    def twice(x, axis=1):
        return jnp.concatenate([x, x], axis=axis)

    def both(x, y, axis=1):
        return jnp.concatenate([x, y], axis=axis)

    def step(exact):
        for cols, k in ((top, wide), (low, size)):
            y = dot_rows(both(gh[:, :k], gl[:, :k]), twice(wb[cols, :k]))
            if exact:
                yh[:, cols], yl[:, cols] = halves(y)
            else:
                yh[:, cols] = y.astype(BF16)
        norm = jnp.zeros((1, 1), F32)
        strips = []
        for part, k in ((top, wide), (low, size)):
            if exact:
                m = dot(twice(wb[part, :k]), both(yh[:k, :k], yl[:k, :k], 0))
            else:
                m = dot(wb[part, :k], yh[:k, :k])
            corner = m[:, k - wide :] * half_mask[...] - half_eye[...]
            p = corner if k == wide else both(m[:, :wide], corner)
            ph[part, :k] = p.astype(BF16)
            strips.append(p)
            if exact:
                norm = norm + jnp.sum(p * p, keepdims=True)
        for p, part, k in zip(strips, (top, low), (wide, size)):
            square = dot(ph[part, :k], ph[:k, :k])
            cross = dot_rows(ph[part, :k], ph[:k, :k])
            corner = cross[:, k - wide :] * half_mask[...]
            cross = corner if k == wide else both(cross[:, :wide], corner)
            d = p - square - cross
            if exact:
                dh[part, :k], dl[part, :k] = halves(d)
            else:
                dh[part, :k] = d.astype(BF16)
        for part, k in ((top, wide), (low, size)):
            if exact:
                change = dot(both(dh[part, :k], dl[part, :k]), twice(wb[:k, :k], 0))
            else:
                change = dot(dh[part, :k], wb[:k, :k])
            w[part, :k] = wb[part, :k].astype(F32) - change
        return jnp.sum(norm)

    def rounded():
        for part, k in ((top, wide), (low, size)):
            wb[part, :k] = w[part, :k].astype(BF16)

    step(False)

    def not_done(state):
        count, norm = state
        return jnp.logical_and(count < rounds, jnp.logical_not(norm < SMALL))

    def again(state):
        rounded()
        return state[0] + 1, step(True)

    _, norm = lax.while_loop(not_done, again, (jnp.int32(0), jnp.float32(1.0)))
    flag[0] = jnp.where(norm < SMALL, 1, 0).astype(jnp.int32)
    for part, k in ((top, wide), (low, size)):
        wb[part, :k], dl[part, :k] = halves(w[part, :k])
    for part, k in ((top, wide), (low, size)):
        upper = times((wb[part, :k], dl[part, :k]), (gh[:k, k - wide :], gl[:k, k - wide :]))
        corner = jnp.where(r <= c, upper[:, :wide], 0.0)
        upper = both(corner, upper[:, wide:]) if k == wide else corner
        triangle[part, k - wide :] = upper * (1.0 / scale)
    triangle[low, top] = jnp.zeros((wide, wide), F32)
    copies = [pltpu.make_async_copy(triangle, triangle_out, out_sem.at[0])]
    copies[0].start()
    first = 0
    for part in rows:
        for head in range(0, part.shape[0], wide):
            count = min(wide, part.shape[0] - head)
            sh, sl = halves(part[head : head + count])
            here = pl.ds(first, count)
            for cols, k in ((top, wide), (low, size)):
                out = against((sh[:, :k], sl[:, :k]), (wb[cols, :k], dl[cols, :k]))
                basis[here, cols] = out * scale
            sem = out_sem.at[len(copies)]
            copies.append(pltpu.make_async_copy(basis.at[here], basis_out.at[here], sem))
            copies[-1].start()
            first += count
    for copy in copies:
        copy.wait()


def factor(pieces, rows, scale):
    width = rows[0].shape[1]
    square = (width, width)
    local = sum(part.shape[0] for part in rows)
    number = len(block_list(width // BLOCK))
    return pl.pallas_call(
        functools.partial(factor_kernel, len(rows), scale, 12),
        out_shape=[
            pltpu.HBM((local, width), F32),
            pltpu.HBM(square, F32),
            jax.ShapeDtypeStruct(square, F32),
            jax.ShapeDtypeStruct((1,), jnp.int32),
        ],
        in_specs=[VMEM] * (8 + len(rows)),
        out_specs=[HBM, HBM, VMEM, SMEM],
        scratch_shapes=[
            pltpu.VMEM((number * BLOCK, BLOCK), F32),
            pltpu.VMEM((width // 2, width // 2), F32),
            pltpu.VMEM((width // 2, width // 2), F32),
            pltpu.VMEM(square, F32),
            pltpu.VMEM((local, width), F32),
            pltpu.VMEM(square, F32),
            pltpu.SemaphoreType.DMA((1 + sum(-(-part.shape[0] * 2 // width) for part in rows),)),
        ]
        + [pltpu.VMEM(square, BF16)] * 8,
        compiler_params=params(24 << 20),
    )(*pieces, *rows)


def direct(gram, rows, scale):
    lower = jnp.linalg.cholesky(gram)
    own_rows = jnp.concatenate(rows, axis=0)
    basis = jax.scipy.linalg.solve_triangular(lower, own_rows.T, lower=True).T * scale
    return basis, lower.T / scale


def body(tile_values, tile_places, tile_counts, sketch):
    tiles = tile_values[0, 0]
    size = tiles.shape[1]
    width = sketch.shape[1]
    row_devices = lax.axis_size("row")
    col_devices = lax.axis_size("col")
    local_rows = sketch.shape[0] // row_devices
    tile_rows = local_rows * col_devices // size
    panels = sketch.reshape(-1, size, width)
    places = tile_places[0, 0]
    scale = math.sqrt(local_rows * row_devices * col_devices)
    per_owner = tile_rows // col_devices
    first = max(1, per_owner // 6)
    sizes = (first, per_owner - first) if per_owner > first else (first,)
    chunks = len(sizes)

    def products(flip):
        out = tile_products(tile_counts, places, tiles, panels, tile_rows, sizes, flip)
        return list(out[:chunks]), list(out[chunks:])

    send, keep = products(1)
    own, core = [], None
    for n in range(chunks):
        if n:
            send[n], core = lax.optimization_barrier((send[n], core))
        core = swapped(send[n], 0, 1)
        own.append(keep[n] + core)
    across = [swapped(x, 0, 2) for x in own]
    places, own = lax.optimization_barrier((places, own))
    send, keep = products(0)
    send, keep, across[0] = lax.optimization_barrier((send, keep, across[0]))
    rows, grams = [], []
    for n in range(chunks):
        out = gram_chunk(keep[n], swapped(send[n], 0, 1), across[n], grams, n == chunks - 1)
        rows.append(out[0])
        grams.append(out[1])
    mine, theirs = gram_sum(*out[1:])
    basis, triangle, gram, flag = factor(mine + theirs, rows, scale)
    return lax.cond(
        flag[0] == 1,
        lambda: (basis, triangle),
        lambda: direct(gram, rows, scale),
    )


def solution(mesh):
    in_specs = (
        P("row", "col", None, None, None),
        P("row", "col", None, None),
        P("row", "col"),
        P("col", None),
    )
    out_specs = (P(("row", "col"), None), P())
    return jax.shard_map(body, mesh=mesh, in_specs=in_specs, out_specs=out_specs, check_vma=False)
```

```python
import functools
import math

import jax
import jax.numpy as jnp
from jax import lax
from jax.experimental import pallas as pl
from jax.experimental.pallas import tpu as pltpu
from jax.sharding import PartitionSpec as P

BF16 = jnp.bfloat16
F32 = jnp.float32
PAIR = 2
TURN = 12
PARTS = 2
BLOCK = 128
SMALL = 0.01
SMEM = pl.BlockSpec(memory_space=pltpu.SMEM)
VMEM = pl.BlockSpec(memory_space=pltpu.VMEM)
HBM = pl.BlockSpec(memory_space=pltpu.HBM)

def in_hbm(x):
    return pltpu.with_memory_space_constraint(x, pltpu.HBM)


def params(size):
    return pltpu.CompilerParams(vmem_limit_bytes=size)


def halves(x):
    high = x.astype(BF16)
    return high, (x - high.astype(F32)).astype(BF16)


def tile_kernel(resident, flip, stride, counts, places, tiles, panels, *refs):
    outs, refs = refs[:-12], refs[-12:]
    tile_buf, panel_buf, place_of, key, fill, slot, column, first_of, key_of = refs[:9]
    acc, load_sem, panel_sem = refs[9:]
    slots = tiles.shape[0]
    blocks = acc.shape[0]
    per_owner = blocks // 2
    place_load = pltpu.make_async_copy(places, place_of, load_sem.at[0])
    panel_loads = [pltpu.make_async_copy(panels, panel_buf, panel_sem.at[0])] if resident else []
    cuts = [slots * n // PARTS for n in range(PARTS + 1)]
    tile_loads = [
        pltpu.make_async_copy(
            tiles.at[pl.ds(a, b - a)], tile_buf.at[pl.ds(a, b - a)], load_sem.at[1 + n]
        )
        for n, (a, b) in enumerate(zip(cuts, cuts[1:]))
    ]
    for load in [place_load] + panel_loads + tile_loads:
        load.start()
    own = lax.axis_index("col")

    for owner in range(key.shape[0] // per_owner):
        base = jnp.where((owner & 1) == (own & 1), per_owner, 0)
        wanted = (owner >> 1) == ((own >> 1) ^ flip)
        for inside in range(per_owner):
            key[owner * per_owner + inside] = jnp.where(wanted, base + inside, blocks)
    lists = PARTS * blocks
    for k in range(lists + 1):
        fill[k] = k * stride
    place_load.wait()
    live = counts[0, 0]

    unroll = math.gcd(slots, 8)

    def put(g, carry):
        for i in range(unroll):
            t = g * unroll + i
            part = sum(jnp.where(t >= cut, blocks, 0) for cut in cuts[1:-1])
            row = key[place_of[0, t]]
            k = jnp.where(jnp.logical_and(t < live, row < blocks), part + row, lists)
            p = fill[k]
            fill[k] = p + 1
            slot[p] = t
            column[p] = place_of[1, t]
        return carry

    lax.fori_loop(0, (live + unroll - 1) // unroll, put, 0)

    empty = lists * stride + slots
    for i in range(PAIR):
        slot[empty + i] = slots
        column[empty + i] = 0
    number, bounds = 0, [0]
    for k in range(lists):
        size = fill[k] - k * stride
        for i in range(PAIR - 1):
            slot[fill[k] + i] = slots
            column[fill[k] + i] = 0

        def add_pair(j, at, k=k):
            first_of[at + j] = k * stride + j * PAIR
            key_of[at + j] = k % blocks
            return at

        pairs = (size + PAIR - 1) // PAIR
        lax.fori_loop(0, pairs, add_pair, number)
        number += pairs
        if (k + 1) % blocks == 0:
            for i in range(TURN - 1):
                first_of[number + i] = empty
                key_of[number + i] = 0
            number = (number + TURN - 1) // TURN * TURN
            bounds.append(number // TURN)
    acc[...] = jnp.zeros_like(acc)
    tile_buf[slots] = jnp.zeros_like(tile_buf[slots])
    for load in panel_loads:
        load.wait()

    def turn(g, carry):
        firsts = [first_of[g * TURN + i] for i in range(TURN)]
        if not resident:
            copies = [
                pltpu.make_async_copy(
                    panels.at[column[firsts[i] + j]],
                    panel_buf.at[i * PAIR + j],
                    panel_sem.at[i * PAIR + j],
                )
                for i in range(TURN)
                for j in range(PAIR)
            ]
            for copy in copies:
                copy.start()
            for copy in copies:
                copy.wait()
        for i, at in enumerate(firsts):
            left = jnp.concatenate([tile_buf[slot[at + j]] for j in range(PAIR)], axis=1)
            right = jnp.concatenate(
                [
                    panel_buf[column[at + j] if resident else i * PAIR + j]
                    for j in range(PAIR)
                ],
                axis=0,
            )
            acc[key_of[g * TURN + i]] += jnp.dot(left, right, preferred_element_type=F32)
        return carry

    for n, load in enumerate(tile_loads):
        load.wait()
        lax.fori_loop(bounds[n], bounds[n + 1], turn, 0)
    first = 0
    for out in outs:
        out[...] = acc[first : first + out.shape[0]]
        first += out.shape[0]


def tile_products(counts, places, tiles, panels, tile_rows, sizes, flip):
    slots, size, _ = tiles.shape
    width = panels.shape[2]
    blocks = 2 * sum(sizes)
    stride = (min(slots, panels.shape[0]) // PAIR + 1) * PAIR
    lists = PARTS * blocks
    entries = lists * stride + slots + PAIR
    pairs = lists * stride // PAIR + TURN * (PARTS + 1)
    resident = panels.size * 2 <= 16 << 20
    panel_shape = (panels.shape[0] if resident else PAIR * TURN, size, width)
    return pl.pallas_call(
        functools.partial(tile_kernel, resident, flip, stride),
        out_shape=[jax.ShapeDtypeStruct((n, size, width), F32) for n in (*sizes, *sizes)],
        in_specs=[SMEM, HBM, HBM, HBM],
        out_specs=[VMEM] * (2 * len(sizes)),
        scratch_shapes=[
            pltpu.VMEM((slots + 1, size, size), BF16),
            pltpu.VMEM(panel_shape, BF16),
            pltpu.SMEM((2, slots), jnp.int32),
            pltpu.SMEM((tile_rows,), jnp.int32),
            pltpu.SMEM((lists + 1,), jnp.int32),
            pltpu.SMEM((entries,), jnp.int32),
            pltpu.SMEM((entries,), jnp.int32),
            pltpu.SMEM((pairs,), jnp.int32),
            pltpu.SMEM((pairs,), jnp.int32),
            pltpu.VMEM((blocks, size, width), F32),
            pltpu.SemaphoreType.DMA((1 + PARTS,)),
            pltpu.SemaphoreType.DMA((1 if resident else PAIR * TURN,)),
        ],
        compiler_params=params(50 << 20),
    )(counts, in_hbm(places), tiles, panels)


def gram_rows(order):
    under = [(i, j) for i in range(order) for j in range(i)]
    heads = {block: n * BLOCK for n, block in enumerate(under)}
    first = len(under) * BLOCK
    pairs = []
    for i in range(0, order, 2):
        pairs.append((i, i + 1, first, 0))
        first += BLOCK
    pairs = [(i, j, head, first + n) for n, (i, j, head, _) in enumerate(pairs)]
    return heads, pairs, first, -(-(first + len(pairs)) // 64) * 64


def square_index():
    return (
        lax.broadcasted_iota(jnp.int32, (BLOCK, BLOCK), 0),
        lax.broadcasted_iota(jnp.int32, (BLOCK, BLOCK), 1),
    )


def gram_kernel(last, *refs):
    if last:
        keep, core, across, *earlier, rows, own, send, acc = refs
    else:
        keep, core, across, rows, acc = refs
    total = (keep[...] + core[...]) + across[...]
    total = total.reshape(rows.shape)
    rows[...] = total
    high, low = halves(total)
    left = jnp.concatenate([high, high, low], axis=0)
    right = jnp.concatenate([high, low, high], axis=0)
    order = rows.shape[1] // BLOCK
    heads, pairs, slab, number = gram_rows(order)
    diagonal = {}
    for i in range(order):
        strip = lax.dot_general(
            left[:, i * BLOCK : (i + 1) * BLOCK],
            right[:, : (i + 1) * BLOCK],
            (((0,), (0,)), ((), ())),
            preferred_element_type=F32,
        )
        for j in range(i):
            acc[pl.ds(heads[i, j], BLOCK)] = strip[:, j * BLOCK : (j + 1) * BLOCK]
        diagonal[i] = strip[:, i * BLOCK :]
    acc[pl.ds(slab, number - slab)] = jnp.zeros((number - slab, BLOCK), F32)
    r, c = square_index()
    for i, j, head, line in pairs:
        acc[pl.ds(head, BLOCK)] = jnp.where(r >= c, diagonal[i], diagonal[j])
        acc[pl.ds(line, 1)] = jnp.sum(jnp.where(r == c, diagonal[j], 0.0), axis=0, keepdims=True)
    if last:
        for gram in earlier:
            acc[...] += gram[...]
    if last:
        core_bit, me = place()
        size = own.shape[1]
        half = acc.shape[0] // 2
        for d in range(own.shape[0]):
            at = (me ^ d) * size
            own[d] = acc[pl.ds(pl.multiple_of(core_bit * half + at, 8), size)]
            send[d] = acc[pl.ds(pl.multiple_of((1 - core_bit) * half + at, 8), size)]


def place():
    row, col = lax.axis_index("row"), lax.axis_index("col")
    return col & 1, (row & 1) | (col & 2)


def gram_chunk(keep, core, across, earlier, last):
    width = keep.shape[2]
    rows = keep.shape[0] * keep.shape[1]
    number = gram_rows(width // BLOCK)[3]
    whole = jax.ShapeDtypeStruct((number, BLOCK), F32)
    pieces = jax.ShapeDtypeStruct((4, number // 8, BLOCK), F32)
    row_shape = jax.ShapeDtypeStruct((rows, width), F32)
    args = [keep, core, across] + (list(earlier) if last else [])
    outs = [row_shape] + ([pieces, pieces] if last else [whole])
    return pl.pallas_call(
        functools.partial(gram_kernel, last),
        out_shape=outs,
        in_specs=[VMEM] * len(args),
        out_specs=[VMEM] * len(outs),
        scratch_shapes=[pltpu.VMEM(whole.shape, F32)] if last else [],
        compiler_params=params(16 << 20),
    )(*args)


def swapped(x, row_flip, col_flip):
    rows, cols = lax.axis_size("row"), lax.axis_size("col")
    if not row_flip:
        return lax.ppermute(x, "col", [(c, c ^ col_flip) for c in range(cols)])
    if not col_flip:
        return lax.ppermute(x, "row", [(r, r ^ row_flip) for r in range(rows)])
    route = [
        (r * cols + c, (r ^ row_flip) * cols + (c ^ col_flip))
        for r in range(rows)
        for c in range(cols)
    ]
    return lax.ppermute(x, ("row", "col"), route)


FLIPS = ((1, 0), (0, 2), (1, 2))


def gram_sum(own, send):
    theirs = swapped(send, 0, 1)
    part = [own[d] + theirs[d] for d in range(4)]
    got = [swapped(x, *flip) for x, flip in zip(part[1:], FLIPS)]
    piece = (part[0] + got[0]) + (got[1] + got[2])
    bits = lax.axis_size("row").bit_length() - 1
    bit = 1
    while bit < bits:
        if bit + 1 < bits:
            a, b = 1 << bit, 2 << bit
            got = [swapped(piece, flip, 0) for flip in (a, b, a | b)]
            piece = (piece + got[0]) + (got[1] + got[2])
            bit += 2
        else:
            piece = piece + swapped(piece, 1 << bit, 0)
            bit += 1
    mine = [piece] + [swapped(piece, *flip) for flip in FLIPS]
    return mine, [swapped(x, 0, 1) for x in mine]


def against(left, right_rows):
    lh, ll = left
    rh, rl = right_rows
    return lax.dot_general(
        jnp.concatenate([lh, lh, ll], axis=1),
        jnp.concatenate([rh, rl, rh], axis=1),
        (((1,), (1,)), ((), ())),
        preferred_element_type=F32,
    )


def times(left, right):
    lh, ll = left
    rh, rl = right
    return jnp.dot(
        jnp.concatenate([lh, lh, ll], axis=1),
        jnp.concatenate([rh, rl, rh], axis=0),
        preferred_element_type=F32,
    )


def factor_kernel(chunks, scale, rounds, *refs):
    pieces, rows = refs[:8], refs[8 : 8 + chunks]
    basis_out, triangle_out, gram, flag = refs[8 + chunks : 12 + chunks]
    blocks, half_mask, half_eye, w, basis, triangle, out_sem = refs[12 + chunks : 19 + chunks]
    wb, gh, gl, yh, yl, ph, dh, dl = refs[19 + chunks :]
    size = gram.shape[0]
    order = size // BLOCK
    core_bit, me = place()
    half = blocks.shape[0] // 2
    for n, piece in enumerate(pieces):
        at = (core_bit ^ (n // 4)) * half + (me ^ (n % 4)) * piece.shape[0]
        blocks[pl.ds(pl.multiple_of(at, 8), piece.shape[0])] = piece[...]
    at = [slice(i * BLOCK, (i + 1) * BLOCK) for i in range(order)]

    r, c = square_index()
    row_scale, col_scale = [], []
    heads, pairs, _, _ = gram_rows(order)
    lower = {}
    for i, j, head, line in pairs:
        packed = blocks[pl.ds(head, BLOCK)]
        turned = packed.T
        lower[i, i] = jnp.where(r >= c, packed, turned)
        lower[j, j] = jnp.where(
            r < c, packed, jnp.where(r == c, blocks[pl.ds(line, 1)], turned)
        )
    for i in range(order):
        diagonal = jnp.where(r == c, lower[i, i], 0.0)
        row_scale.append(lax.rsqrt(jnp.sum(diagonal, axis=1, keepdims=True)))
        col_scale.append(lax.rsqrt(jnp.sum(diagonal, axis=0, keepdims=True)))
    for i, j in [(i, j) for i in range(order) for j in range(i + 1)]:
        block = lower[i, i] if i == j else blocks[pl.ds(heads[i, j], BLOCK)]
        first = -(block * row_scale[i] * col_scale[j])
        if i == j:
            first = jnp.where(r > c, first, jnp.where(r == c, 1.0, 0.0))
        wb[at[i], at[j]] = (first * col_scale[j]).astype(BF16)
        for p, q, x in [(i, j, block)] + ([(j, i, block.T)] if i != j else []):
            gram[at[p], at[q]] = x
            gh[at[p], at[q]], gl[at[p], at[q]] = halves(x)
        if i != j:
            wb[at[j], at[i]] = jnp.zeros((BLOCK, BLOCK), BF16)

    wide = size // 2
    top, low = slice(0, wide), slice(wide, size)
    r = lax.broadcasted_iota(jnp.int32, (wide, wide), 0)
    c = lax.broadcasted_iota(jnp.int32, (wide, wide), 1)
    half_mask[...] = jnp.where(r > c, 1.0, jnp.where(r == c, 0.5, 0.0))
    half_eye[...] = jnp.where(r == c, 0.5, 0.0)
    for ref in (ph, dh, dl):
        ref[top, low] = jnp.zeros((wide, wide), BF16)

    def dot(left, right):
        return jnp.dot(left, right, preferred_element_type=F32)

    def dot_rows(left, right):
        return lax.dot_general(left, right, (((1,), (1,)), ((), ())), preferred_element_type=F32)

    def twice(x, axis=1):
        return jnp.concatenate([x, x], axis=axis)

    def both(x, y, axis=1):
        return jnp.concatenate([x, y], axis=axis)

    def step(exact):
        for cols, k in ((top, wide), (low, size)):
            y = dot_rows(both(gh[:, :k], gl[:, :k]), twice(wb[cols, :k]))
            if exact:
                yh[:, cols], yl[:, cols] = halves(y)
            else:
                yh[:, cols] = y.astype(BF16)
        norm = jnp.zeros((1, 1), F32)
        strips = []
        for part, k in ((top, wide), (low, size)):
            if exact:
                m = dot(twice(wb[part, :k]), both(yh[:k, :k], yl[:k, :k], 0))
            else:
                m = dot(wb[part, :k], yh[:k, :k])
            corner = m[:, k - wide :] * half_mask[...] - half_eye[...]
            p = corner if k == wide else both(m[:, :wide], corner)
            ph[part, :k] = p.astype(BF16)
            strips.append(p)
            if exact:
                norm = norm + jnp.sum(p * p, keepdims=True)
        for p, part, k in zip(strips, (top, low), (wide, size)):
            square = dot(ph[part, :k], ph[:k, :k])
            cross = dot_rows(ph[part, :k], ph[:k, :k])
            corner = cross[:, k - wide :] * half_mask[...]
            cross = corner if k == wide else both(cross[:, :wide], corner)
            d = p - square - cross
            if exact:
                dh[part, :k], dl[part, :k] = halves(d)
            else:
                dh[part, :k] = d.astype(BF16)
        for part, k in ((top, wide), (low, size)):
            if exact:
                change = dot(both(dh[part, :k], dl[part, :k]), twice(wb[:k, :k], 0))
            else:
                change = dot(dh[part, :k], wb[:k, :k])
            w[part, :k] = wb[part, :k].astype(F32) - change
        return jnp.sum(norm)

    def rounded():
        for part, k in ((top, wide), (low, size)):
            wb[part, :k] = w[part, :k].astype(BF16)

    step(False)

    def not_done(state):
        count, norm = state
        return jnp.logical_and(count < rounds, jnp.logical_not(norm < SMALL))

    def again(state):
        rounded()
        return state[0] + 1, step(True)

    _, norm = lax.while_loop(not_done, again, (jnp.int32(0), jnp.float32(1.0)))
    flag[0] = jnp.where(norm < SMALL, 1, 0).astype(jnp.int32)
    for part, k in ((top, wide), (low, size)):
        wb[part, :k], dl[part, :k] = halves(w[part, :k])
    for part, k in ((top, wide), (low, size)):
        upper = times((wb[part, :k], dl[part, :k]), (gh[:k, k - wide :], gl[:k, k - wide :]))
        corner = jnp.where(r <= c, upper[:, :wide], 0.0)
        upper = both(corner, upper[:, wide:]) if k == wide else corner
        triangle[part, k - wide :] = upper * (1.0 / scale)
    triangle[low, top] = jnp.zeros((wide, wide), F32)
    copies = [pltpu.make_async_copy(triangle, triangle_out, out_sem.at[0])]
    copies[0].start()
    first = 0
    for part in rows:
        for head in range(0, part.shape[0], wide):
            count = min(wide, part.shape[0] - head)
            sh, sl = halves(part[head : head + count])
            here = pl.ds(first, count)
            for cols, k in ((top, wide), (low, size)):
                out = against((sh[:, :k], sl[:, :k]), (wb[cols, :k], dl[cols, :k]))
                basis[here, cols] = out * scale
            sem = out_sem.at[len(copies)]
            copies.append(pltpu.make_async_copy(basis.at[here], basis_out.at[here], sem))
            copies[-1].start()
            first += count
    for copy in copies:
        copy.wait()


def factor(pieces, rows, scale):
    width = rows[0].shape[1]
    square = (width, width)
    local = sum(part.shape[0] for part in rows)
    number = gram_rows(width // BLOCK)[3]
    return pl.pallas_call(
        functools.partial(factor_kernel, len(rows), scale, 12),
        out_shape=[
            pltpu.HBM((local, width), F32),
            pltpu.HBM(square, F32),
            jax.ShapeDtypeStruct(square, F32),
            jax.ShapeDtypeStruct((1,), jnp.int32),
        ],
        in_specs=[VMEM] * (8 + len(rows)),
        out_specs=[HBM, HBM, VMEM, SMEM],
        scratch_shapes=[
            pltpu.VMEM((number, BLOCK), F32),
            pltpu.VMEM((width // 2, width // 2), F32),
            pltpu.VMEM((width // 2, width // 2), F32),
            pltpu.VMEM(square, F32),
            pltpu.VMEM((local, width), F32),
            pltpu.VMEM(square, F32),
            pltpu.SemaphoreType.DMA((1 + sum(-(-part.shape[0] * 2 // width) for part in rows),)),
        ]
        + [pltpu.VMEM(square, BF16)] * 8,
        compiler_params=params(24 << 20),
    )(*pieces, *rows)


def direct(gram, rows, scale):
    lower = jnp.linalg.cholesky(gram)
    own_rows = jnp.concatenate(rows, axis=0)
    basis = jax.scipy.linalg.solve_triangular(lower, own_rows.T, lower=True).T * scale
    return basis, lower.T / scale


def body(tile_values, tile_places, tile_counts, sketch):
    tiles = tile_values[0, 0]
    size = tiles.shape[1]
    width = sketch.shape[1]
    row_devices = lax.axis_size("row")
    col_devices = lax.axis_size("col")
    local_rows = sketch.shape[0] // row_devices
    tile_rows = local_rows * col_devices // size
    panels = sketch.reshape(-1, size, width)
    places = tile_places[0, 0]
    scale = math.sqrt(local_rows * row_devices * col_devices)
    per_owner = tile_rows // col_devices
    sizes = tuple(n for n in (per_owner // 6, per_owner - 3 * (per_owner // 6), 2 * (per_owner // 6)) if n)
    chunks = len(sizes)

    def products(flip):
        out = tile_products(tile_counts, places, tiles, panels, tile_rows, sizes, flip)
        return list(out[:chunks]), list(out[chunks:])

    send, keep = products(1)
    own, core = [], None
    for n in range(chunks):
        if n:
            send[n], core = lax.optimization_barrier((send[n], core))
        core = swapped(send[n], 0, 1)
        own.append(keep[n] + core)
    across = [swapped(x, 0, 2) for x in own]
    places, own = lax.optimization_barrier((places, own))
    send, keep = products(0)
    send, keep, across[0] = lax.optimization_barrier((send, keep, across[0]))
    rows, grams = [], []
    for n in range(chunks):
        out = gram_chunk(keep[n], swapped(send[n], 0, 1), across[n], grams, n == chunks - 1)
        rows.append(out[0])
        grams.append(out[1])
    mine, theirs = gram_sum(*out[1:])
    basis, triangle, gram, flag = factor(mine + theirs, rows, scale)
    return lax.cond(
        flag[0] == 1,
        lambda: (basis, triangle),
        lambda: direct(gram, rows, scale),
    )


def solution(mesh):
    in_specs = (
        P("row", "col", None, None, None),
        P("row", "col", None, None),
        P("row", "col"),
        P("col", None),
    )
    out_specs = (P(("row", "col"), None), P())
    return jax.shard_map(body, mesh=mesh, in_specs=in_specs, out_specs=out_specs, check_vma=False)
```

```python
import functools
import math

import jax
import jax.numpy as jnp
from jax import lax
from jax.experimental import pallas as pl
from jax.experimental.pallas import tpu as pltpu
from jax.sharding import PartitionSpec as P

BF16 = jnp.bfloat16
F32 = jnp.float32
PAIR = 2
TURN = 16
PARTS = 2
BLOCK = 128
SMALL = 0.01
SMEM = pl.BlockSpec(memory_space=pltpu.SMEM)
VMEM = pl.BlockSpec(memory_space=pltpu.VMEM)
HBM = pl.BlockSpec(memory_space=pltpu.HBM)

def in_hbm(x):
    return pltpu.with_memory_space_constraint(x, pltpu.HBM)


def params(size):
    return pltpu.CompilerParams(vmem_limit_bytes=size)


def halves(x):
    high = x.astype(BF16)
    return high, (x - high.astype(F32)).astype(BF16)


def tile_kernel(resident, spans, stride, counts, places, tiles, panels, *refs):
    outs, refs = refs[: 2 * len(spans)], refs[2 * len(spans) :]
    tile_buf, panel_buf, place_of, key, first_of, key_of, acc, load_sem, panel_sem = refs[:9]
    fill, entry = refs[9 : 9 + PARTS], refs[9 + PARTS :]
    slots = tiles.shape[0]
    blocks = acc.shape[0]
    per_owner = key.shape[0] // lax.axis_size("col")
    panel_loads = [pltpu.make_async_copy(panels, panel_buf, panel_sem.at[0])] if resident else []
    cuts = [-(-slots * n // PARTS) for n in range(PARTS + 1)]
    tile_loads = [
        pltpu.make_async_copy(
            tiles.at[pl.ds(a, b - a)], tile_buf.at[pl.ds(a, b - a)], load_sem.at[1 + n]
        )
        for n, (a, b) in enumerate(zip(cuts, cuts[1:]))
    ]
    place_load = pltpu.make_async_copy(places, place_of, load_sem.at[0])
    for load in [place_load] + panel_loads + tile_loads:
        load.start()
    own = lax.axis_index("col")

    heads = {}
    for n, (flip, head, end) in enumerate(spans):
        for inside in range(head, end):
            heads[flip, inside] = sum(e - h for _, h, e in spans[:n]) + inside - head
    for owner in range(key.shape[0] // per_owner):
        base = jnp.where((owner & 1) == (own & 1), blocks // 2, 0)
        flipped = (owner >> 1) != (own >> 1)
        for inside in range(per_owner):
            name = [base + heads[f, inside] if (f, inside) in heads else blocks for f in (0, 1)]
            key[owner * per_owner + inside] = jnp.where(flipped, name[1], name[0])
    for n in range(PARTS):
        for k in range(blocks + 1):
            fill[n][k] = k * stride
    place_load.wait()
    live = counts[0, 0]
    shift = panels.shape[0].bit_length()
    unroll = math.gcd(cuts[1], 6)

    def put(g, carry):
        for i in range(unroll):
            mine = [jnp.minimum(cut + g * unroll + i, slots - 1) for cut in cuts[:-1]]
            names = [key[place_of[0, t]] for t in mine]
            made = [(t << shift) | place_of[1, t] for t in mine]
            lists = [
                jnp.where(cut + g * unroll + i < live, name, blocks)
                for cut, name in zip(cuts, names)
            ]
            spots = [fill[n][k] for n, k in enumerate(lists)]
            for n in range(PARTS):
                fill[n][lists[n]] = spots[n] + 1
                entry[n][spots[n]] = made[n]
        return carry

    lax.fori_loop(0, (jnp.minimum(live, cuts[1]) + unroll - 1) // unroll, put, 0)

    empty = blocks * stride + cuts[1]
    number, bounds = 0, [0]
    for n in range(PARTS):
        for i in range(PAIR):
            entry[n][empty + i] = slots << shift
        for k in range(blocks):
            size = fill[n][k] - k * stride
            for i in range(PAIR - 1):
                entry[n][fill[n][k] + i] = slots << shift

            def add_pair(j, at, k=k):
                first_of[at + j] = k * stride + j * PAIR
                key_of[at + j] = k
                return at

            pairs = (size + PAIR - 1) // PAIR
            lax.fori_loop(0, pairs, add_pair, number)
            number += pairs
        for i in range(TURN - 1):
            first_of[number + i] = empty
            key_of[number + i] = 0
        number = (number + TURN - 1) // TURN * TURN
        bounds.append(number // TURN)
    acc[...] = jnp.zeros_like(acc)
    tile_buf[slots] = jnp.zeros_like(tile_buf[slots])
    for load in panel_loads:
        load.wait()

    def turn(n, g, carry):
        firsts = [first_of[g * TURN + i] for i in range(TURN)]
        entries = [[entry[n][at + j] for j in range(PAIR)] for at in firsts]
        slot = [[e >> shift for e in pair] for pair in entries]
        column = [[e & ((1 << shift) - 1) for e in pair] for pair in entries]
        if not resident:
            copies = [
                pltpu.make_async_copy(
                    panels.at[column[i][j]],
                    panel_buf.at[i * PAIR + j],
                    panel_sem.at[i * PAIR + j],
                )
                for i in range(TURN)
                for j in range(PAIR)
            ]
            for copy in copies:
                copy.start()
            for copy in copies:
                copy.wait()
        for i in range(TURN):
            left = jnp.concatenate([tile_buf[slot[i][j]] for j in range(PAIR)], axis=1)
            right = jnp.concatenate(
                [panel_buf[column[i][j] if resident else i * PAIR + j] for j in range(PAIR)],
                axis=0,
            )
            acc[key_of[g * TURN + i]] += jnp.dot(left, right, preferred_element_type=F32)
        return carry

    for n, load in enumerate(tile_loads):
        load.wait()
        lax.fori_loop(bounds[n], bounds[n + 1], functools.partial(turn, n), 0)
    first = 0
    for out in outs:
        out[...] = acc[first : first + out.shape[0]]
        first += out.shape[0]


def tile_products(counts, places, tiles, panels, tile_rows, spans):
    slots, size, _ = tiles.shape
    width = panels.shape[2]
    sizes = [end - head for _, head, end in spans] * 2
    blocks = sum(sizes)
    part = -(-slots // PARTS)
    stride = (min(part, panels.shape[0]) // PAIR + 1) * PAIR
    pairs = PARTS * blocks * stride // PAIR + TURN * (PARTS + 1)
    resident = panels.size * 2 <= 16 << 20
    panel_shape = (panels.shape[0] if resident else PAIR * TURN, size, width)
    return pl.pallas_call(
        functools.partial(tile_kernel, resident, spans, stride),
        out_shape=[jax.ShapeDtypeStruct((n, size, width), F32) for n in sizes],
        in_specs=[SMEM, HBM, HBM, HBM],
        out_specs=[VMEM] * len(sizes),
        scratch_shapes=[
            pltpu.VMEM((slots + 1, size, size), BF16),
            pltpu.VMEM(panel_shape, BF16),
            pltpu.SMEM((2, slots), jnp.int32),
            pltpu.SMEM((tile_rows,), jnp.int32),
            pltpu.SMEM((pairs,), jnp.int32),
            pltpu.SMEM((pairs,), jnp.int32),
            pltpu.VMEM((blocks, size, width), F32),
            pltpu.SemaphoreType.DMA((1 + PARTS,)),
            pltpu.SemaphoreType.DMA((1 if resident else PAIR * TURN,)),
        ]
        + [pltpu.SMEM((blocks + 1,), jnp.int32)] * PARTS
        + [pltpu.SMEM((blocks * stride + part + PAIR,), jnp.int32)] * PARTS,
        compiler_params=params(50 << 20),
    )(counts, in_hbm(places), tiles, panels)


def gram_rows(order):
    under = [(i, j) for i in range(order) for j in range(i)]
    heads = {block: n * BLOCK for n, block in enumerate(under)}
    first = len(under) * BLOCK
    pairs = []
    for i in range(0, order, 2):
        pairs.append((i, i + 1, first, 0))
        first += BLOCK
    pairs = [(i, j, head, first + n) for n, (i, j, head, _) in enumerate(pairs)]
    return heads, pairs, first, -(-(first + len(pairs)) // 64) * 64


def square_index():
    return (
        lax.broadcasted_iota(jnp.int32, (BLOCK, BLOCK), 0),
        lax.broadcasted_iota(jnp.int32, (BLOCK, BLOCK), 1),
    )


def gram_kernel(last, *refs):
    if last:
        keep, core, across, *earlier, rows, own, send, acc = refs
    else:
        keep, core, across, rows, acc = refs
    total = (keep[...] + core[...]) + across[...]
    total = total.reshape(rows.shape)
    rows[...] = total
    high, low = halves(total)
    left = jnp.concatenate([high, high, low], axis=0)
    right = jnp.concatenate([high, low, high], axis=0)
    order = rows.shape[1] // BLOCK
    heads, pairs, slab, number = gram_rows(order)
    diagonal = {}
    for i in range(order):
        strip = lax.dot_general(
            left[:, i * BLOCK : (i + 1) * BLOCK],
            right[:, : (i + 1) * BLOCK],
            (((0,), (0,)), ((), ())),
            preferred_element_type=F32,
        )
        for j in range(i):
            acc[pl.ds(heads[i, j], BLOCK)] = strip[:, j * BLOCK : (j + 1) * BLOCK]
        diagonal[i] = strip[:, i * BLOCK :]
    acc[pl.ds(slab, number - slab)] = jnp.zeros((number - slab, BLOCK), F32)
    r, c = square_index()
    for i, j, head, line in pairs:
        acc[pl.ds(head, BLOCK)] = jnp.where(r >= c, diagonal[i], diagonal[j])
        acc[pl.ds(line, 1)] = jnp.sum(jnp.where(r == c, diagonal[j], 0.0), axis=0, keepdims=True)
    if last:
        for gram in earlier:
            acc[...] += gram[...]
    if last:
        core_bit, me = place()
        size = own.shape[1]
        half = acc.shape[0] // 2
        for d in range(own.shape[0]):
            at = (me ^ d) * size
            own[d] = acc[pl.ds(pl.multiple_of(core_bit * half + at, 8), size)]
            send[d] = acc[pl.ds(pl.multiple_of((1 - core_bit) * half + at, 8), size)]


def place():
    row, col = lax.axis_index("row"), lax.axis_index("col")
    return col & 1, (row & 1) | (col & 2)


def gram_chunk(keep, core, across, earlier, last):
    width = keep.shape[2]
    rows = keep.shape[0] * keep.shape[1]
    number = gram_rows(width // BLOCK)[3]
    whole = jax.ShapeDtypeStruct((number, BLOCK), F32)
    pieces = jax.ShapeDtypeStruct((4, number // 8, BLOCK), F32)
    row_shape = jax.ShapeDtypeStruct((rows, width), F32)
    args = [keep, core, across] + (list(earlier) if last else [])
    outs = [row_shape] + ([pieces, pieces] if last else [whole])
    return pl.pallas_call(
        functools.partial(gram_kernel, last),
        out_shape=outs,
        in_specs=[VMEM] * len(args),
        out_specs=[VMEM] * len(outs),
        scratch_shapes=[pltpu.VMEM(whole.shape, F32)] if last else [],
        compiler_params=params(16 << 20),
    )(*args)


def swapped(x, row_flip, col_flip):
    rows, cols = lax.axis_size("row"), lax.axis_size("col")
    if not row_flip:
        return lax.ppermute(x, "col", [(c, c ^ col_flip) for c in range(cols)])
    if not col_flip:
        return lax.ppermute(x, "row", [(r, r ^ row_flip) for r in range(rows)])
    route = [
        (r * cols + c, (r ^ row_flip) * cols + (c ^ col_flip))
        for r in range(rows)
        for c in range(cols)
    ]
    return lax.ppermute(x, ("row", "col"), route)


FLIPS = ((1, 0), (0, 2), (1, 2))


def gram_sum(own, send):
    theirs = swapped(send, 0, 1)
    part = [own[d] + theirs[d] for d in range(4)]
    got = [swapped(x, *flip) for x, flip in zip(part[1:], FLIPS)]
    piece = (part[0] + got[0]) + (got[1] + got[2])
    bits = lax.axis_size("row").bit_length() - 1
    bit = 1
    while bit < bits:
        if bit + 1 < bits:
            a, b = 1 << bit, 2 << bit
            got = [swapped(piece, flip, 0) for flip in (a, b, a | b)]
            piece = (piece + got[0]) + (got[1] + got[2])
            bit += 2
        else:
            piece = piece + swapped(piece, 1 << bit, 0)
            bit += 1
    mine = [piece] + [swapped(piece, *flip) for flip in FLIPS]
    return mine, [swapped(x, 0, 1) for x in mine]


def against(left, right_rows):
    lh, ll = left
    rh, rl = right_rows
    return lax.dot_general(
        jnp.concatenate([lh, lh, ll], axis=1),
        jnp.concatenate([rh, rl, rh], axis=1),
        (((1,), (1,)), ((), ())),
        preferred_element_type=F32,
    )


def times(left, right):
    lh, ll = left
    rh, rl = right
    return jnp.dot(
        jnp.concatenate([lh, lh, ll], axis=1),
        jnp.concatenate([rh, rl, rh], axis=0),
        preferred_element_type=F32,
    )


def factor_kernel(chunks, scale, rounds, *refs):
    pieces, rows = refs[:8], refs[8 : 8 + chunks]
    basis_out, triangle_out, gram, flag = refs[8 + chunks : 12 + chunks]
    blocks, half_mask, half_eye, w, basis, triangle, out_sem = refs[12 + chunks : 19 + chunks]
    wb, gh, gl, yh, yl, ph, dh, dl = refs[19 + chunks :]
    size = gram.shape[0]
    order = size // BLOCK
    core_bit, me = place()
    half = blocks.shape[0] // 2
    for n, piece in enumerate(pieces):
        at = (core_bit ^ (n // 4)) * half + (me ^ (n % 4)) * piece.shape[0]
        blocks[pl.ds(pl.multiple_of(at, 8), piece.shape[0])] = piece[...]
    at = [slice(i * BLOCK, (i + 1) * BLOCK) for i in range(order)]

    r, c = square_index()
    row_scale, col_scale = [], []
    heads, pairs, _, _ = gram_rows(order)
    lower = {}
    for i, j, head, line in pairs:
        packed = blocks[pl.ds(head, BLOCK)]
        turned = packed.T
        lower[i, i] = jnp.where(r >= c, packed, turned)
        lower[j, j] = jnp.where(
            r < c, packed, jnp.where(r == c, blocks[pl.ds(line, 1)], turned)
        )
    for i in range(order):
        diagonal = jnp.where(r == c, lower[i, i], 0.0)
        row_scale.append(lax.rsqrt(jnp.sum(diagonal, axis=1, keepdims=True)))
        col_scale.append(lax.rsqrt(jnp.sum(diagonal, axis=0, keepdims=True)))
    for i, j in [(i, j) for i in range(order) for j in range(i + 1)]:
        block = lower[i, i] if i == j else blocks[pl.ds(heads[i, j], BLOCK)]
        first = -(block * row_scale[i] * col_scale[j])
        if i == j:
            first = jnp.where(r > c, first, jnp.where(r == c, 1.0, 0.0))
        wb[at[i], at[j]] = (first * col_scale[j]).astype(BF16)
        for p, q, x in [(i, j, block)] + ([(j, i, block.T)] if i != j else []):
            gram[at[p], at[q]] = x
            gh[at[p], at[q]], gl[at[p], at[q]] = halves(x)
        if i != j:
            wb[at[j], at[i]] = jnp.zeros((BLOCK, BLOCK), BF16)

    wide = size // 2
    top, low = slice(0, wide), slice(wide, size)
    r = lax.broadcasted_iota(jnp.int32, (wide, wide), 0)
    c = lax.broadcasted_iota(jnp.int32, (wide, wide), 1)
    half_mask[...] = jnp.where(r > c, 1.0, jnp.where(r == c, 0.5, 0.0))
    half_eye[...] = jnp.where(r == c, 0.5, 0.0)
    for ref in (ph, dh, dl):
        ref[top, low] = jnp.zeros((wide, wide), BF16)

    def dot(left, right):
        return jnp.dot(left, right, preferred_element_type=F32)

    def dot_rows(left, right):
        return lax.dot_general(left, right, (((1,), (1,)), ((), ())), preferred_element_type=F32)

    def twice(x, axis=1):
        return jnp.concatenate([x, x], axis=axis)

    def both(x, y, axis=1):
        return jnp.concatenate([x, y], axis=axis)

    def step(exact):
        for cols, k in ((top, wide), (low, size)):
            y = dot_rows(both(gh[:, :k], gl[:, :k]), twice(wb[cols, :k]))
            if exact:
                yh[:, cols], yl[:, cols] = halves(y)
            else:
                yh[:, cols] = y.astype(BF16)
        norm = jnp.zeros((1, 1), F32)
        strips = []
        for part, k in ((top, wide), (low, size)):
            if exact:
                m = dot(twice(wb[part, :k]), both(yh[:k, :k], yl[:k, :k], 0))
            else:
                m = dot(wb[part, :k], yh[:k, :k])
            corner = m[:, k - wide :] * half_mask[...] - half_eye[...]
            p = corner if k == wide else both(m[:, :wide], corner)
            ph[part, :k] = p.astype(BF16)
            strips.append(p)
            if exact:
                norm = norm + jnp.sum(p * p, keepdims=True)
        for p, part, k in zip(strips, (top, low), (wide, size)):
            square = dot(ph[part, :k], ph[:k, :k])
            cross = dot_rows(ph[part, :k], ph[:k, :k])
            corner = cross[:, k - wide :] * half_mask[...]
            cross = corner if k == wide else both(cross[:, :wide], corner)
            d = p - square - cross
            if exact:
                dh[part, :k], dl[part, :k] = halves(d)
            else:
                dh[part, :k] = d.astype(BF16)
        for part, k in ((top, wide), (low, size)):
            if exact:
                change = dot(both(dh[part, :k], dl[part, :k]), twice(wb[:k, :k], 0))
            else:
                change = dot(dh[part, :k], wb[:k, :k])
            w[part, :k] = wb[part, :k].astype(F32) - change
        return jnp.sum(norm)

    def rounded():
        for part, k in ((top, wide), (low, size)):
            wb[part, :k] = w[part, :k].astype(BF16)

    step(False)

    def not_done(state):
        count, norm = state
        return jnp.logical_and(count < rounds, jnp.logical_not(norm < SMALL))

    def again(state):
        rounded()
        return state[0] + 1, step(True)

    _, norm = lax.while_loop(not_done, again, (jnp.int32(0), jnp.float32(1.0)))
    flag[0] = jnp.where(norm < SMALL, 1, 0).astype(jnp.int32)
    for part, k in ((top, wide), (low, size)):
        wb[part, :k], dl[part, :k] = halves(w[part, :k])
    for part, k in ((top, wide), (low, size)):
        upper = times((wb[part, :k], dl[part, :k]), (gh[:k, k - wide :], gl[:k, k - wide :]))
        corner = jnp.where(r <= c, upper[:, :wide], 0.0)
        upper = both(corner, upper[:, wide:]) if k == wide else corner
        triangle[part, k - wide :] = upper * (1.0 / scale)
    triangle[low, top] = jnp.zeros((wide, wide), F32)
    copies = [pltpu.make_async_copy(triangle, triangle_out, out_sem.at[0])]
    copies[0].start()
    first = 0
    for part in rows:
        for head in range(0, part.shape[0], wide):
            count = min(wide, part.shape[0] - head)
            sh, sl = halves(part[head : head + count])
            here = pl.ds(first, count)
            for cols, k in ((top, wide), (low, size)):
                out = against((sh[:, :k], sl[:, :k]), (wb[cols, :k], dl[cols, :k]))
                basis[here, cols] = out * scale
            sem = out_sem.at[len(copies)]
            copies.append(pltpu.make_async_copy(basis.at[here], basis_out.at[here], sem))
            copies[-1].start()
            first += count
    for copy in copies:
        copy.wait()


def factor(pieces, rows, scale):
    width = rows[0].shape[1]
    square = (width, width)
    local = sum(part.shape[0] for part in rows)
    number = gram_rows(width // BLOCK)[3]
    return pl.pallas_call(
        functools.partial(factor_kernel, len(rows), scale, 12),
        out_shape=[
            pltpu.HBM((local, width), F32),
            pltpu.HBM(square, F32),
            jax.ShapeDtypeStruct(square, F32),
            jax.ShapeDtypeStruct((1,), jnp.int32),
        ],
        in_specs=[VMEM] * (8 + len(rows)),
        out_specs=[HBM, HBM, VMEM, SMEM],
        scratch_shapes=[
            pltpu.VMEM((number, BLOCK), F32),
            pltpu.VMEM((width // 2, width // 2), F32),
            pltpu.VMEM((width // 2, width // 2), F32),
            pltpu.VMEM(square, F32),
            pltpu.VMEM((local, width), F32),
            pltpu.VMEM(square, F32),
            pltpu.SemaphoreType.DMA((1 + sum(-(-part.shape[0] * 2 // width) for part in rows),)),
        ]
        + [pltpu.VMEM(square, BF16)] * 8,
        compiler_params=params(24 << 20),
    )(*pieces, *rows)


def direct(gram, rows, scale):
    lower = jnp.linalg.cholesky(gram)
    own_rows = jnp.concatenate(rows, axis=0)
    basis = jax.scipy.linalg.solve_triangular(lower, own_rows.T, lower=True).T * scale
    return basis, lower.T / scale


def body(tile_values, tile_places, tile_counts, sketch):
    tiles = tile_values[0, 0]
    size = tiles.shape[1]
    width = sketch.shape[1]
    row_devices = lax.axis_size("row")
    col_devices = lax.axis_size("col")
    local_rows = sketch.shape[0] // row_devices
    tile_rows = local_rows * col_devices // size
    panels = sketch.reshape(-1, size, width)
    places = tile_places[0, 0]
    scale = math.sqrt(local_rows * row_devices * col_devices)
    per_owner = tile_rows // col_devices
    cuts = sorted({0, per_owner // 6, per_owner * 5 // 6, per_owner})
    chunks = list(zip(cuts, cuts[1:]))
    early = chunks[:-1] or chunks
    late = chunks[len(early) :]

    def products(spans):
        out = tile_products(tile_counts, places, tiles, panels, tile_rows, tuple(spans))
        return out[: len(spans)], out[len(spans) :]

    def across_cores(send, keep):
        own = []
        for n in range(len(send)):
            if n == 1:
                *send[1:], core = lax.optimization_barrier((*send[1:], core))
            core = swapped(send[n], 0, 1)
            own.append(keep[n] + core)
        return own

    send, keep = products([(1, head, end) for head, end in early])
    own = across_cores(list(send), keep)
    across = [swapped(x, 0, 2) for x in own]
    places, own = lax.optimization_barrier((places, own))
    send, keep = products([(1, *chunk) for chunk in late] + [(0, *chunk) for chunk in chunks])
    send, keep, across[0] = lax.optimization_barrier((send, keep, across[0]))
    across += [swapped(x, 0, 2) for x in across_cores(send[: len(late)], keep[: len(late)])]
    send, keep = send[len(late) :], keep[len(late) :]
    chunks = len(chunks)
    rows, grams = [], []
    for n in range(chunks):
        out = gram_chunk(keep[n], swapped(send[n], 0, 1), across[n], grams, n == chunks - 1)
        rows.append(out[0])
        grams.append(out[1])
    mine, theirs = gram_sum(*out[1:])
    basis, triangle, gram, flag = factor(mine + theirs, rows, scale)
    return lax.switch(
        flag[0],
        (lambda: direct(gram, rows, scale), lambda: (basis, triangle)),
    )


def solution(mesh):
    in_specs = (
        P("row", "col", None, None, None),
        P("row", "col", None, None),
        P("row", "col"),
        P("col", None),
    )
    out_specs = (P(("row", "col"), None), P())
    return jax.shard_map(body, mesh=mesh, in_specs=in_specs, out_specs=out_specs, check_vma=False)
```

```python
import functools
import math

import jax
import jax.numpy as jnp
from jax import lax
from jax.experimental import pallas as pl
from jax.experimental.pallas import tpu as pltpu
from jax.sharding import PartitionSpec as P

BF16 = jnp.bfloat16
F32 = jnp.float32
PAIR = 2
TURN = 16
PARTS = 2
BLOCK = 128
SMALL = 0.01
SMEM = pl.BlockSpec(memory_space=pltpu.SMEM)
VMEM = pl.BlockSpec(memory_space=pltpu.VMEM)
HBM = pl.BlockSpec(memory_space=pltpu.HBM)

def in_hbm(x):
    return pltpu.with_memory_space_constraint(x, pltpu.HBM)


def params(size):
    return pltpu.CompilerParams(vmem_limit_bytes=size)


def halves(x):
    high = x.astype(BF16)
    return high, (x - high.astype(F32)).astype(BF16)


def tile_kernel(resident, spans, stride, counts, places, tiles, panels, *refs):
    outs, refs = refs[: 2 * len(spans)], refs[2 * len(spans) :]
    tile_buf, panel_buf, place_of, key, first_of, key_of, acc, load_sem, panel_sem = refs[:9]
    fill, entry = refs[9 : 9 + PARTS], refs[9 + PARTS :]
    slots = tiles.shape[0]
    blocks = acc.shape[0]
    per_owner = key.shape[0] // lax.axis_size("col")
    panel_loads = [pltpu.make_async_copy(panels, panel_buf, panel_sem.at[0])] if resident else []
    cuts = [-(-slots * n // PARTS) for n in range(PARTS + 1)]
    tile_loads = [
        pltpu.make_async_copy(
            tiles.at[pl.ds(a, b - a)], tile_buf.at[pl.ds(a, b - a)], load_sem.at[1 + n]
        )
        for n, (a, b) in enumerate(zip(cuts, cuts[1:]))
    ]
    place_load = pltpu.make_async_copy(places, place_of, load_sem.at[0])
    for load in [place_load] + panel_loads + tile_loads:
        load.start()
    own = lax.axis_index("col")

    heads = {}
    for n, (flip, head, end) in enumerate(spans):
        for inside in range(head, end):
            heads[flip, inside] = sum(e - h for _, h, e in spans[:n]) + inside - head
    for owner in range(key.shape[0] // per_owner):
        base = jnp.where((owner & 1) == (own & 1), blocks // 2, 0)
        flipped = (owner >> 1) != (own >> 1)
        for inside in range(per_owner):
            name = [base + heads[f, inside] if (f, inside) in heads else blocks for f in (0, 1)]
            key[owner * per_owner + inside] = jnp.where(flipped, name[1], name[0])
    for n in range(PARTS):
        for k in range(blocks + 1):
            fill[n][k] = k * stride
    place_load.wait()
    live = counts[0, 0]
    shift = panels.shape[0].bit_length()
    unroll = math.gcd(cuts[1], 6)

    def put(g, carry):
        for i in range(unroll):
            mine = [jnp.minimum(cut + g * unroll + i, slots - 1) for cut in cuts[:-1]]
            names = [key[place_of[0, t]] for t in mine]
            made = [(t << shift) | place_of[1, t] for t in mine]
            lists = [
                jnp.where(cut + g * unroll + i < live, name, blocks)
                for cut, name in zip(cuts, names)
            ]
            spots = [fill[n][k] for n, k in enumerate(lists)]
            for n in range(PARTS):
                fill[n][lists[n]] = spots[n] + 1
                entry[n][spots[n]] = made[n]
        return carry

    lax.fori_loop(0, (jnp.minimum(live, cuts[1]) + unroll - 1) // unroll, put, 0)

    empty = blocks * stride + cuts[1]
    number, bounds = 0, [0]
    for n in range(PARTS):
        for i in range(PAIR):
            entry[n][empty + i] = slots << shift
        for k in range(blocks):
            size = fill[n][k] - k * stride
            for i in range(PAIR - 1):
                entry[n][fill[n][k] + i] = slots << shift

            def add_pair(j, at, k=k):
                first_of[at + j] = k * stride + j * PAIR
                key_of[at + j] = k
                return at

            pairs = (size + PAIR - 1) // PAIR
            lax.fori_loop(0, pairs, add_pair, number)
            number += pairs
        for i in range(TURN - 1):
            first_of[number + i] = empty
            key_of[number + i] = 0
        number = (number + TURN - 1) // TURN * TURN
        bounds.append(number // TURN)
    acc[...] = jnp.zeros_like(acc)
    tile_buf[slots] = jnp.zeros_like(tile_buf[slots])
    for load in panel_loads:
        load.wait()

    def turn(n, g, carry):
        firsts = [first_of[g * TURN + i] for i in range(TURN)]
        entries = [[entry[n][at + j] for j in range(PAIR)] for at in firsts]
        slot = [[e >> shift for e in pair] for pair in entries]
        column = [[e & ((1 << shift) - 1) for e in pair] for pair in entries]
        if not resident:
            copies = [
                pltpu.make_async_copy(
                    panels.at[column[i][j]],
                    panel_buf.at[i * PAIR + j],
                    panel_sem.at[i * PAIR + j],
                )
                for i in range(TURN)
                for j in range(PAIR)
            ]
            for copy in copies:
                copy.start()
            for copy in copies:
                copy.wait()
        for i in range(TURN):
            left = jnp.concatenate([tile_buf[slot[i][j]] for j in range(PAIR)], axis=1)
            right = jnp.concatenate(
                [panel_buf[column[i][j] if resident else i * PAIR + j] for j in range(PAIR)],
                axis=0,
            )
            acc[key_of[g * TURN + i]] += jnp.dot(left, right, preferred_element_type=F32)
        return carry

    for n, load in enumerate(tile_loads):
        load.wait()
        lax.fori_loop(bounds[n], bounds[n + 1], functools.partial(turn, n), 0)
    first = 0
    for out in outs:
        out[...] = acc[first : first + out.shape[0]]
        first += out.shape[0]


def tile_products(counts, places, tiles, panels, tile_rows, spans):
    slots, size, _ = tiles.shape
    width = panels.shape[2]
    sizes = [end - head for _, head, end in spans] * 2
    blocks = sum(sizes)
    part = -(-slots // PARTS)
    stride = (min(part, panels.shape[0]) // PAIR + 1) * PAIR
    pairs = PARTS * blocks * stride // PAIR + TURN * (PARTS + 1)
    resident = panels.size * 2 <= 16 << 20
    panel_shape = (panels.shape[0] if resident else PAIR * TURN, size, width)
    return pl.pallas_call(
        functools.partial(tile_kernel, resident, spans, stride),
        out_shape=[jax.ShapeDtypeStruct((n, size, width), F32) for n in sizes],
        in_specs=[SMEM, HBM, HBM, HBM],
        out_specs=[VMEM] * len(sizes),
        scratch_shapes=[
            pltpu.VMEM((slots + 1, size, size), BF16),
            pltpu.VMEM(panel_shape, BF16),
            pltpu.SMEM((2, slots), jnp.int32),
            pltpu.SMEM((tile_rows,), jnp.int32),
            pltpu.SMEM((pairs,), jnp.int32),
            pltpu.SMEM((pairs,), jnp.int32),
            pltpu.VMEM((blocks, size, width), F32),
            pltpu.SemaphoreType.DMA((1 + PARTS,)),
            pltpu.SemaphoreType.DMA((1 if resident else PAIR * TURN,)),
        ]
        + [pltpu.SMEM((blocks + 1,), jnp.int32)] * PARTS
        + [pltpu.SMEM((blocks * stride + part + PAIR,), jnp.int32)] * PARTS,
        compiler_params=params(50 << 20),
    )(counts, in_hbm(places), tiles, panels)


def gram_rows(order):
    under = [(i, j) for i in range(order) for j in range(i)]
    heads = {block: n * BLOCK for n, block in enumerate(under)}
    first = len(under) * BLOCK
    pairs = []
    for i in range(0, order, 2):
        pairs.append((i, i + 1, first, 0))
        first += BLOCK
    pairs = [(i, j, head, first + n) for n, (i, j, head, _) in enumerate(pairs)]
    return heads, pairs, first, -(-(first + len(pairs)) // 64) * 64


def square_index():
    return (
        lax.broadcasted_iota(jnp.int32, (BLOCK, BLOCK), 0),
        lax.broadcasted_iota(jnp.int32, (BLOCK, BLOCK), 1),
    )


def gram_kernel(last, *refs):
    if last:
        keep, core, across, *earlier, rows, own, send, acc = refs
    else:
        keep, core, across, rows, acc = refs
    total = (keep[...] + core[...]) + across[...]
    total = total.reshape(rows.shape)
    rows[...] = total
    high, low = halves(total)
    left = jnp.concatenate([high, high, low], axis=0)
    right = jnp.concatenate([high, low, high], axis=0)
    order = rows.shape[1] // BLOCK
    heads, pairs, slab, number = gram_rows(order)
    diagonal = {}
    for i in range(order):
        strip = lax.dot_general(
            left[:, i * BLOCK : (i + 1) * BLOCK],
            right[:, : (i + 1) * BLOCK],
            (((0,), (0,)), ((), ())),
            preferred_element_type=F32,
        )
        for j in range(i):
            acc[pl.ds(heads[i, j], BLOCK)] = strip[:, j * BLOCK : (j + 1) * BLOCK]
        diagonal[i] = strip[:, i * BLOCK :]
    acc[pl.ds(slab, number - slab)] = jnp.zeros((number - slab, BLOCK), F32)
    r, c = square_index()
    for i, j, head, line in pairs:
        acc[pl.ds(head, BLOCK)] = jnp.where(r >= c, diagonal[i], diagonal[j])
        acc[pl.ds(line, 1)] = jnp.sum(jnp.where(r == c, diagonal[j], 0.0), axis=0, keepdims=True)
    if last:
        for gram in earlier:
            acc[...] += gram[...]
    if last:
        core_bit, me, partner = place()
        size = own.shape[1]
        half = acc.shape[0] // 2
        for d in range(own.shape[0]):
            at = core_bit * half + (me ^ d) * size
            own[d] = acc[pl.ds(pl.multiple_of(at, 8), size)]
            at = (1 - core_bit) * half + (partner ^ d) * size
            send[d] = acc[pl.ds(pl.multiple_of(at, 8), size)]


def place():
    row, col = lax.axis_index("row"), lax.axis_index("col")
    core_bit = col & 1
    near, far = (row & 1) | (col & 2), (row >> 1) & 3
    if lax.axis_size("row") < 8:
        return core_bit, near, near
    return core_bit, jnp.where(core_bit == 0, far, near), jnp.where(core_bit == 0, near, far)


def gram_chunk(keep, core, across, earlier, last):
    width = keep.shape[2]
    rows = keep.shape[0] * keep.shape[1]
    number = gram_rows(width // BLOCK)[3]
    whole = jax.ShapeDtypeStruct((number, BLOCK), F32)
    pieces = jax.ShapeDtypeStruct((4, number // 8, BLOCK), F32)
    row_shape = jax.ShapeDtypeStruct((rows, width), F32)
    args = [keep, core, across] + (list(earlier) if last else [])
    outs = [row_shape] + ([pieces, pieces] if last else [whole])
    return pl.pallas_call(
        functools.partial(gram_kernel, last),
        out_shape=outs,
        in_specs=[VMEM] * len(args),
        out_specs=[VMEM] * len(outs),
        scratch_shapes=[pltpu.VMEM(whole.shape, F32)] if last else [],
        compiler_params=params(16 << 20),
    )(*args)


def routed(x, flips):
    rows, cols = lax.axis_size("row"), lax.axis_size("col")
    if flips[0] == flips[1] and not flips[0][0]:
        return lax.ppermute(x, "col", [(c, c ^ flips[0][1]) for c in range(cols)])
    route = []
    for r in range(rows):
        for c in range(cols):
            row_flip, col_flip = flips[c & 1]
            route.append((r * cols + c, (r ^ row_flip) * cols + (c ^ col_flip)))
    return lax.ppermute(x, ("row", "col"), route)


def swapped(x, row_flip, col_flip):
    return routed(x, ((row_flip, col_flip),) * 2)


NEAR = ((1, 0), (0, 2), (1, 2))
FAR = ((2, 0), (4, 0), (6, 0))


def gram_sum(own, send):
    theirs = swapped(send, 0, 1)
    bits = lax.axis_size("row").bit_length() - 1
    if bits >= 3:
        shared, added, rest = list(zip(FAR, NEAR)), [list(zip(NEAR, FAR))], range(3, bits)
    else:
        shared, added, rest = list(zip(NEAR, NEAR)), [], range(1, bits)
    added += [[((1 << bit, 0),) * 2] for bit in rest]
    part = [own[d] + theirs[d] for d in range(4)]
    got = [routed(x, flips) for x, flips in zip(part[1:], shared)]
    piece = (part[0] + got[0]) + (got[1] + got[2])
    for stage in added:
        got = [routed(piece, flips) for flips in stage]
        piece = piece + got[0] if len(got) == 1 else (piece + got[0]) + (got[1] + got[2])
    mine = [piece] + [routed(piece, flips) for flips in shared]
    return mine, [swapped(x, 0, 1) for x in mine]


def against(left, right_rows):
    lh, ll = left
    rh, rl = right_rows
    return lax.dot_general(
        jnp.concatenate([lh, lh, ll], axis=1),
        jnp.concatenate([rh, rl, rh], axis=1),
        (((1,), (1,)), ((), ())),
        preferred_element_type=F32,
    )


def times(left, right):
    lh, ll = left
    rh, rl = right
    return jnp.dot(
        jnp.concatenate([lh, lh, ll], axis=1),
        jnp.concatenate([rh, rl, rh], axis=0),
        preferred_element_type=F32,
    )


def factor_kernel(chunks, scale, rounds, *refs):
    pieces, rows = refs[:8], refs[8 : 8 + chunks]
    basis_out, triangle_out, gram, flag = refs[8 + chunks : 12 + chunks]
    blocks, half_mask, half_eye, w, basis, triangle, out_sem = refs[12 + chunks : 19 + chunks]
    wb, gh, gl, yh, yl, ph, dh, dl = refs[19 + chunks :]
    size = gram.shape[0]
    order = size // BLOCK
    core_bit, me, partner = place()
    half = blocks.shape[0] // 2
    for n, piece in enumerate(pieces):
        first, number = (core_bit, me) if n < 4 else (1 - core_bit, partner)
        at = first * half + (number ^ (n % 4)) * piece.shape[0]
        blocks[pl.ds(pl.multiple_of(at, 8), piece.shape[0])] = piece[...]
    at = [slice(i * BLOCK, (i + 1) * BLOCK) for i in range(order)]

    r, c = square_index()
    row_scale, col_scale = [], []
    heads, pairs, _, _ = gram_rows(order)
    lower = {}
    for i, j, head, line in pairs:
        packed = blocks[pl.ds(head, BLOCK)]
        turned = packed.T
        lower[i, i] = jnp.where(r >= c, packed, turned)
        lower[j, j] = jnp.where(
            r < c, packed, jnp.where(r == c, blocks[pl.ds(line, 1)], turned)
        )
    for i in range(order):
        diagonal = jnp.where(r == c, lower[i, i], 0.0)
        row_scale.append(lax.rsqrt(jnp.sum(diagonal, axis=1, keepdims=True)))
        col_scale.append(lax.rsqrt(jnp.sum(diagonal, axis=0, keepdims=True)))
    for i, j in [(i, j) for i in range(order) for j in range(i + 1)]:
        block = lower[i, i] if i == j else blocks[pl.ds(heads[i, j], BLOCK)]
        first = -(block * row_scale[i] * col_scale[j])
        if i == j:
            first = jnp.where(r > c, first, jnp.where(r == c, 1.0, 0.0))
        wb[at[i], at[j]] = (first * col_scale[j]).astype(BF16)
        for p, q, x in [(i, j, block)] + ([(j, i, block.T)] if i != j else []):
            gram[at[p], at[q]] = x
            gh[at[p], at[q]], gl[at[p], at[q]] = halves(x)
        if i != j:
            wb[at[j], at[i]] = jnp.zeros((BLOCK, BLOCK), BF16)

    wide = size // 2
    top, low = slice(0, wide), slice(wide, size)
    r = lax.broadcasted_iota(jnp.int32, (wide, wide), 0)
    c = lax.broadcasted_iota(jnp.int32, (wide, wide), 1)
    half_mask[...] = jnp.where(r > c, 1.0, jnp.where(r == c, 0.5, 0.0))
    half_eye[...] = jnp.where(r == c, 0.5, 0.0)
    for ref in (ph, dh, dl):
        ref[top, low] = jnp.zeros((wide, wide), BF16)

    def dot(left, right):
        return jnp.dot(left, right, preferred_element_type=F32)

    def dot_rows(left, right):
        return lax.dot_general(left, right, (((1,), (1,)), ((), ())), preferred_element_type=F32)

    def twice(x, axis=1):
        return jnp.concatenate([x, x], axis=axis)

    def both(x, y, axis=1):
        return jnp.concatenate([x, y], axis=axis)

    def step(exact):
        for cols, k in ((top, wide), (low, size)):
            y = dot_rows(both(gh[:, :k], gl[:, :k]), twice(wb[cols, :k]))
            if exact:
                yh[:, cols], yl[:, cols] = halves(y)
            else:
                yh[:, cols] = y.astype(BF16)
        norm = jnp.zeros((1, 1), F32)
        strips = []
        for part, k in ((top, wide), (low, size)):
            if exact:
                m = dot(twice(wb[part, :k]), both(yh[:k, :k], yl[:k, :k], 0))
            else:
                m = dot(wb[part, :k], yh[:k, :k])
            corner = m[:, k - wide :] * half_mask[...] - half_eye[...]
            p = corner if k == wide else both(m[:, :wide], corner)
            ph[part, :k] = p.astype(BF16)
            strips.append(p)
            if exact:
                norm = norm + jnp.sum(p * p, keepdims=True)
        for p, part, k in zip(strips, (top, low), (wide, size)):
            square = dot(ph[part, :k], ph[:k, :k])
            cross = dot_rows(ph[part, :k], ph[:k, :k])
            corner = cross[:, k - wide :] * half_mask[...]
            cross = corner if k == wide else both(cross[:, :wide], corner)
            d = p - square - cross
            if exact:
                dh[part, :k], dl[part, :k] = halves(d)
            else:
                dh[part, :k] = d.astype(BF16)
        for part, k in ((top, wide), (low, size)):
            if exact:
                change = dot(both(dh[part, :k], dl[part, :k]), twice(wb[:k, :k], 0))
            else:
                change = dot(dh[part, :k], wb[:k, :k])
            w[part, :k] = wb[part, :k].astype(F32) - change
        return jnp.sum(norm)

    def rounded():
        for part, k in ((top, wide), (low, size)):
            wb[part, :k] = w[part, :k].astype(BF16)

    step(False)

    def not_done(state):
        count, norm = state
        return jnp.logical_and(count < rounds, jnp.logical_not(norm < SMALL))

    def again(state):
        rounded()
        return state[0] + 1, step(True)

    _, norm = lax.while_loop(not_done, again, (jnp.int32(0), jnp.float32(1.0)))
    flag[0] = jnp.where(norm < SMALL, 1, 0).astype(jnp.int32)
    for part, k in ((top, wide), (low, size)):
        wb[part, :k], dl[part, :k] = halves(w[part, :k])
    for part, k in ((top, wide), (low, size)):
        upper = times((wb[part, :k], dl[part, :k]), (gh[:k, k - wide :], gl[:k, k - wide :]))
        corner = jnp.where(r <= c, upper[:, :wide], 0.0)
        upper = both(corner, upper[:, wide:]) if k == wide else corner
        triangle[part, k - wide :] = upper * (1.0 / scale)
    triangle[low, top] = jnp.zeros((wide, wide), F32)
    copies = [pltpu.make_async_copy(triangle, triangle_out, out_sem.at[0])]
    copies[0].start()
    first = 0
    for part in rows:
        for head in range(0, part.shape[0], wide):
            count = min(wide, part.shape[0] - head)
            sh, sl = halves(part[head : head + count])
            here = pl.ds(first, count)
            for cols, k in ((top, wide), (low, size)):
                out = against((sh[:, :k], sl[:, :k]), (wb[cols, :k], dl[cols, :k]))
                basis[here, cols] = out * scale
            sem = out_sem.at[len(copies)]
            copies.append(pltpu.make_async_copy(basis.at[here], basis_out.at[here], sem))
            copies[-1].start()
            first += count
    for copy in copies:
        copy.wait()


def factor(pieces, rows, scale):
    width = rows[0].shape[1]
    square = (width, width)
    local = sum(part.shape[0] for part in rows)
    number = gram_rows(width // BLOCK)[3]
    return pl.pallas_call(
        functools.partial(factor_kernel, len(rows), scale, 12),
        out_shape=[
            pltpu.HBM((local, width), F32),
            pltpu.HBM(square, F32),
            jax.ShapeDtypeStruct(square, F32),
            jax.ShapeDtypeStruct((1,), jnp.int32),
        ],
        in_specs=[VMEM] * (8 + len(rows)),
        out_specs=[HBM, HBM, VMEM, SMEM],
        scratch_shapes=[
            pltpu.VMEM((number, BLOCK), F32),
            pltpu.VMEM((width // 2, width // 2), F32),
            pltpu.VMEM((width // 2, width // 2), F32),
            pltpu.VMEM(square, F32),
            pltpu.VMEM((local, width), F32),
            pltpu.VMEM(square, F32),
            pltpu.SemaphoreType.DMA((1 + sum(-(-part.shape[0] * 2 // width) for part in rows),)),
        ]
        + [pltpu.VMEM(square, BF16)] * 8,
        compiler_params=params(24 << 20),
    )(*pieces, *rows)


def direct(gram, rows, scale):
    lower = jnp.linalg.cholesky(gram)
    own_rows = jnp.concatenate(rows, axis=0)
    basis = jax.scipy.linalg.solve_triangular(lower, own_rows.T, lower=True).T * scale
    return basis, lower.T / scale


def body(tile_values, tile_places, tile_counts, sketch):
    tiles = tile_values[0, 0]
    size = tiles.shape[1]
    width = sketch.shape[1]
    row_devices = lax.axis_size("row")
    col_devices = lax.axis_size("col")
    local_rows = sketch.shape[0] // row_devices
    tile_rows = local_rows * col_devices // size
    panels = sketch.reshape(-1, size, width)
    places = tile_places[0, 0]
    scale = math.sqrt(local_rows * row_devices * col_devices)
    per_owner = tile_rows // col_devices
    cuts = sorted({0, per_owner // 6, per_owner * 5 // 6, per_owner})
    chunks = list(zip(cuts, cuts[1:]))
    early = chunks[:-1] or chunks
    late = chunks[len(early) :]

    def products(spans):
        out = tile_products(tile_counts, places, tiles, panels, tile_rows, tuple(spans))
        return out[: len(spans)], out[len(spans) :]

    def across_cores(send, keep):
        own = []
        for n in range(len(send)):
            if n == 1:
                *send[1:], core = lax.optimization_barrier((*send[1:], core))
            core = swapped(send[n], 0, 1)
            own.append(keep[n] + core)
        return own

    send, keep = products([(1, head, end) for head, end in early])
    own = across_cores(list(send), keep)
    across = [swapped(x, 0, 2) for x in own]
    places, own = lax.optimization_barrier((places, own))
    send, keep = products([(1, *chunk) for chunk in late] + [(0, *chunk) for chunk in chunks])
    send, keep, across[0] = lax.optimization_barrier((send, keep, across[0]))
    across += [swapped(x, 0, 2) for x in across_cores(send[: len(late)], keep[: len(late)])]
    send, keep = send[len(late) :], keep[len(late) :]
    chunks = len(chunks)
    rows, grams = [], []
    for n in range(chunks):
        out = gram_chunk(keep[n], swapped(send[n], 0, 1), across[n], grams, n == chunks - 1)
        rows.append(out[0])
        grams.append(out[1])
    mine, theirs = gram_sum(*out[1:])
    basis, triangle, gram, flag = factor(mine + theirs, rows, scale)
    return lax.switch(
        flag[0],
        (lambda: direct(gram, rows, scale), lambda: (basis, triangle)),
    )


def solution(mesh):
    in_specs = (
        P("row", "col", None, None, None),
        P("row", "col", None, None),
        P("row", "col"),
        P("col", None),
    )
    out_specs = (P(("row", "col"), None), P())
    return jax.shard_map(body, mesh=mesh, in_specs=in_specs, out_specs=out_specs, check_vma=False)
```

```python
import functools
import math

import jax
import jax.numpy as jnp
from jax import lax
from jax.experimental import pallas as pl
from jax.experimental.pallas import tpu as pltpu
from jax.sharding import PartitionSpec as P

BF16 = jnp.bfloat16
F32 = jnp.float32
PAIR = 2
TURN = 16
PARTS = 2
BLOCK = 128
SMALL = 0.01
SMEM = pl.BlockSpec(memory_space=pltpu.SMEM)
VMEM = pl.BlockSpec(memory_space=pltpu.VMEM)
HBM = pl.BlockSpec(memory_space=pltpu.HBM)

def in_hbm(x):
    return pltpu.with_memory_space_constraint(x, pltpu.HBM)


def params(size):
    return pltpu.CompilerParams(vmem_limit_bytes=size)


def halves(x):
    high = x.astype(BF16)
    return high, (x - high.astype(F32)).astype(BF16)


def tile_kernel(resident, spans, stride, counts, places, tiles, panels, *refs):
    outs, refs = refs[: 2 * len(spans)], refs[2 * len(spans) :]
    tile_buf, panel_buf, place_of, key, first_of, key_of, acc, load_sem, panel_sem = refs[:9]
    fill, entry = refs[9 : 9 + PARTS], refs[9 + PARTS :]
    slots = tiles.shape[0]
    blocks = acc.shape[0]
    per_owner = key.shape[0] // lax.axis_size("col")
    panel_loads = [pltpu.make_async_copy(panels, panel_buf, panel_sem.at[0])] if resident else []
    cuts = [-(-slots * n // PARTS) for n in range(PARTS + 1)]
    tile_loads = [
        pltpu.make_async_copy(
            tiles.at[pl.ds(a, b - a)], tile_buf.at[pl.ds(a, b - a)], load_sem.at[1 + n]
        )
        for n, (a, b) in enumerate(zip(cuts, cuts[1:]))
    ]
    place_load = pltpu.make_async_copy(places, place_of, load_sem.at[0])
    for load in [place_load] + panel_loads + tile_loads:
        load.start()
    own = lax.axis_index("col")

    heads = {}
    for n, (flip, head, end) in enumerate(spans):
        for inside in range(head, end):
            heads[flip, inside] = sum(e - h for _, h, e in spans[:n]) + inside - head
    for owner in range(key.shape[0] // per_owner):
        base = jnp.where((owner & 1) == (own & 1), blocks // 2, 0)
        flipped = (owner >> 1) != (own >> 1)
        for inside in range(per_owner):
            name = [base + heads[f, inside] if (f, inside) in heads else blocks for f in (0, 1)]
            key[owner * per_owner + inside] = jnp.where(flipped, name[1], name[0])
    for n in range(PARTS):
        for k in range(blocks + 1):
            fill[n][k] = k * stride
    place_load.wait()
    live = counts[0, 0]
    shift = panels.shape[0].bit_length()
    unroll = math.gcd(cuts[1], 6)

    def put(g, carry):
        for i in range(unroll):
            mine = [jnp.minimum(cut + g * unroll + i, slots - 1) for cut in cuts[:-1]]
            names = [key[place_of[0, t]] for t in mine]
            made = [(t << shift) | place_of[1, t] for t in mine]
            lists = [
                jnp.where(cut + g * unroll + i < live, name, blocks)
                for cut, name in zip(cuts, names)
            ]
            spots = [fill[n][k] for n, k in enumerate(lists)]
            for n in range(PARTS):
                fill[n][lists[n]] = spots[n] + 1
                entry[n][spots[n]] = made[n]
        return carry

    lax.fori_loop(0, (jnp.minimum(live, cuts[1]) + unroll - 1) // unroll, put, 0)

    empty = blocks * stride + cuts[1]
    number, bounds = 0, [0]
    for n in range(PARTS):
        for i in range(PAIR):
            entry[n][empty + i] = slots << shift
        for k in range(blocks):
            size = fill[n][k] - k * stride
            for i in range(PAIR - 1):
                entry[n][fill[n][k] + i] = slots << shift

            def add_pair(j, at, k=k):
                first_of[at + j] = k * stride + j * PAIR
                key_of[at + j] = k
                return at

            pairs = (size + PAIR - 1) // PAIR
            lax.fori_loop(0, pairs, add_pair, number)
            number += pairs
        for i in range(TURN - 1):
            first_of[number + i] = empty
            key_of[number + i] = 0
        number = (number + TURN - 1) // TURN * TURN
        bounds.append(number // TURN)
    acc[...] = jnp.zeros_like(acc)
    tile_buf[slots] = jnp.zeros_like(tile_buf[slots])
    for load in panel_loads:
        load.wait()

    def turn(n, g, carry):
        firsts = [first_of[g * TURN + i] for i in range(TURN)]
        entries = [[entry[n][at + j] for j in range(PAIR)] for at in firsts]
        slot = [[e >> shift for e in pair] for pair in entries]
        column = [[e & ((1 << shift) - 1) for e in pair] for pair in entries]
        if not resident:
            copies = [
                pltpu.make_async_copy(
                    panels.at[column[i][j]],
                    panel_buf.at[i * PAIR + j],
                    panel_sem.at[i * PAIR + j],
                )
                for i in range(TURN)
                for j in range(PAIR)
            ]
            for copy in copies:
                copy.start()
            for copy in copies:
                copy.wait()
        for i in range(TURN):
            left = jnp.concatenate([tile_buf[slot[i][j]] for j in range(PAIR)], axis=1)
            right = jnp.concatenate(
                [panel_buf[column[i][j] if resident else i * PAIR + j] for j in range(PAIR)],
                axis=0,
            )
            acc[key_of[g * TURN + i]] += jnp.dot(left, right, preferred_element_type=F32)
        return carry

    for n, load in enumerate(tile_loads):
        load.wait()
        lax.fori_loop(bounds[n], bounds[n + 1], functools.partial(turn, n), 0)
    first = 0
    for out in outs:
        out[...] = acc[first : first + out.shape[0]]
        first += out.shape[0]


def tile_products(counts, places, tiles, panels, tile_rows, spans):
    slots, size, _ = tiles.shape
    width = panels.shape[2]
    sizes = [end - head for _, head, end in spans] * 2
    blocks = sum(sizes)
    part = -(-slots // PARTS)
    stride = (min(part, panels.shape[0]) // PAIR + 1) * PAIR
    pairs = PARTS * blocks * stride // PAIR + TURN * (PARTS + 1)
    resident = panels.size * 2 <= 16 << 20
    panel_shape = (panels.shape[0] if resident else PAIR * TURN, size, width)
    return pl.pallas_call(
        functools.partial(tile_kernel, resident, spans, stride),
        out_shape=[jax.ShapeDtypeStruct((n, size, width), F32) for n in sizes],
        in_specs=[SMEM, HBM, HBM, HBM],
        out_specs=[VMEM] * len(sizes),
        scratch_shapes=[
            pltpu.VMEM((slots + 1, size, size), BF16),
            pltpu.VMEM(panel_shape, BF16),
            pltpu.SMEM((2, slots), jnp.int32),
            pltpu.SMEM((tile_rows,), jnp.int32),
            pltpu.SMEM((pairs,), jnp.int32),
            pltpu.SMEM((pairs,), jnp.int32),
            pltpu.VMEM((blocks, size, width), F32),
            pltpu.SemaphoreType.DMA((1 + PARTS,)),
            pltpu.SemaphoreType.DMA((1 if resident else PAIR * TURN,)),
        ]
        + [pltpu.SMEM((blocks + 1,), jnp.int32)] * PARTS
        + [pltpu.SMEM((blocks * stride + part + PAIR,), jnp.int32)] * PARTS,
        compiler_params=params(50 << 20),
    )(counts, in_hbm(places), tiles, panels)


def gram_rows(order):
    under = [(i, j) for i in range(order) for j in range(i)]
    heads = {block: n * BLOCK for n, block in enumerate(under)}
    first = len(under) * BLOCK
    pairs = []
    for i in range(0, order, 2):
        pairs.append((i, i + 1, first, 0))
        first += BLOCK
    pairs = [(i, j, head, first + n) for n, (i, j, head, _) in enumerate(pairs)]
    return heads, pairs, first, -(-(first + len(pairs)) // 64) * 64


def square_index():
    return (
        lax.broadcasted_iota(jnp.int32, (BLOCK, BLOCK), 0),
        lax.broadcasted_iota(jnp.int32, (BLOCK, BLOCK), 1),
    )


def gram_kernel(last, *refs):
    if last:
        keep, core, across, *earlier, rows, own, send, acc = refs
    else:
        keep, core, across, rows, acc = refs
    total = (keep[...] + core[...]) + across[...]
    total = total.reshape(rows.shape)
    rows[...] = total
    high, low = halves(total)
    left = jnp.concatenate([high, high, low], axis=0)
    right = jnp.concatenate([high, low, high], axis=0)
    order = rows.shape[1] // BLOCK
    heads, pairs, slab, number = gram_rows(order)
    diagonal = {}
    for i in range(order):
        strip = lax.dot_general(
            left[:, i * BLOCK : (i + 1) * BLOCK],
            right[:, : (i + 1) * BLOCK],
            (((0,), (0,)), ((), ())),
            preferred_element_type=F32,
        )
        for j in range(i):
            acc[pl.ds(heads[i, j], BLOCK)] = strip[:, j * BLOCK : (j + 1) * BLOCK]
        diagonal[i] = strip[:, i * BLOCK :]
    acc[pl.ds(slab, number - slab)] = jnp.zeros((number - slab, BLOCK), F32)
    r, c = square_index()
    for i, j, head, line in pairs:
        acc[pl.ds(head, BLOCK)] = jnp.where(r >= c, diagonal[i], diagonal[j])
        acc[pl.ds(line, 1)] = jnp.sum(jnp.where(r == c, diagonal[j], 0.0), axis=0, keepdims=True)
    if last:
        for gram in earlier:
            acc[...] += gram[...]
    if last:
        core_bit, me = place()
        size = own.shape[1]
        half = acc.shape[0] // 2
        for d in range(own.shape[0]):
            at = (me ^ d) * size
            own[d] = acc[pl.ds(pl.multiple_of(core_bit * half + at, 8), size)]
            send[d] = acc[pl.ds(pl.multiple_of((1 - core_bit) * half + at, 8), size)]


def place():
    row, col = lax.axis_index("row"), lax.axis_index("col")
    return col & 1, (row & 1) | (col & 2)


def gram_chunk(keep, core, across, earlier, last):
    width = keep.shape[2]
    rows = keep.shape[0] * keep.shape[1]
    number = gram_rows(width // BLOCK)[3]
    whole = jax.ShapeDtypeStruct((number, BLOCK), F32)
    pieces = jax.ShapeDtypeStruct((4, number // 8, BLOCK), F32)
    row_shape = jax.ShapeDtypeStruct((rows, width), F32)
    args = [keep, core, across] + (list(earlier) if last else [])
    outs = [row_shape] + ([pieces, pieces] if last else [whole])
    return pl.pallas_call(
        functools.partial(gram_kernel, last),
        out_shape=outs,
        in_specs=[VMEM] * len(args),
        out_specs=[VMEM] * len(outs),
        scratch_shapes=[pltpu.VMEM(whole.shape, F32)] if last else [],
        compiler_params=params(16 << 20),
    )(*args)


def swapped(x, row_flip, col_flip):
    rows, cols = lax.axis_size("row"), lax.axis_size("col")
    if not row_flip:
        return lax.ppermute(x, "col", [(c, c ^ col_flip) for c in range(cols)])
    if not col_flip:
        return lax.ppermute(x, "row", [(r, r ^ row_flip) for r in range(rows)])
    route = [
        (r * cols + c, (r ^ row_flip) * cols + (c ^ col_flip))
        for r in range(rows)
        for c in range(cols)
    ]
    return lax.ppermute(x, ("row", "col"), route)


FLIPS = ((1, 0), (0, 2), (1, 2))


def gram_sum(own, send):
    theirs = swapped(send, 0, 1)
    part = [own[d] + theirs[d] for d in range(4)]
    got = [swapped(x, *flip) for x, flip in zip(part[1:], FLIPS)]
    piece = (part[0] + got[0]) + (got[1] + got[2])
    bits = lax.axis_size("row").bit_length() - 1
    bit = 1
    while bit < bits:
        if bit + 1 < bits:
            a, b = 1 << bit, 2 << bit
            got = [swapped(piece, flip, 0) for flip in (a, b, a | b)]
            piece = (piece + got[0]) + (got[1] + got[2])
            bit += 2
        else:
            piece = piece + swapped(piece, 1 << bit, 0)
            bit += 1
    mine = [piece] + [swapped(piece, *flip) for flip in FLIPS]
    return mine, [swapped(x, 0, 1) for x in mine]


def against(left, right_rows):
    lh, ll = left
    rh, rl = right_rows
    return lax.dot_general(
        jnp.concatenate([lh, lh, ll], axis=1),
        jnp.concatenate([rh, rl, rh], axis=1),
        (((1,), (1,)), ((), ())),
        preferred_element_type=F32,
    )


def times(left, right):
    lh, ll = left
    rh, rl = right
    return jnp.dot(
        jnp.concatenate([lh, lh, ll], axis=1),
        jnp.concatenate([rh, rl, rh], axis=0),
        preferred_element_type=F32,
    )


def factor_kernel(chunks, scale, rounds, *refs):
    pieces, rows = refs[:8], refs[8 : 8 + chunks]
    basis_out, triangle_out = refs[8 + chunks : 10 + chunks]
    blocks, gram, half_mask, half_eye, w, basis, triangle, out_sem = refs[10 + chunks : 18 + chunks]
    wb, gh, gl, yh, yl, ph, dh, dl = refs[18 + chunks :]
    size = gram.shape[0]
    order = size // BLOCK
    core_bit, me = place()
    half = blocks.shape[0] // 2
    for n, piece in enumerate(pieces):
        at = (core_bit ^ (n // 4)) * half + (me ^ (n % 4)) * piece.shape[0]
        blocks[pl.ds(pl.multiple_of(at, 8), piece.shape[0])] = piece[...]
    at = [slice(i * BLOCK, (i + 1) * BLOCK) for i in range(order)]

    r, c = square_index()
    row_scale, col_scale = [], []
    heads, pairs, _, _ = gram_rows(order)
    lower = {}
    for i, j, head, line in pairs:
        packed = blocks[pl.ds(head, BLOCK)]
        turned = packed.T
        lower[i, i] = jnp.where(r >= c, packed, turned)
        lower[j, j] = jnp.where(
            r < c, packed, jnp.where(r == c, blocks[pl.ds(line, 1)], turned)
        )
    for i in range(order):
        diagonal = jnp.where(r == c, lower[i, i], 0.0)
        row_scale.append(lax.rsqrt(jnp.sum(diagonal, axis=1, keepdims=True)))
        col_scale.append(lax.rsqrt(jnp.sum(diagonal, axis=0, keepdims=True)))
    for i, j in [(i, j) for i in range(order) for j in range(i + 1)]:
        block = lower[i, i] if i == j else blocks[pl.ds(heads[i, j], BLOCK)]
        first = -(block * row_scale[i] * col_scale[j])
        if i == j:
            first = jnp.where(r > c, first, jnp.where(r == c, 1.0, 0.0))
        wb[at[i], at[j]] = (first * col_scale[j]).astype(BF16)
        for p, q, x in [(i, j, block)] + ([(j, i, block.T)] if i != j else []):
            gram[at[p], at[q]] = x
            gh[at[p], at[q]], gl[at[p], at[q]] = halves(x)
        if i != j:
            wb[at[j], at[i]] = jnp.zeros((BLOCK, BLOCK), BF16)

    wide = size // 2
    top, low = slice(0, wide), slice(wide, size)
    r = lax.broadcasted_iota(jnp.int32, (wide, wide), 0)
    c = lax.broadcasted_iota(jnp.int32, (wide, wide), 1)
    half_mask[...] = jnp.where(r > c, 1.0, jnp.where(r == c, 0.5, 0.0))
    half_eye[...] = jnp.where(r == c, 0.5, 0.0)
    for ref in (ph, dh, dl):
        ref[top, low] = jnp.zeros((wide, wide), BF16)

    def dot(left, right):
        return jnp.dot(left, right, preferred_element_type=F32)

    def dot_rows(left, right):
        return lax.dot_general(left, right, (((1,), (1,)), ((), ())), preferred_element_type=F32)

    def twice(x, axis=1):
        return jnp.concatenate([x, x], axis=axis)

    def both(x, y, axis=1):
        return jnp.concatenate([x, y], axis=axis)

    def step(exact):
        for cols, k in ((top, wide), (low, size)):
            if exact:
                y = dot_rows(both(gh[:, :k], gl[:, :k]), twice(wb[cols, :k]))
                yh[:, cols], yl[:, cols] = halves(y)
            else:
                yh[:, cols] = dot_rows(gh[:, :k], wb[cols, :k]).astype(BF16)
        norm = jnp.zeros((1, 1), F32)
        strips = []
        for part, k in ((top, wide), (low, size)):
            if exact:
                m = dot(twice(wb[part, :k]), both(yh[:k, :k], yl[:k, :k], 0))
            else:
                m = dot(wb[part, :k], yh[:k, :k])
            corner = m[:, k - wide :] * half_mask[...] - half_eye[...]
            p = corner if k == wide else both(m[:, :wide], corner)
            ph[part, :k] = p.astype(BF16)
            strips.append(p)
            if exact:
                norm = norm + jnp.sum(p * p, keepdims=True)
        for p, part, k in zip(strips, (top, low), (wide, size)):
            square = dot(ph[part, :k], ph[:k, :k])
            cross = dot_rows(ph[part, :k], ph[:k, :k])
            corner = cross[:, k - wide :] * half_mask[...]
            cross = corner if k == wide else both(cross[:, :wide], corner)
            d = p - square - cross
            if exact:
                dh[part, :k], dl[part, :k] = halves(d)
            else:
                dh[part, :k] = d.astype(BF16)
        for part, k in ((top, wide), (low, size)):
            if exact:
                change = dot(both(dh[part, :k], dl[part, :k]), twice(wb[:k, :k], 0))
            else:
                change = dot(dh[part, :k], wb[:k, :k])
            w[part, :k] = wb[part, :k].astype(F32) - change
        return jnp.sum(norm)

    def rounded():
        for part, k in ((top, wide), (low, size)):
            wb[part, :k] = w[part, :k].astype(BF16)

    step(False)

    def not_done(state):
        count, norm = state
        return jnp.logical_and(count < rounds, jnp.logical_not(norm < SMALL))

    def again(state):
        rounded()
        return state[0] + 1, step(True)

    _, norm = lax.while_loop(not_done, again, (jnp.int32(0), jnp.float32(1.0)))
    triangle_copy = pltpu.make_async_copy(triangle, triangle_out, out_sem.at[0])
    found = norm < SMALL

    @pl.when(found)
    def _():
        for part, k in ((top, wide), (low, size)):
            wb[part, :k], dl[part, :k] = halves(w[part, :k])
        for part, k in ((top, wide), (low, size)):
            upper = times((wb[part, :k], dl[part, :k]), (gh[:k, k - wide :], gl[:k, k - wide :]))
            corner = jnp.where(r <= c, upper[:, :wide], 0.0)
            upper = both(corner, upper[:, wide:]) if k == wide else corner
            triangle[part, k - wide :] = upper * (1.0 / scale)
        triangle[low, top] = jnp.zeros((wide, wide), F32)
        triangle_copy.start()
        copies = [triangle_copy]
        first = 0
        for part in rows:
            for head in range(0, part.shape[0], wide):
                count = min(wide, part.shape[0] - head)
                sh, sl = halves(part[head : head + count])
                here = pl.ds(first, count)
                for cols, k in ((top, wide), (low, size)):
                    out = against((sh[:, :k], sl[:, :k]), (wb[cols, :k], dl[cols, :k]))
                    basis[here, cols] = out * scale
                sem = out_sem.at[len(copies)]
                copies.append(pltpu.make_async_copy(basis.at[here], basis_out.at[here], sem))
                copies[-1].start()
                first += count
        for copy in copies:
            copy.wait()

    @pl.when(jnp.logical_not(found))
    def _():
        eliminate(gram, triangle, w)
        triangle[...] = triangle[...] * (1.0 / scale)
        first = 0
        for part in rows:

            def strip(n, carry, part=part, first=first):
                at = pl.ds(pl.multiple_of(n * BLOCK, BLOCK), BLOCK)
                out = exact_dot(part[at, :], w[...], (((1,), (1,)), ((), ())))
                here = pl.multiple_of(first + n * BLOCK, BLOCK)
                basis[pl.ds(here, BLOCK), :] = out * scale
                return carry

            lax.fori_loop(0, part.shape[0] // BLOCK, strip, 0)
            first += part.shape[0]
        basis_copy = pltpu.make_async_copy(basis, basis_out, out_sem.at[1])
        triangle_copy.start()
        basis_copy.start()
        triangle_copy.wait()
        basis_copy.wait()


def exact_dot(left, right, dims):
    return lax.dot_general(
        left, right, dims, precision=lax.Precision.HIGHEST, preferred_element_type=F32
    )


def eliminate(gram, upper, inverse):
    size = gram.shape[0]
    columns = lax.broadcasted_iota(jnp.int32, (BLOCK, size), 1)
    lines = lax.broadcasted_iota(jnp.int32, (BLOCK, size), 0)
    r, c = square_index()
    line = r[:, :1]
    for n in range(size // BLOCK):
        here = slice(n * BLOCK, (n + 1) * BLOCK)
        left = gram[here, :]
        right = jnp.where(columns == lines + n * BLOCK, 1.0, 0.0)
        if n:
            above = upper[: n * BLOCK, here]
            over = (((0,), (0,)), ((), ()))
            left = left - exact_dot(above, upper[: n * BLOCK, :], over)
            right = right - exact_dot(above, inverse[: n * BLOCK, :], over)
        upper[here, :] = left
        inverse[here, :] = right

        def row(j, carry, n=n, here=here):
            at = pl.ds(n * BLOCK + j, 1)
            corner = upper[here, here]
            column = jnp.sum(jnp.where(c == j, corner, 0.0), axis=1, keepdims=True)
            pivot = jnp.sum(jnp.where(line == j, column, 0.0), axis=0, keepdims=True)
            root = lax.rsqrt(pivot)
            left = upper[at, :] * root
            right = inverse[at, :] * root
            factor_of = jnp.where(line > j, column * root, 0.0)
            upper[here, :] = upper[here, :] - factor_of * left
            inverse[here, :] = inverse[here, :] - factor_of * right
            upper[at, :] = left
            inverse[at, :] = right
            return carry

        lax.fori_loop(0, BLOCK, row, 0)
        upper[here, :] = jnp.where(columns >= lines + n * BLOCK, upper[here, :], 0.0)


def factor(pieces, rows, scale):
    width = rows[0].shape[1]
    square = (width, width)
    local = sum(part.shape[0] for part in rows)
    number = gram_rows(width // BLOCK)[3]
    return pl.pallas_call(
        functools.partial(factor_kernel, len(rows), scale, 6),
        out_shape=[
            pltpu.HBM((local, width), F32),
            pltpu.HBM(square, F32),
        ],
        in_specs=[VMEM] * (8 + len(rows)),
        out_specs=[HBM, HBM],
        scratch_shapes=[
            pltpu.VMEM((number, BLOCK), F32),
            pltpu.VMEM(square, F32),
            pltpu.VMEM((width // 2, width // 2), F32),
            pltpu.VMEM((width // 2, width // 2), F32),
            pltpu.VMEM(square, F32),
            pltpu.VMEM((local, width), F32),
            pltpu.VMEM(square, F32),
            pltpu.SemaphoreType.DMA((1 + sum(-(-part.shape[0] * 2 // width) for part in rows),)),
        ]
        + [pltpu.VMEM(square, BF16)] * 8,
        compiler_params=params(24 << 20),
    )(*pieces, *rows)


def body(tile_values, tile_places, tile_counts, sketch):
    tiles = tile_values[0, 0]
    size = tiles.shape[1]
    width = sketch.shape[1]
    row_devices = lax.axis_size("row")
    col_devices = lax.axis_size("col")
    local_rows = sketch.shape[0] // row_devices
    tile_rows = local_rows * col_devices // size
    panels = sketch.reshape(-1, size, width)
    places = tile_places[0, 0]
    scale = math.sqrt(local_rows * row_devices * col_devices)
    per_owner = tile_rows // col_devices
    cuts = sorted({0, per_owner // 6, per_owner * 5 // 6, per_owner})
    chunks = list(zip(cuts, cuts[1:]))
    early = chunks[:-1] or chunks
    late = chunks[len(early) :]

    def products(spans):
        out = tile_products(tile_counts, places, tiles, panels, tile_rows, tuple(spans))
        return out[: len(spans)], out[len(spans) :]

    def across_cores(send, keep):
        own = []
        for n in range(len(send)):
            if n == 1:
                *send[1:], core = lax.optimization_barrier((*send[1:], core))
            core = swapped(send[n], 0, 1)
            own.append(keep[n] + core)
        return own

    send, keep = products([(1, head, end) for head, end in early])
    own = across_cores(list(send), keep)
    across = [swapped(x, 0, 2) for x in own]
    places, own = lax.optimization_barrier((places, own))
    send, keep = products([(1, *chunk) for chunk in late] + [(0, *chunk) for chunk in chunks])
    send, keep, across[0] = lax.optimization_barrier((send, keep, across[0]))
    across += [swapped(x, 0, 2) for x in across_cores(send[: len(late)], keep[: len(late)])]
    send, keep = send[len(late) :], keep[len(late) :]
    chunks = len(chunks)
    rows, grams = [], []
    for n in range(chunks):
        out = gram_chunk(keep[n], swapped(send[n], 0, 1), across[n], grams, n == chunks - 1)
        rows.append(out[0])
        grams.append(out[1])
    mine, theirs = gram_sum(*out[1:])
    basis, triangle = factor(mine + theirs, rows, scale)
    return basis, triangle


def solution(mesh):
    in_specs = (
        P("row", "col", None, None, None),
        P("row", "col", None, None),
        P("row", "col"),
        P("col", None),
    )
    out_specs = (P(("row", "col"), None), P())
    return jax.shard_map(body, mesh=mesh, in_specs=in_specs, out_specs=out_specs, check_vma=False)
```

```python
import functools
import math

import jax
import jax.numpy as jnp
from jax import lax
from jax.experimental import pallas as pl
from jax.experimental.pallas import tpu as pltpu
from jax.sharding import PartitionSpec as P

BF16 = jnp.bfloat16
F32 = jnp.float32
PAIR = 2
TURN = 20
PARTS = 2
BLOCK = 128
SMALL = 0.01
SMEM = pl.BlockSpec(memory_space=pltpu.SMEM)
VMEM = pl.BlockSpec(memory_space=pltpu.VMEM)
HBM = pl.BlockSpec(memory_space=pltpu.HBM)

def in_hbm(x):
    return pltpu.with_memory_space_constraint(x, pltpu.HBM)


def params(size):
    return pltpu.CompilerParams(vmem_limit_bytes=size)


def halves(x):
    high = x.astype(BF16)
    return high, (x - high.astype(F32)).astype(BF16)


def tile_kernel(resident, spans, stride, counts, places, tiles, panels, *refs):
    outs, refs = refs[: 2 * len(spans)], refs[2 * len(spans) :]
    tile_buf, panel_buf, place_of, key, first_of, key_of, acc, load_sem, panel_sem = refs[:9]
    fill, entry = refs[9:-1], refs[-1]
    slots = tiles.shape[0]
    blocks = acc.shape[0]
    per_owner = key.shape[0] // lax.axis_size("col")
    panel_loads = [pltpu.make_async_copy(panels, panel_buf, panel_sem.at[0])] if resident else []
    cuts = [-(-slots * n // PARTS) for n in range(PARTS + 1)]
    tile_loads = [
        pltpu.make_async_copy(
            tiles.at[pl.ds(a, b - a)], tile_buf.at[pl.ds(a, b - a)], load_sem.at[1 + n]
        )
        for n, (a, b) in enumerate(zip(cuts, cuts[1:]))
    ]
    place_load = pltpu.make_async_copy(places, place_of, load_sem.at[0])
    for load in [place_load] + panel_loads + tile_loads:
        load.start()
    own = lax.axis_index("col")

    heads = {}
    for n, (flip, head, end) in enumerate(spans):
        for inside in range(head, end):
            heads[flip, inside] = sum(e - h for _, h, e in spans[:n]) + inside - head
    for owner in range(key.shape[0] // per_owner):
        base = jnp.where((owner & 1) == (own & 1), blocks // 2, 0)
        flipped = (owner >> 1) != (own >> 1)
        for inside in range(per_owner):
            name = [base + heads[f, inside] if (f, inside) in heads else blocks for f in (0, 1)]
            key[owner * per_owner + inside] = jnp.where(flipped, name[1], name[0])
    base = [n * (blocks * stride + cuts[1]) for n in range(PARTS + 1)]
    for n in range(PARTS):
        for k in range(blocks + 1):
            fill[n][k] = base[n] + k * stride
    place_load.wait()
    live = counts[0, 0]
    shift = panels.shape[0].bit_length()
    unroll = math.gcd(cuts[1], 6)

    def put(g, carry):
        for i in range(unroll):
            mine = [jnp.minimum(cut + g * unroll + i, slots - 1) for cut in cuts[:-1]]
            names = [key[place_of[0, t]] for t in mine]
            made = [(t << shift) | place_of[1, t] for t in mine]
            lists = [
                jnp.where(cut + g * unroll + i < live, name, blocks)
                for cut, name in zip(cuts, names)
            ]
            spots = [fill[n][k] for n, k in enumerate(lists)]
            for n in range(PARTS):
                fill[n][lists[n]] = spots[n] + 1
                entry[spots[n]] = made[n]
        return carry

    lax.fori_loop(0, (jnp.minimum(live, cuts[1]) + unroll - 1) // unroll, put, 0)

    for i in range(PAIR):
        entry[base[-1] + i] = slots << shift
    number, bounds = 0, [0]
    for n in range(PARTS):
        for k in range(blocks):
            head = base[n] + k * stride
            end = fill[n][k]
            for i in range(PAIR - 1):
                entry[end + i] = slots << shift

            def add_pair(j, at, head=head, k=k):
                first_of[at + j] = head + j * PAIR
                key_of[at + j] = k
                return at

            pairs = (end - head + PAIR - 1) // PAIR
            lax.fori_loop(0, pairs, add_pair, number)
            number += pairs
        bounds.append(number // TURN)
    for i in range(TURN - 1):
        first_of[number + i] = base[-1]
        key_of[number + i] = 0
    bounds[-1] = (number + TURN - 1) // TURN
    acc[...] = jnp.zeros_like(acc)
    tile_buf[slots] = jnp.zeros_like(tile_buf[slots])
    for load in panel_loads:
        load.wait()

    def turn(g, carry):
        firsts = [first_of[g * TURN + i] for i in range(TURN)]
        entries = [[entry[at + j] for j in range(PAIR)] for at in firsts]
        slot = [[e >> shift for e in pair] for pair in entries]
        column = [[e & ((1 << shift) - 1) for e in pair] for pair in entries]
        if not resident:
            copies = [
                pltpu.make_async_copy(
                    panels.at[column[i][j]],
                    panel_buf.at[i * PAIR + j],
                    panel_sem.at[i * PAIR + j],
                )
                for i in range(TURN)
                for j in range(PAIR)
            ]
            for copy in copies:
                copy.start()
            for copy in copies:
                copy.wait()
        for i in range(TURN):
            left = jnp.concatenate([tile_buf[slot[i][j]] for j in range(PAIR)], axis=1)
            right = jnp.concatenate(
                [panel_buf[column[i][j] if resident else i * PAIR + j] for j in range(PAIR)],
                axis=0,
            )
            acc[key_of[g * TURN + i]] += jnp.dot(left, right, preferred_element_type=F32)
        return carry

    for n, load in enumerate(tile_loads):
        load.wait()
        lax.fori_loop(bounds[n], bounds[n + 1], turn, 0)
    first = 0
    for out in outs:
        out[...] = acc[first : first + out.shape[0]]
        first += out.shape[0]


def tile_products(counts, places, tiles, panels, tile_rows, spans):
    slots, size, _ = tiles.shape
    width = panels.shape[2]
    sizes = [end - head for _, head, end in spans] * 2
    blocks = sum(sizes)
    part = -(-slots // PARTS)
    stride = (min(part, panels.shape[0]) // PAIR + 1) * PAIR
    pairs = PARTS * blocks * stride // PAIR + TURN
    resident = panels.size * 2 <= 16 << 20
    panel_shape = (panels.shape[0] if resident else PAIR * TURN, size, width)
    return pl.pallas_call(
        functools.partial(tile_kernel, resident, spans, stride),
        out_shape=[jax.ShapeDtypeStruct((n, size, width), F32) for n in sizes],
        in_specs=[SMEM, HBM, HBM, HBM],
        out_specs=[VMEM] * len(sizes),
        scratch_shapes=[
            pltpu.VMEM((slots + 1, size, size), BF16),
            pltpu.VMEM(panel_shape, BF16),
            pltpu.SMEM((2, slots), jnp.int32),
            pltpu.SMEM((tile_rows,), jnp.int32),
            pltpu.SMEM((pairs,), jnp.int32),
            pltpu.SMEM((pairs,), jnp.int32),
            pltpu.VMEM((blocks, size, width), F32),
            pltpu.SemaphoreType.DMA((1 + PARTS,)),
            pltpu.SemaphoreType.DMA((1 if resident else PAIR * TURN,)),
        ]
        + [pltpu.SMEM((blocks + 1,), jnp.int32)] * PARTS
        + [pltpu.SMEM((PARTS * (blocks * stride + part) + PAIR,), jnp.int32)],
        compiler_params=params(50 << 20),
    )(counts, in_hbm(places), tiles, panels)


def gram_rows(order):
    under = [(i, j) for i in range(order) for j in range(i)]
    heads = {block: n * BLOCK for n, block in enumerate(under)}
    first = len(under) * BLOCK
    pairs = []
    for i in range(0, order, 2):
        pairs.append((i, i + 1, first, 0))
        first += BLOCK
    pairs = [(i, j, head, first + n) for n, (i, j, head, _) in enumerate(pairs)]
    return heads, pairs, first, -(-(first + len(pairs)) // 64) * 64


def square_index():
    return (
        lax.broadcasted_iota(jnp.int32, (BLOCK, BLOCK), 0),
        lax.broadcasted_iota(jnp.int32, (BLOCK, BLOCK), 1),
    )


def gram_kernel(last, *refs):
    if last:
        keep, core, across, *earlier, rows, own, send, acc = refs
    else:
        keep, core, across, rows, acc = refs
    total = (keep[...] + core[...]) + across[...]
    total = total.reshape(rows.shape)
    rows[...] = total
    high, low = halves(total)
    left = jnp.concatenate([high, high, low], axis=0)
    right = jnp.concatenate([high, low, high], axis=0)
    order = rows.shape[1] // BLOCK
    heads, pairs, slab, number = gram_rows(order)
    diagonal = {}
    for i in range(order):
        strip = lax.dot_general(
            left[:, i * BLOCK : (i + 1) * BLOCK],
            right[:, : (i + 1) * BLOCK],
            (((0,), (0,)), ((), ())),
            preferred_element_type=F32,
        )
        for j in range(i):
            acc[pl.ds(heads[i, j], BLOCK)] = strip[:, j * BLOCK : (j + 1) * BLOCK]
        diagonal[i] = strip[:, i * BLOCK :]
    acc[pl.ds(slab, number - slab)] = jnp.zeros((number - slab, BLOCK), F32)
    r, c = square_index()
    for i, j, head, line in pairs:
        acc[pl.ds(head, BLOCK)] = jnp.where(r >= c, diagonal[i], diagonal[j])
        acc[pl.ds(line, 1)] = jnp.sum(jnp.where(r == c, diagonal[j], 0.0), axis=0, keepdims=True)
    if last:
        for gram in earlier:
            acc[...] += gram[...]
    if last:
        core_bit, me = place()
        size = own.shape[1]
        half = acc.shape[0] // 2
        for d in range(own.shape[0]):
            at = (me ^ d) * size
            own[d] = acc[pl.ds(pl.multiple_of(core_bit * half + at, 8), size)]
            send[d] = acc[pl.ds(pl.multiple_of((1 - core_bit) * half + at, 8), size)]


def place():
    row, col = lax.axis_index("row"), lax.axis_index("col")
    return col & 1, (row & 1) | (col & 2)


def gram_chunk(keep, core, across, earlier, last):
    width = keep.shape[2]
    rows = keep.shape[0] * keep.shape[1]
    number = gram_rows(width // BLOCK)[3]
    whole = jax.ShapeDtypeStruct((number, BLOCK), F32)
    pieces = jax.ShapeDtypeStruct((4, number // 8, BLOCK), F32)
    row_shape = jax.ShapeDtypeStruct((rows, width), F32)
    args = [keep, core, across] + (list(earlier) if last else [])
    outs = [row_shape] + ([pieces, pieces] if last else [whole])
    return pl.pallas_call(
        functools.partial(gram_kernel, last),
        out_shape=outs,
        in_specs=[VMEM] * len(args),
        out_specs=[VMEM] * len(outs),
        scratch_shapes=[pltpu.VMEM(whole.shape, F32)] if last else [],
        compiler_params=params(16 << 20),
    )(*args)


def swapped(x, row_flip, col_flip):
    rows, cols = lax.axis_size("row"), lax.axis_size("col")
    if not row_flip:
        return lax.ppermute(x, "col", [(c, c ^ col_flip) for c in range(cols)])
    if not col_flip:
        return lax.ppermute(x, "row", [(r, r ^ row_flip) for r in range(rows)])
    route = [
        (r * cols + c, (r ^ row_flip) * cols + (c ^ col_flip))
        for r in range(rows)
        for c in range(cols)
    ]
    return lax.ppermute(x, ("row", "col"), route)


FLIPS = ((1, 0), (0, 2), (1, 2))


def gram_sum(own, send):
    theirs = swapped(send, 0, 1)
    part = [own[d] + theirs[d] for d in range(4)]
    got = [swapped(x, *flip) for x, flip in zip(part[1:], FLIPS)]
    piece = (part[0] + got[0]) + (got[1] + got[2])
    bits = lax.axis_size("row").bit_length() - 1
    bit = 1
    while bit < bits:
        if bit + 1 < bits:
            a, b = 1 << bit, 2 << bit
            got = [swapped(piece, flip, 0) for flip in (a, b, a | b)]
            piece = (piece + got[0]) + (got[1] + got[2])
            bit += 2
        else:
            piece = piece + swapped(piece, 1 << bit, 0)
            bit += 1
    mine = [piece] + [swapped(piece, *flip) for flip in FLIPS]
    return mine, [swapped(x, 0, 1) for x in mine]


def against(left, right_rows):
    lh, ll = left
    rh, rl = right_rows
    return lax.dot_general(
        jnp.concatenate([lh, lh, ll], axis=1),
        jnp.concatenate([rh, rl, rh], axis=1),
        (((1,), (1,)), ((), ())),
        preferred_element_type=F32,
    )


def times(left, right):
    lh, ll = left
    rh, rl = right
    return jnp.dot(
        jnp.concatenate([lh, lh, ll], axis=1),
        jnp.concatenate([rh, rl, rh], axis=0),
        preferred_element_type=F32,
    )


def factor_kernel(chunks, scale, rounds, *refs):
    pieces, rows = refs[:8], refs[8 : 8 + chunks]
    basis_out, triangle_out = refs[8 + chunks : 10 + chunks]
    blocks, gram, half_mask, half_eye, w, basis, triangle, out_sem = refs[10 + chunks : 18 + chunks]
    wb, gh, gl, yh, yl, ph, dh, dl = refs[18 + chunks :]
    size = gram.shape[0]
    order = size // BLOCK
    core_bit, me = place()
    half = blocks.shape[0] // 2
    for n, piece in enumerate(pieces):
        at = (core_bit ^ (n // 4)) * half + (me ^ (n % 4)) * piece.shape[0]
        blocks[pl.ds(pl.multiple_of(at, 8), piece.shape[0])] = piece[...]
    at = [slice(i * BLOCK, (i + 1) * BLOCK) for i in range(order)]

    r, c = square_index()
    row_scale, col_scale = [], []
    heads, pairs, _, _ = gram_rows(order)
    lower = {}
    for i, j, head, line in pairs:
        packed = blocks[pl.ds(head, BLOCK)]
        turned = packed.T
        lower[i, i] = jnp.where(r >= c, packed, turned)
        lower[j, j] = jnp.where(
            r < c, packed, jnp.where(r == c, blocks[pl.ds(line, 1)], turned)
        )
    for i in range(order):
        diagonal = jnp.where(r == c, lower[i, i], 0.0)
        row_scale.append(lax.rsqrt(jnp.sum(diagonal, axis=1, keepdims=True)))
        col_scale.append(lax.rsqrt(jnp.sum(diagonal, axis=0, keepdims=True)))
    for i, j in [(i, j) for i in range(order) for j in range(i + 1)]:
        block = lower[i, i] if i == j else blocks[pl.ds(heads[i, j], BLOCK)]
        first = -(block * row_scale[i] * col_scale[j])
        if i == j:
            first = jnp.where(r > c, first, jnp.where(r == c, 1.0, 0.0))
        wb[at[i], at[j]] = (first * col_scale[j]).astype(BF16)
        for p, q, x in [(i, j, block)] + ([(j, i, block.T)] if i != j else []):
            gram[at[p], at[q]] = x
            gh[at[p], at[q]], gl[at[p], at[q]] = halves(x)
        if i != j:
            wb[at[j], at[i]] = jnp.zeros((BLOCK, BLOCK), BF16)

    wide = size // 2
    top, low = slice(0, wide), slice(wide, size)
    r = lax.broadcasted_iota(jnp.int32, (wide, wide), 0)
    c = lax.broadcasted_iota(jnp.int32, (wide, wide), 1)
    half_mask[...] = jnp.where(r > c, 1.0, jnp.where(r == c, 0.5, 0.0))
    half_eye[...] = jnp.where(r == c, 0.5, 0.0)
    ph[top, low] = jnp.zeros((wide, wide), BF16)

    def dot(left, right):
        return jnp.dot(left, right, preferred_element_type=F32)

    def dot_rows(left, right):
        return lax.dot_general(left, right, (((1,), (1,)), ((), ())), preferred_element_type=F32)

    def twice(x, axis=1):
        return jnp.concatenate([x, x], axis=axis)

    def both(x, y, axis=1):
        return jnp.concatenate([x, y], axis=axis)

    def step(exact):
        for cols, k in ((top, wide), (low, size)):
            if exact:
                y = dot_rows(both(gh[:, :k], gl[:, :k]), twice(wb[cols, :k]))
                yh[:, cols], yl[:, cols] = halves(y)
            else:
                yh[:, cols] = dot_rows(gh[:, :k], wb[cols, :k]).astype(BF16)
        norm = jnp.zeros((1, 1), F32)
        strips = []
        for part, k in ((top, wide), (low, size)):
            if exact:
                m = dot(twice(wb[part, :k]), both(yh[:k, :k], yl[:k, :k], 0))
            else:
                m = dot(wb[part, :k], yh[:k, :k])
            corner = m[:, k - wide :] * half_mask[...] - half_eye[...]
            p = corner if k == wide else both(m[:, :wide], corner)
            ph[part, :k] = p.astype(BF16)
            strips.append(p)
            if exact:
                norm = norm + jnp.sum(p * p, keepdims=True)
        for p, part, k in zip(strips, (top, low), (wide, size)):
            corner = dot_rows(ph[part, :k], ph[part, :k]) * half_mask[...]
            corner = p[:, k - wide :] - dot(ph[part, part], ph[part, part]) - corner
            dh[part, part] = corner.astype(BF16)
            if k == size:
                side = dot(ph[low, :], ph[:, top]) + dot_rows(ph[low, top], ph[top, top])
                dh[low, top] = (p[:, :wide] - side).astype(BF16)
        for part in (top, low):
            w[part, part] = wb[part, part].astype(F32) - dot(dh[part, part], wb[part, part])
        w[low, top] = wb[low, top].astype(F32) - dot(dh[low, :], wb[:, top])
        return jnp.sum(norm)

    def rounded():
        for part, k in ((top, wide), (low, size)):
            wb[part, :k] = w[part, :k].astype(BF16)

    step(False)

    def not_done(state):
        count, norm = state
        return jnp.logical_and(count < rounds, jnp.logical_not(norm < SMALL))

    def again(state):
        rounded()
        return state[0] + 1, step(True)

    _, norm = lax.while_loop(not_done, again, (jnp.int32(0), jnp.float32(1.0)))
    found = norm < SMALL

    @pl.when(found)
    def _():
        for part, k in ((top, wide), (low, size)):
            wb[part, :k], dl[part, :k] = halves(w[part, :k])
        copies = []

        def send(source, target):
            copies.append(pltpu.make_async_copy(source, target, out_sem.at[len(copies)]))
            copies[-1].start()

        own_rows = jnp.concatenate([part[...] for part in rows], axis=0)
        count = own_rows.shape[0] // 2
        for n in range(2):
            here = pl.ds(n * count, count)
            sh, sl = halves(own_rows[n * count : (n + 1) * count])
            for cols, k in ((low, size), (top, wide)):
                out = against((sh[:, :k], sl[:, :k]), (wb[cols, :k], dl[cols, :k]))
                basis[here, cols] = out * scale
                send(basis.at[here, cols], basis_out.at[here, cols])
            if n == 1:
                for part, k in ((top, wide), (low, size)):
                    upper = times(
                        (wb[part, :k], dl[part, :k]), (gh[:k, k - wide :], gl[:k, k - wide :])
                    )
                    corner = jnp.where(r <= c, upper[:, :wide], 0.0)
                    upper = both(corner, upper[:, wide:]) if k == wide else corner
                    triangle[part, k - wide :] = upper * (1.0 / scale)
                triangle[low, top] = jnp.zeros((wide, wide), F32)
                send(triangle, triangle_out)
        for copy in copies:
            copy.wait()

    @pl.when(jnp.logical_not(found))
    def _():
        eliminate(gram, triangle, w)
        triangle[...] = triangle[...] * (1.0 / scale)
        first = 0
        for part in rows:

            def strip(n, carry, part=part, first=first):
                at = pl.ds(pl.multiple_of(n * BLOCK, BLOCK), BLOCK)
                out = exact_dot(part[at, :], w[...], (((1,), (1,)), ((), ())))
                here = pl.multiple_of(first + n * BLOCK, BLOCK)
                basis[pl.ds(here, BLOCK), :] = out * scale
                return carry

            lax.fori_loop(0, part.shape[0] // BLOCK, strip, 0)
            first += part.shape[0]
        copies = [
            pltpu.make_async_copy(triangle, triangle_out, out_sem.at[0]),
            pltpu.make_async_copy(basis, basis_out, out_sem.at[1]),
        ]
        for copy in copies:
            copy.start()
        for copy in copies:
            copy.wait()


def exact_dot(left, right, dims):
    return lax.dot_general(
        left, right, dims, precision=lax.Precision.HIGHEST, preferred_element_type=F32
    )


def eliminate(gram, upper, inverse):
    size = gram.shape[0]
    columns = lax.broadcasted_iota(jnp.int32, (BLOCK, size), 1)
    lines = lax.broadcasted_iota(jnp.int32, (BLOCK, size), 0)
    r, c = square_index()
    line = r[:, :1]
    for n in range(size // BLOCK):
        here = slice(n * BLOCK, (n + 1) * BLOCK)
        left = gram[here, :]
        right = jnp.where(columns == lines + n * BLOCK, 1.0, 0.0)
        if n:
            above = upper[: n * BLOCK, here]
            over = (((0,), (0,)), ((), ()))
            left = left - exact_dot(above, upper[: n * BLOCK, :], over)
            right = right - exact_dot(above, inverse[: n * BLOCK, :], over)
        upper[here, :] = left
        inverse[here, :] = right

        def row(j, carry, n=n, here=here):
            at = pl.ds(n * BLOCK + j, 1)
            corner = upper[here, here]
            column = jnp.sum(jnp.where(c == j, corner, 0.0), axis=1, keepdims=True)
            pivot = jnp.sum(jnp.where(line == j, column, 0.0), axis=0, keepdims=True)
            root = lax.rsqrt(pivot)
            left = upper[at, :] * root
            right = inverse[at, :] * root
            factor_of = jnp.where(line > j, column * root, 0.0)
            upper[here, :] = upper[here, :] - factor_of * left
            inverse[here, :] = inverse[here, :] - factor_of * right
            upper[at, :] = left
            inverse[at, :] = right
            return carry

        lax.fori_loop(0, BLOCK, row, 0)
        upper[here, :] = jnp.where(columns >= lines + n * BLOCK, upper[here, :], 0.0)


def factor(pieces, rows, scale):
    width = rows[0].shape[1]
    square = (width, width)
    local = sum(part.shape[0] for part in rows)
    number = gram_rows(width // BLOCK)[3]
    return pl.pallas_call(
        functools.partial(factor_kernel, len(rows), scale, 6),
        out_shape=[
            pltpu.HBM((local, width), F32),
            pltpu.HBM(square, F32),
        ],
        in_specs=[VMEM] * (8 + len(rows)),
        out_specs=[HBM, HBM],
        scratch_shapes=[
            pltpu.VMEM((number, BLOCK), F32),
            pltpu.VMEM(square, F32),
            pltpu.VMEM((width // 2, width // 2), F32),
            pltpu.VMEM((width // 2, width // 2), F32),
            pltpu.VMEM(square, F32),
            pltpu.VMEM((local, width), F32),
            pltpu.VMEM(square, F32),
            pltpu.SemaphoreType.DMA((5,)),
        ]
        + [pltpu.VMEM(square, BF16)] * 8,
        compiler_params=params(24 << 20),
    )(*pieces, *rows)


def body(tile_values, tile_places, tile_counts, sketch):
    tiles = tile_values[0, 0]
    size = tiles.shape[1]
    width = sketch.shape[1]
    row_devices = lax.axis_size("row")
    col_devices = lax.axis_size("col")
    local_rows = sketch.shape[0] // row_devices
    tile_rows = local_rows * col_devices // size
    panels = sketch.reshape(-1, size, width)
    places = tile_places[0, 0]
    scale = math.sqrt(local_rows * row_devices * col_devices)
    per_owner = tile_rows // col_devices
    cuts = sorted({0, per_owner // 6, per_owner * 5 // 6, per_owner})
    chunks = list(zip(cuts, cuts[1:]))
    early = chunks[:-1] or chunks
    late = chunks[len(early) :]

    def products(spans):
        out = tile_products(tile_counts, places, tiles, panels, tile_rows, tuple(spans))
        return out[: len(spans)], out[len(spans) :]

    def across_cores(send, keep):
        own = []
        for n in range(len(send)):
            if n == 1:
                *send[1:], core = lax.optimization_barrier((*send[1:], core))
            core = swapped(send[n], 0, 1)
            own.append(keep[n] + core)
        return own

    send, keep = products([(1, head, end) for head, end in early])
    own = across_cores(list(send), keep)
    across = [swapped(x, 0, 2) for x in own]
    places, own = lax.optimization_barrier((places, own))
    send, keep = products([(1, *chunk) for chunk in late] + [(0, *chunk) for chunk in chunks])
    send, keep, across[0] = lax.optimization_barrier((send, keep, across[0]))
    across += [swapped(x, 0, 2) for x in across_cores(list(send[: len(late)]), keep[: len(late)])]
    send, keep = send[len(late) :], keep[len(late) :]
    chunks = len(chunks)
    rows, grams = [], []
    for n in range(chunks):
        out = gram_chunk(keep[n], swapped(send[n], 0, 1), across[n], grams, n == chunks - 1)
        rows.append(out[0])
        grams.append(out[1])
    mine, theirs = gram_sum(*out[1:])
    basis, triangle = factor(mine + theirs, rows, scale)
    return basis, triangle


def solution(mesh):
    in_specs = (
        P("row", "col", None, None, None),
        P("row", "col", None, None),
        P("row", "col"),
        P("col", None),
    )
    out_specs = (P(("row", "col"), None), P())
    return jax.shard_map(body, mesh=mesh, in_specs=in_specs, out_specs=out_specs, check_vma=False)
```

```python
import functools
import math

import jax
import jax.numpy as jnp
from jax import lax
from jax.experimental import pallas as pl
from jax.experimental.pallas import tpu as pltpu
from jax.sharding import PartitionSpec as P

BF16 = jnp.bfloat16
F32 = jnp.float32
PAIR = 2
TURN = 20
PARTS = 2
BLOCK = 128
SMALL = 0.01
SMEM = pl.BlockSpec(memory_space=pltpu.SMEM)
VMEM = pl.BlockSpec(memory_space=pltpu.VMEM)
HBM = pl.BlockSpec(memory_space=pltpu.HBM)

def in_hbm(x):
    return pltpu.with_memory_space_constraint(x, pltpu.HBM)


def params(size):
    return pltpu.CompilerParams(vmem_limit_bytes=size)


def halves(x):
    high = x.astype(BF16)
    return high, (x - high.astype(F32)).astype(BF16)


def tile_kernel(resident, spans, stride, counts, places, tiles, panels, *refs):
    outs, refs = refs[: 2 * len(spans)], refs[2 * len(spans) :]
    tile_buf, panel_buf, place_of, key, first_of, key_of, acc, load_sem, panel_sem = refs[:9]
    fill, entry = refs[9:-1], refs[-1]
    slots = tiles.shape[0]
    blocks = acc.shape[0]
    per_owner = key.shape[0] // lax.axis_size("col")
    panel_loads = [pltpu.make_async_copy(panels, panel_buf, panel_sem.at[0])] if resident else []
    cuts = [-(-slots * n // PARTS) for n in range(PARTS + 1)]
    tile_loads = [
        pltpu.make_async_copy(
            tiles.at[pl.ds(a, b - a)], tile_buf.at[pl.ds(a, b - a)], load_sem.at[1 + n]
        )
        for n, (a, b) in enumerate(zip(cuts, cuts[1:]))
    ]
    place_load = pltpu.make_async_copy(places, place_of, load_sem.at[0])
    for load in [place_load] + panel_loads + tile_loads:
        load.start()
    own = lax.axis_index("col")

    heads = {}
    for n, (flip, head, end) in enumerate(spans):
        for inside in range(head, end):
            heads[flip, inside] = sum(e - h for _, h, e in spans[:n]) + inside - head
    for owner in range(key.shape[0] // per_owner):
        base = jnp.where((owner & 1) == (own & 1), blocks // 2, 0)
        flipped = (owner >> 1) != (own >> 1)
        for inside in range(per_owner):
            name = [base + heads[f, inside] if (f, inside) in heads else blocks for f in (0, 1)]
            key[owner * per_owner + inside] = jnp.where(flipped, name[1], name[0])
    base = [n * (blocks * stride + cuts[1]) for n in range(PARTS + 1)]
    for n in range(PARTS):
        for k in range(blocks + 1):
            fill[n][k] = base[n] + k * stride
    place_load.wait()
    live = counts[0, 0]
    unroll = math.gcd(cuts[1], 6)

    def put(g, carry):
        for i in range(unroll):
            mine = [cut + g * unroll + i for cut in cuts[:-1]]
            if slots % PARTS:
                mine = [jnp.minimum(t, slots - 1) for t in mine]
            names = [key[place_of[0, t]] for t in mine]
            lists = [
                jnp.where(cut + g * unroll + i < live, name, blocks)
                for cut, name in zip(cuts, names)
            ]
            spots = [fill[n][k] for n, k in enumerate(lists)]
            for n in range(PARTS):
                fill[n][lists[n]] = spots[n] + 1
                entry[spots[n]] = mine[n]
        return carry

    lax.fori_loop(0, (jnp.minimum(live, cuts[1]) + unroll - 1) // unroll, put, 0)

    for i in range(PAIR):
        entry[base[-1] + i] = slots
    number, bounds = 0, [0]
    for n in range(PARTS):
        for k in range(blocks):
            head = base[n] + k * stride
            end = fill[n][k]
            for i in range(PAIR - 1):
                entry[end + i] = slots

            def add_pair(j, at, head=head, k=k):
                first_of[at + j] = head + j * PAIR
                key_of[at + j] = k
                return at

            pairs = (end - head + PAIR - 1) // PAIR
            lax.fori_loop(0, pairs, add_pair, number)
            number += pairs
        bounds.append(number // TURN)
    for i in range(TURN - 1):
        first_of[number + i] = base[-1]
        key_of[number + i] = 0
    bounds[-1] = (number + TURN - 1) // TURN
    acc[...] = jnp.zeros_like(acc)
    tile_buf[slots] = jnp.zeros_like(tile_buf[slots])
    for load in panel_loads:
        load.wait()

    def turn(g, carry):
        firsts = [first_of[g * TURN + i] for i in range(TURN)]
        slot = [[entry[at + j] for j in range(PAIR)] for at in firsts]
        column = [[place_of[1, jnp.minimum(t, slots - 1)] for t in pair] for pair in slot]
        if not resident:
            copies = [
                pltpu.make_async_copy(
                    panels.at[column[i][j]],
                    panel_buf.at[i * PAIR + j],
                    panel_sem.at[i * PAIR + j],
                )
                for i in range(TURN)
                for j in range(PAIR)
            ]
            for copy in copies:
                copy.start()
            for copy in copies:
                copy.wait()
        for i in range(TURN):
            left = jnp.concatenate([tile_buf[slot[i][j]] for j in range(PAIR)], axis=1)
            right = jnp.concatenate(
                [panel_buf[column[i][j] if resident else i * PAIR + j] for j in range(PAIR)],
                axis=0,
            )
            acc[key_of[g * TURN + i]] += jnp.dot(left, right, preferred_element_type=F32)
        return carry

    for n, load in enumerate(tile_loads):
        load.wait()
        lax.fori_loop(bounds[n], bounds[n + 1], turn, 0)
    first = 0
    for out in outs:
        out[...] = acc[first : first + out.shape[0]]
        first += out.shape[0]


def tile_products(counts, places, tiles, panels, tile_rows, spans):
    slots, size, _ = tiles.shape
    width = panels.shape[2]
    sizes = [end - head for _, head, end in spans] * 2
    blocks = sum(sizes)
    part = -(-slots // PARTS)
    stride = (min(part, panels.shape[0]) // PAIR + 1) * PAIR
    pairs = PARTS * blocks * stride // PAIR + TURN
    resident = panels.size * 2 <= 16 << 20
    panel_shape = (panels.shape[0] if resident else PAIR * TURN, size, width)
    return pl.pallas_call(
        functools.partial(tile_kernel, resident, spans, stride),
        out_shape=[jax.ShapeDtypeStruct((n, size, width), F32) for n in sizes],
        in_specs=[SMEM, HBM, HBM, HBM],
        out_specs=[VMEM] * len(sizes),
        scratch_shapes=[
            pltpu.VMEM((slots + 1, size, size), BF16),
            pltpu.VMEM(panel_shape, BF16),
            pltpu.SMEM((2, slots), jnp.int32),
            pltpu.SMEM((tile_rows,), jnp.int32),
            pltpu.SMEM((pairs,), jnp.int32),
            pltpu.SMEM((pairs,), jnp.int32),
            pltpu.VMEM((blocks, size, width), F32),
            pltpu.SemaphoreType.DMA((1 + PARTS,)),
            pltpu.SemaphoreType.DMA((1 if resident else PAIR * TURN,)),
        ]
        + [pltpu.SMEM((blocks + 1,), jnp.int32)] * PARTS
        + [pltpu.SMEM((PARTS * (blocks * stride + part) + PAIR,), jnp.int32)],
        compiler_params=params(50 << 20),
    )(counts, in_hbm(places), tiles, panels)


def gram_rows(order):
    under = [(i, j) for i in range(order) for j in range(i)]
    heads = {block: n * BLOCK for n, block in enumerate(under)}
    first = len(under) * BLOCK
    pairs = []
    for i in range(0, order, 2):
        pairs.append((i, i + 1, first, 0))
        first += BLOCK
    pairs = [(i, j, head, first + n) for n, (i, j, head, _) in enumerate(pairs)]
    return heads, pairs, first, -(-(first + len(pairs)) // 64) * 64


def square_index():
    return (
        lax.broadcasted_iota(jnp.int32, (BLOCK, BLOCK), 0),
        lax.broadcasted_iota(jnp.int32, (BLOCK, BLOCK), 1),
    )


def gram_kernel(last, *refs):
    if last:
        keep, core, across, *earlier, rows, own, send, acc = refs
    else:
        keep, core, across, rows, acc = refs
    total = (keep[...] + core[...]) + across[...]
    total = total.reshape(rows.shape)
    rows[...] = total
    high, low = halves(total)
    left = jnp.concatenate([high, high, low], axis=0)
    right = jnp.concatenate([high, low, high], axis=0)
    order = rows.shape[1] // BLOCK
    heads, pairs, slab, number = gram_rows(order)
    diagonal = {}
    for i in range(order):
        strip = lax.dot_general(
            left[:, i * BLOCK : (i + 1) * BLOCK],
            right[:, : (i + 1) * BLOCK],
            (((0,), (0,)), ((), ())),
            preferred_element_type=F32,
        )
        for j in range(i):
            acc[pl.ds(heads[i, j], BLOCK)] = strip[:, j * BLOCK : (j + 1) * BLOCK]
        diagonal[i] = strip[:, i * BLOCK :]
    acc[pl.ds(slab, number - slab)] = jnp.zeros((number - slab, BLOCK), F32)
    r, c = square_index()
    for i, j, head, line in pairs:
        acc[pl.ds(head, BLOCK)] = jnp.where(r >= c, diagonal[i], diagonal[j])
        acc[pl.ds(line, 1)] = jnp.sum(jnp.where(r == c, diagonal[j], 0.0), axis=0, keepdims=True)
    if last:
        for gram in earlier:
            acc[...] += gram[...]
    if last:
        core_bit, me = place()
        size = own.shape[1]
        half = acc.shape[0] // 2
        for d in range(own.shape[0]):
            at = (me ^ d) * size
            own[d] = acc[pl.ds(pl.multiple_of(core_bit * half + at, 8), size)]
            send[d] = acc[pl.ds(pl.multiple_of((1 - core_bit) * half + at, 8), size)]


def place():
    row, col = lax.axis_index("row"), lax.axis_index("col")
    return col & 1, (row & 1) | (col & 2)


def gram_chunk(keep, core, across, earlier, last):
    width = keep.shape[2]
    rows = keep.shape[0] * keep.shape[1]
    number = gram_rows(width // BLOCK)[3]
    whole = jax.ShapeDtypeStruct((number, BLOCK), F32)
    pieces = jax.ShapeDtypeStruct((4, number // 8, BLOCK), F32)
    row_shape = jax.ShapeDtypeStruct((rows, width), F32)
    args = [keep, core, across] + (list(earlier) if last else [])
    outs = [row_shape] + ([pieces, pieces] if last else [whole])
    return pl.pallas_call(
        functools.partial(gram_kernel, last),
        out_shape=outs,
        in_specs=[VMEM] * len(args),
        out_specs=[VMEM] * len(outs),
        scratch_shapes=[pltpu.VMEM(whole.shape, F32)] if last else [],
        compiler_params=params(16 << 20),
    )(*args)


def swapped(x, row_flip, col_flip):
    rows, cols = lax.axis_size("row"), lax.axis_size("col")
    if not row_flip:
        return lax.ppermute(x, "col", [(c, c ^ col_flip) for c in range(cols)])
    if not col_flip:
        return lax.ppermute(x, "row", [(r, r ^ row_flip) for r in range(rows)])
    route = [
        (r * cols + c, (r ^ row_flip) * cols + (c ^ col_flip))
        for r in range(rows)
        for c in range(cols)
    ]
    return lax.ppermute(x, ("row", "col"), route)


FLIPS = ((1, 0), (0, 2), (1, 2))


def gram_sum(own, send):
    theirs = swapped(send, 0, 1)
    part = [own[d] + theirs[d] for d in range(4)]
    got = [swapped(x, *flip) for x, flip in zip(part[1:], FLIPS)]
    piece = (part[0] + got[0]) + (got[1] + got[2])
    bits = lax.axis_size("row").bit_length() - 1
    bit = 1
    while bit < bits:
        if bit + 1 < bits:
            a, b = 1 << bit, 2 << bit
            got = [swapped(piece, flip, 0) for flip in (a, b, a | b)]
            piece = (piece + got[0]) + (got[1] + got[2])
            bit += 2
        else:
            piece = piece + swapped(piece, 1 << bit, 0)
            bit += 1
    mine = [piece] + [swapped(piece, *flip) for flip in FLIPS]
    return mine, [swapped(x, 0, 1) for x in mine]


def against(left, right_rows):
    lh, ll = left
    rh, rl = right_rows
    return lax.dot_general(
        jnp.concatenate([lh, lh, ll], axis=1),
        jnp.concatenate([rh, rl, rh], axis=1),
        (((1,), (1,)), ((), ())),
        preferred_element_type=F32,
    )


def times(left, right):
    lh, ll = left
    rh, rl = right
    return jnp.dot(
        jnp.concatenate([lh, lh, ll], axis=1),
        jnp.concatenate([rh, rl, rh], axis=0),
        preferred_element_type=F32,
    )


def factor_kernel(chunks, scale, rounds, *refs):
    pieces, rows = refs[:8], refs[8 : 8 + chunks]
    basis_out, triangle_out = refs[8 + chunks : 10 + chunks]
    blocks, gram, half_mask, half_eye, w, basis, triangle, out_sem = refs[10 + chunks : 18 + chunks]
    wb, gh, gl, yh, yl, ph, dh, dl = refs[18 + chunks :]
    size = gram.shape[0]
    order = size // BLOCK
    core_bit, me = place()
    half = blocks.shape[0] // 2
    for n, piece in enumerate(pieces):
        at = (core_bit ^ (n // 4)) * half + (me ^ (n % 4)) * piece.shape[0]
        blocks[pl.ds(pl.multiple_of(at, 8), piece.shape[0])] = piece[...]
    at = [slice(i * BLOCK, (i + 1) * BLOCK) for i in range(order)]

    r, c = square_index()
    row_scale, col_scale = [], []
    heads, pairs, _, _ = gram_rows(order)
    lower = {}
    for i, j, head, line in pairs:
        packed = blocks[pl.ds(head, BLOCK)]
        turned = packed.T
        lower[i, i] = jnp.where(r >= c, packed, turned)
        lower[j, j] = jnp.where(
            r < c, packed, jnp.where(r == c, blocks[pl.ds(line, 1)], turned)
        )
    for i in range(order):
        diagonal = jnp.where(r == c, lower[i, i], 0.0)
        row_scale.append(lax.rsqrt(jnp.sum(diagonal, axis=1, keepdims=True)))
        col_scale.append(lax.rsqrt(jnp.sum(diagonal, axis=0, keepdims=True)))
    for i, j in [(i, j) for i in range(order) for j in range(i + 1)]:
        block = lower[i, i] if i == j else blocks[pl.ds(heads[i, j], BLOCK)]
        first = -(block * row_scale[i] * col_scale[j])
        if i == j:
            first = jnp.where(r > c, first, jnp.where(r == c, 1.0, 0.0))
        wb[at[i], at[j]] = (first * col_scale[j]).astype(BF16)
        for p, q, x in [(i, j, block)] + ([(j, i, block.T)] if i != j else []):
            gram[at[p], at[q]] = x
            gh[at[p], at[q]], gl[at[p], at[q]] = halves(x)
        if i != j:
            wb[at[j], at[i]] = jnp.zeros((BLOCK, BLOCK), BF16)

    wide = size // 2
    top, low = slice(0, wide), slice(wide, size)
    r = lax.broadcasted_iota(jnp.int32, (wide, wide), 0)
    c = lax.broadcasted_iota(jnp.int32, (wide, wide), 1)
    half_mask[...] = jnp.where(r > c, 1.0, jnp.where(r == c, 0.5, 0.0))
    half_eye[...] = jnp.where(r == c, 0.5, 0.0)
    ph[top, low] = jnp.zeros((wide, wide), BF16)

    def dot(left, right):
        return jnp.dot(left, right, preferred_element_type=F32)

    def dot_rows(left, right):
        return lax.dot_general(left, right, (((1,), (1,)), ((), ())), preferred_element_type=F32)

    def twice(x, axis=1):
        return jnp.concatenate([x, x], axis=axis)

    def both(x, y, axis=1):
        return jnp.concatenate([x, y], axis=axis)

    def step(exact):
        for cols, k in ((top, wide), (low, size)):
            if exact:
                y = dot_rows(both(gh[:, :k], gl[:, :k]), twice(wb[cols, :k]))
                yh[:, cols], yl[:, cols] = halves(y)
            else:
                yh[:, cols] = dot_rows(gh[:, :k], wb[cols, :k]).astype(BF16)
        norm = jnp.zeros((1, 1), F32)
        strips = []
        for part, k in ((top, wide), (low, size)):
            if exact:
                m = dot(twice(wb[part, :k]), both(yh[:k, :k], yl[:k, :k], 0))
            else:
                m = dot(wb[part, :k], yh[:k, :k])
            corner = m[:, k - wide :] * half_mask[...] - half_eye[...]
            p = corner if k == wide else both(m[:, :wide], corner)
            ph[part, :k] = p.astype(BF16)
            strips.append(p)
            if exact:
                norm = norm + jnp.sum(p * p, keepdims=True)
        for p, part, k in zip(strips, (top, low), (wide, size)):
            corner = dot_rows(ph[part, :k], ph[part, :k]) * half_mask[...]
            corner = p[:, k - wide :] - dot(ph[part, part], ph[part, part]) - corner
            dh[part, part] = corner.astype(BF16)
            if k == size:
                side = dot(ph[low, :], ph[:, top]) + dot_rows(ph[low, top], ph[top, top])
                dh[low, top] = (p[:, :wide] - side).astype(BF16)
        for part in (top, low):
            w[part, part] = wb[part, part].astype(F32) - dot(dh[part, part], wb[part, part])
        w[low, top] = wb[low, top].astype(F32) - dot(dh[low, :], wb[:, top])
        return jnp.sum(norm)

    def rounded():
        for part, k in ((top, wide), (low, size)):
            wb[part, :k] = w[part, :k].astype(BF16)

    step(False)

    def not_done(state):
        count, norm = state
        return jnp.logical_and(count < rounds, jnp.logical_not(norm < SMALL))

    def again(state):
        rounded()
        return state[0] + 1, step(True)

    _, norm = lax.while_loop(not_done, again, (jnp.int32(0), jnp.float32(1.0)))
    found = norm < SMALL

    @pl.when(found)
    def _():
        for part, k in ((top, wide), (low, size)):
            wb[part, :k], dl[part, :k] = halves(w[part, :k])
        copies = []

        def send(source, target):
            copies.append(pltpu.make_async_copy(source, target, out_sem.at[len(copies)]))
            copies[-1].start()

        own_rows = jnp.concatenate([part[...] for part in rows], axis=0)
        count = own_rows.shape[0] // 2
        for n in range(2):
            here = pl.ds(n * count, count)
            sh, sl = halves(own_rows[n * count : (n + 1) * count])
            for cols, k in ((low, size), (top, wide)):
                out = against((sh[:, :k], sl[:, :k]), (wb[cols, :k], dl[cols, :k]))
                basis[here, cols] = out * scale
                send(basis.at[here, cols], basis_out.at[here, cols])
            if n == 1:
                for part, k in ((top, wide), (low, size)):
                    upper = times(
                        (wb[part, :k], dl[part, :k]), (gh[:k, k - wide :], gl[:k, k - wide :])
                    )
                    corner = jnp.where(r <= c, upper[:, :wide], 0.0)
                    upper = both(corner, upper[:, wide:]) if k == wide else corner
                    triangle[part, k - wide :] = upper * (1.0 / scale)
                triangle[low, top] = jnp.zeros((wide, wide), F32)
                send(triangle, triangle_out)
        for copy in copies:
            copy.wait()

    @pl.when(jnp.logical_not(found))
    def _():
        eliminate(gram, triangle, w)
        triangle[...] = triangle[...] * (1.0 / scale)
        first = 0
        for part in rows:

            def strip(n, carry, part=part, first=first):
                at = pl.ds(pl.multiple_of(n * BLOCK, BLOCK), BLOCK)
                out = exact_dot(part[at, :], w[...], (((1,), (1,)), ((), ())))
                here = pl.multiple_of(first + n * BLOCK, BLOCK)
                basis[pl.ds(here, BLOCK), :] = out * scale
                return carry

            lax.fori_loop(0, part.shape[0] // BLOCK, strip, 0)
            first += part.shape[0]
        copies = [
            pltpu.make_async_copy(triangle, triangle_out, out_sem.at[0]),
            pltpu.make_async_copy(basis, basis_out, out_sem.at[1]),
        ]
        for copy in copies:
            copy.start()
        for copy in copies:
            copy.wait()


def exact_dot(left, right, dims):
    return lax.dot_general(
        left, right, dims, precision=lax.Precision.HIGHEST, preferred_element_type=F32
    )


def eliminate(gram, upper, inverse):
    size = gram.shape[0]
    columns = lax.broadcasted_iota(jnp.int32, (BLOCK, size), 1)
    lines = lax.broadcasted_iota(jnp.int32, (BLOCK, size), 0)
    r, c = square_index()
    line = r[:, :1]
    for n in range(size // BLOCK):
        here = slice(n * BLOCK, (n + 1) * BLOCK)
        left = gram[here, :]
        right = jnp.where(columns == lines + n * BLOCK, 1.0, 0.0)
        if n:
            above = upper[: n * BLOCK, here]
            over = (((0,), (0,)), ((), ()))
            left = left - exact_dot(above, upper[: n * BLOCK, :], over)
            right = right - exact_dot(above, inverse[: n * BLOCK, :], over)
        upper[here, :] = left
        inverse[here, :] = right

        def row(j, carry, n=n, here=here):
            at = pl.ds(n * BLOCK + j, 1)
            corner = upper[here, here]
            column = jnp.sum(jnp.where(c == j, corner, 0.0), axis=1, keepdims=True)
            pivot = jnp.sum(jnp.where(line == j, column, 0.0), axis=0, keepdims=True)
            root = lax.rsqrt(pivot)
            left = upper[at, :] * root
            right = inverse[at, :] * root
            factor_of = jnp.where(line > j, column * root, 0.0)
            upper[here, :] = upper[here, :] - factor_of * left
            inverse[here, :] = inverse[here, :] - factor_of * right
            upper[at, :] = left
            inverse[at, :] = right
            return carry

        lax.fori_loop(0, BLOCK, row, 0)
        upper[here, :] = jnp.where(columns >= lines + n * BLOCK, upper[here, :], 0.0)


def factor(pieces, rows, scale):
    width = rows[0].shape[1]
    square = (width, width)
    local = sum(part.shape[0] for part in rows)
    number = gram_rows(width // BLOCK)[3]
    return pl.pallas_call(
        functools.partial(factor_kernel, len(rows), scale, 6),
        out_shape=[
            pltpu.HBM((local, width), F32),
            pltpu.HBM(square, F32),
        ],
        in_specs=[VMEM] * (8 + len(rows)),
        out_specs=[HBM, HBM],
        scratch_shapes=[
            pltpu.VMEM((number, BLOCK), F32),
            pltpu.VMEM(square, F32),
            pltpu.VMEM((width // 2, width // 2), F32),
            pltpu.VMEM((width // 2, width // 2), F32),
            pltpu.VMEM(square, F32),
            pltpu.VMEM((local, width), F32),
            pltpu.VMEM(square, F32),
            pltpu.SemaphoreType.DMA((5,)),
        ]
        + [pltpu.VMEM(square, BF16)] * 8,
        compiler_params=params(24 << 20),
    )(*pieces, *rows)


def body(tile_values, tile_places, tile_counts, sketch):
    tiles = tile_values[0, 0]
    size = tiles.shape[1]
    width = sketch.shape[1]
    row_devices = lax.axis_size("row")
    col_devices = lax.axis_size("col")
    local_rows = sketch.shape[0] // row_devices
    tile_rows = local_rows * col_devices // size
    panels = sketch.reshape(-1, size, width)
    places = tile_places[0, 0]
    scale = math.sqrt(local_rows * row_devices * col_devices)
    per_owner = tile_rows // col_devices
    cuts = sorted({0, per_owner // 6, per_owner * 5 // 6, per_owner})
    chunks = list(zip(cuts, cuts[1:]))
    early = chunks[:-1] or chunks
    late = chunks[len(early) :]

    def products(spans):
        out = tile_products(tile_counts, places, tiles, panels, tile_rows, tuple(spans))
        return out[: len(spans)], out[len(spans) :]

    def across_cores(send, keep):
        own = []
        for n in range(len(send)):
            if n == 1:
                *send[1:], core = lax.optimization_barrier((*send[1:], core))
            core = swapped(send[n], 0, 1)
            own.append(keep[n] + core)
        return own

    send, keep = products([(1, head, end) for head, end in early])
    own = across_cores(list(send), keep)
    across = [swapped(x, 0, 2) for x in own]
    places, own = lax.optimization_barrier((places, own))
    send, keep = products([(1, *chunk) for chunk in late] + [(0, *chunk) for chunk in chunks])
    send, keep, across[0] = lax.optimization_barrier((send, keep, across[0]))
    across += [swapped(x, 0, 2) for x in across_cores(list(send[: len(late)]), keep[: len(late)])]
    send, keep = send[len(late) :], keep[len(late) :]
    chunks = len(chunks)
    rows, grams = [], []
    for n in range(chunks):
        out = gram_chunk(keep[n], swapped(send[n], 0, 1), across[n], grams, n == chunks - 1)
        rows.append(out[0])
        grams.append(out[1])
    mine, theirs = gram_sum(*out[1:])
    basis, triangle = factor(mine + theirs, rows, scale)
    return basis, triangle


def solution(mesh):
    in_specs = (
        P("row", "col", None, None, None),
        P("row", "col", None, None),
        P("row", "col"),
        P("col", None),
    )
    out_specs = (P(("row", "col"), None), P())
    return jax.shard_map(body, mesh=mesh, in_specs=in_specs, out_specs=out_specs, check_vma=False)
```

```python
import functools
import math

import jax
import jax.numpy as jnp
from jax import lax
from jax.experimental import pallas as pl
from jax.experimental.pallas import tpu as pltpu
from jax.sharding import PartitionSpec as P

BF16 = jnp.bfloat16
F32 = jnp.float32
PAIR = 2
TURN = 20
PARTS = 2
BLOCK = 128
SMALL = 0.01
SMEM = pl.BlockSpec(memory_space=pltpu.SMEM)
VMEM = pl.BlockSpec(memory_space=pltpu.VMEM)
HBM = pl.BlockSpec(memory_space=pltpu.HBM)

def in_hbm(x):
    return pltpu.with_memory_space_constraint(x, pltpu.HBM)


def params(size):
    return pltpu.CompilerParams(vmem_limit_bytes=size)


def halves(x):
    high = x.astype(BF16)
    return high, (x - high.astype(F32)).astype(BF16)


def tile_kernel(resident, spans, stride, counts, places, tiles, panels, *refs):
    outs, refs = refs[: 2 * len(spans)], refs[2 * len(spans) :]
    tile_buf, panel_buf, place_of, key, first_of, key_of, acc, load_sem, panel_sem = refs[:9]
    fill, entry = refs[9:-1], refs[-1]
    slots = tiles.shape[0]
    blocks = acc.shape[0]
    per_owner = key.shape[0] // lax.axis_size("col")
    panel_loads = [pltpu.make_async_copy(panels, panel_buf, panel_sem.at[0])] if resident else []
    cuts = [-(-slots * n // PARTS) for n in range(PARTS + 1)]
    tile_loads = [
        pltpu.make_async_copy(
            tiles.at[pl.ds(a, b - a)], tile_buf.at[pl.ds(a, b - a)], load_sem.at[1 + n]
        )
        for n, (a, b) in enumerate(zip(cuts, cuts[1:]))
    ]
    place_load = pltpu.make_async_copy(places, place_of, load_sem.at[0])
    for load in [place_load] + panel_loads + tile_loads:
        load.start()
    own = lax.axis_index("col")

    heads = {}
    for n, (flip, head, end) in enumerate(spans):
        for inside in range(head, end):
            heads[flip, inside] = sum(e - h for _, h, e in spans[:n]) + inside - head
    for owner in range(key.shape[0] // per_owner):
        base = jnp.where((owner & 1) == (own & 1), blocks // 2, 0)
        flipped = (owner >> 1) != (own >> 1)
        for inside in range(per_owner):
            name = [base + heads[f, inside] if (f, inside) in heads else blocks for f in (0, 1)]
            key[owner * per_owner + inside] = jnp.where(flipped, name[1], name[0])
    base = [n * (blocks * stride + cuts[1]) for n in range(PARTS + 1)]
    for n in range(PARTS):
        for k in range(blocks + 1):
            fill[n][k] = base[n] + k * stride
    place_load.wait()
    live = counts[0, 0]
    unroll = math.gcd(cuts[1], 6)

    def put(g, carry):
        for i in range(unroll):
            mine = [cut + g * unroll + i for cut in cuts[:-1]]
            if slots % PARTS:
                mine = [jnp.minimum(t, slots - 1) for t in mine]
            names = [key[place_of[0, t]] for t in mine]
            lists = [
                jnp.where(cut + g * unroll + i < live, name, blocks)
                for cut, name in zip(cuts, names)
            ]
            spots = [fill[n][k] for n, k in enumerate(lists)]
            for n in range(PARTS):
                fill[n][lists[n]] = spots[n] + 1
                entry[spots[n]] = mine[n]
        return carry

    lax.fori_loop(0, (jnp.minimum(live, cuts[1]) + unroll - 1) // unroll, put, 0)

    for i in range(PAIR):
        entry[base[-1] + i] = slots
    number, bounds = 0, [0]
    for n in range(PARTS):
        for k in range(blocks):
            head = base[n] + k * stride
            end = fill[n][k]
            for i in range(PAIR - 1):
                entry[end + i] = slots

            def add_pair(j, at, head=head, k=k):
                first_of[at + j] = head + j * PAIR
                key_of[at + j] = k
                return at

            pairs = (end - head + PAIR - 1) // PAIR
            lax.fori_loop(0, pairs, add_pair, number)
            number += pairs
        bounds.append(number // TURN)
    for i in range(TURN - 1):
        first_of[number + i] = base[-1]
        key_of[number + i] = 0
    bounds[-1] = (number + TURN - 1) // TURN
    acc[...] = jnp.zeros_like(acc)
    tile_buf[slots] = jnp.zeros_like(tile_buf[slots])
    for load in panel_loads:
        load.wait()

    def turn(g, carry):
        firsts = [first_of[g * TURN + i] for i in range(TURN)]
        slot = [[entry[at + j] for j in range(PAIR)] for at in firsts]
        column = [[place_of[1, jnp.minimum(t, slots - 1)] for t in pair] for pair in slot]
        if not resident:
            copies = [
                pltpu.make_async_copy(
                    panels.at[column[i][j]],
                    panel_buf.at[i * PAIR + j],
                    panel_sem.at[i * PAIR + j],
                )
                for i in range(TURN)
                for j in range(PAIR)
            ]
            for copy in copies:
                copy.start()
            for copy in copies:
                copy.wait()
        for i in range(TURN):
            left = jnp.concatenate([tile_buf[slot[i][j]] for j in range(PAIR)], axis=1)
            right = jnp.concatenate(
                [panel_buf[column[i][j] if resident else i * PAIR + j] for j in range(PAIR)],
                axis=0,
            )
            acc[key_of[g * TURN + i]] += jnp.dot(left, right, preferred_element_type=F32)
        return carry

    for n, load in enumerate(tile_loads):
        load.wait()
        lax.fori_loop(bounds[n], bounds[n + 1], turn, 0)
    first = 0
    for out in outs:
        out[...] = acc[first : first + out.shape[0]]
        first += out.shape[0]


def tile_products(counts, places, tiles, panels, tile_rows, spans):
    slots, size, _ = tiles.shape
    width = panels.shape[2]
    sizes = [end - head for _, head, end in spans] * 2
    blocks = sum(sizes)
    part = -(-slots // PARTS)
    stride = (min(part, panels.shape[0]) // PAIR + 1) * PAIR
    pairs = PARTS * blocks * stride // PAIR + TURN
    resident = panels.size * 2 <= 16 << 20
    panel_shape = (panels.shape[0] if resident else PAIR * TURN, size, width)
    return pl.pallas_call(
        functools.partial(tile_kernel, resident, spans, stride),
        out_shape=[jax.ShapeDtypeStruct((n, size, width), F32) for n in sizes],
        in_specs=[SMEM, HBM, HBM, HBM],
        out_specs=[VMEM] * len(sizes),
        scratch_shapes=[
            pltpu.VMEM((slots + 1, size, size), BF16),
            pltpu.VMEM(panel_shape, BF16),
            pltpu.SMEM((2, slots), jnp.int32),
            pltpu.SMEM((tile_rows,), jnp.int32),
            pltpu.SMEM((pairs,), jnp.int32),
            pltpu.SMEM((pairs,), jnp.int32),
            pltpu.VMEM((blocks, size, width), F32),
            pltpu.SemaphoreType.DMA((1 + PARTS,)),
            pltpu.SemaphoreType.DMA((1 if resident else PAIR * TURN,)),
        ]
        + [pltpu.SMEM((blocks + 1,), jnp.int32)] * PARTS
        + [pltpu.SMEM((PARTS * (blocks * stride + part) + PAIR,), jnp.int32)],
        compiler_params=params(50 << 20),
    )(counts, in_hbm(places), tiles, panels)


def gram_rows(order):
    under = [(i, j) for i in range(order) for j in range(i)]
    heads = {block: n * BLOCK for n, block in enumerate(under)}
    first = len(under) * BLOCK
    pairs = []
    for i in range(0, order, 2):
        pairs.append((i, i + 1, first, 0))
        first += BLOCK
    pairs = [(i, j, head, first + n) for n, (i, j, head, _) in enumerate(pairs)]
    return heads, pairs, first, -(-(first + len(pairs)) // 64) * 64


def square_index():
    return (
        lax.broadcasted_iota(jnp.int32, (BLOCK, BLOCK), 0),
        lax.broadcasted_iota(jnp.int32, (BLOCK, BLOCK), 1),
    )


def gram_kernel(last, *refs):
    if last:
        keep, core, across, *earlier, rows, own, send, acc = refs
    else:
        keep, core, across, rows, acc = refs
    total = (keep[...] + core[...]) + across[...]
    total = total.reshape(rows.shape)
    rows[...] = total
    high, low = halves(total)
    left = jnp.concatenate([high, high, low], axis=0)
    right = jnp.concatenate([high, low, high], axis=0)
    order = rows.shape[1] // BLOCK
    heads, pairs, slab, number = gram_rows(order)
    diagonal = {}
    for i in range(order):
        strip = lax.dot_general(
            left[:, i * BLOCK : (i + 1) * BLOCK],
            right[:, : (i + 1) * BLOCK],
            (((0,), (0,)), ((), ())),
            preferred_element_type=F32,
        )
        for j in range(i):
            acc[pl.ds(heads[i, j], BLOCK)] = strip[:, j * BLOCK : (j + 1) * BLOCK]
        diagonal[i] = strip[:, i * BLOCK :]
    acc[pl.ds(slab, number - slab)] = jnp.zeros((number - slab, BLOCK), F32)
    r, c = square_index()
    for i, j, head, line in pairs:
        acc[pl.ds(head, BLOCK)] = jnp.where(r >= c, diagonal[i], diagonal[j])
        acc[pl.ds(line, 1)] = jnp.sum(jnp.where(r == c, diagonal[j], 0.0), axis=0, keepdims=True)
    if last:
        for gram in earlier:
            acc[...] += gram[...]
    if last:
        core_bit, me = place()
        size = own.shape[1]
        half = acc.shape[0] // 2
        for d in range(own.shape[0]):
            at = (me ^ d) * size
            own[d] = acc[pl.ds(pl.multiple_of(core_bit * half + at, 8), size)]
            send[d] = acc[pl.ds(pl.multiple_of((1 - core_bit) * half + at, 8), size)]


def place():
    row, col = lax.axis_index("row"), lax.axis_index("col")
    return col & 1, (row & 1) | (col & 2)


def gram_chunk(keep, core, across, earlier, last):
    width = keep.shape[2]
    rows = keep.shape[0] * keep.shape[1]
    number = gram_rows(width // BLOCK)[3]
    whole = jax.ShapeDtypeStruct((number, BLOCK), F32)
    pieces = jax.ShapeDtypeStruct((4, number // 8, BLOCK), F32)
    row_shape = jax.ShapeDtypeStruct((rows, width), F32)
    args = [keep, core, across] + (list(earlier) if last else [])
    outs = [row_shape] + ([pieces, pieces] if last else [whole])
    return pl.pallas_call(
        functools.partial(gram_kernel, last),
        out_shape=outs,
        in_specs=[VMEM] * len(args),
        out_specs=[VMEM] * len(outs),
        scratch_shapes=[pltpu.VMEM(whole.shape, F32)] if last else [],
        compiler_params=params(16 << 20),
    )(*args)


def swapped(x, row_flip, col_flip):
    rows, cols = lax.axis_size("row"), lax.axis_size("col")
    if not row_flip:
        return lax.ppermute(x, "col", [(c, c ^ col_flip) for c in range(cols)])
    if not col_flip:
        return lax.ppermute(x, "row", [(r, r ^ row_flip) for r in range(rows)])
    route = [
        (r * cols + c, (r ^ row_flip) * cols + (c ^ col_flip))
        for r in range(rows)
        for c in range(cols)
    ]
    return lax.ppermute(x, ("row", "col"), route)


FLIPS = ((1, 0), (0, 2), (1, 2))


def gram_sum(own, send):
    theirs = swapped(send, 0, 1)
    part = [own[d] + theirs[d] for d in range(4)]
    got = [swapped(x, *flip) for x, flip in zip(part[1:], FLIPS)]
    piece = (part[0] + got[0]) + (got[1] + got[2])
    bits = lax.axis_size("row").bit_length() - 1
    bit = 1
    while bit < bits:
        if bit + 1 < bits:
            a, b = 1 << bit, 2 << bit
            got = [swapped(piece, flip, 0) for flip in (a, b, a | b)]
            piece = (piece + got[0]) + (got[1] + got[2])
            bit += 2
        else:
            piece = piece + swapped(piece, 1 << bit, 0)
            bit += 1
    mine = [piece] + [swapped(piece, *flip) for flip in FLIPS]
    return mine, [swapped(x, 0, 1) for x in mine]


def against(left, right_rows):
    lh, ll = left
    rh, rl = right_rows
    return lax.dot_general(
        jnp.concatenate([lh, lh, ll], axis=1),
        jnp.concatenate([rh, rl, rh], axis=1),
        (((1,), (1,)), ((), ())),
        preferred_element_type=F32,
    )


def times(left, right):
    lh, ll = left
    rh, rl = right
    return jnp.dot(
        jnp.concatenate([lh, lh, ll], axis=1),
        jnp.concatenate([rh, rl, rh], axis=0),
        preferred_element_type=F32,
    )


def factor_kernel(chunks, scale, rounds, *refs):
    pieces, rows = refs[:8], refs[8 : 8 + chunks]
    basis_out, triangle_out = refs[8 + chunks : 10 + chunks]
    blocks, gram, half_mask, half_eye, w, basis, triangle, out_sem = refs[10 + chunks : 18 + chunks]
    wb, gh, gl, yh, yl, ph, dh, dl = refs[18 + chunks :]
    size = gram.shape[0]
    order = size // BLOCK
    core_bit, me = place()
    half = blocks.shape[0] // 2
    for n, piece in enumerate(pieces):
        at = (core_bit ^ (n // 4)) * half + (me ^ (n % 4)) * piece.shape[0]
        blocks[pl.ds(pl.multiple_of(at, 8), piece.shape[0])] = piece[...]
    at = [slice(i * BLOCK, (i + 1) * BLOCK) for i in range(order)]

    r, c = square_index()
    row_scale, col_scale = [], []
    heads, pairs, _, _ = gram_rows(order)
    lower = {}
    for i, j, head, line in pairs:
        packed = blocks[pl.ds(head, BLOCK)]
        turned = packed.T
        lower[i, i] = jnp.where(r >= c, packed, turned)
        lower[j, j] = jnp.where(
            r < c, packed, jnp.where(r == c, blocks[pl.ds(line, 1)], turned)
        )
    for i in range(order):
        diagonal = jnp.where(r == c, lower[i, i], 0.0)
        row_scale.append(lax.rsqrt(jnp.sum(diagonal, axis=1, keepdims=True)))
        col_scale.append(lax.rsqrt(jnp.sum(diagonal, axis=0, keepdims=True)))
    for i, j in [(i, j) for i in range(order) for j in range(i + 1)]:
        block = lower[i, i] if i == j else blocks[pl.ds(heads[i, j], BLOCK)]
        first = -(block * row_scale[i] * col_scale[j])
        if i == j:
            first = jnp.where(r > c, first, jnp.where(r == c, 1.0, 0.0))
        wb[at[i], at[j]] = (first * col_scale[j]).astype(BF16)
        for p, q, x in [(i, j, block)] + ([(j, i, block.T)] if i != j else []):
            gram[at[p], at[q]] = x
            gh[at[p], at[q]], gl[at[p], at[q]] = halves(x)
        if i != j:
            wb[at[j], at[i]] = jnp.zeros((BLOCK, BLOCK), BF16)

    wide = size // 2
    top, low = slice(0, wide), slice(wide, size)
    r = lax.broadcasted_iota(jnp.int32, (wide, wide), 0)
    c = lax.broadcasted_iota(jnp.int32, (wide, wide), 1)
    half_mask[...] = jnp.where(r > c, 1.0, jnp.where(r == c, 0.5, 0.0))
    half_eye[...] = jnp.where(r == c, 0.5, 0.0)
    ph[top, low] = jnp.zeros((wide, wide), BF16)

    def dot(left, right):
        return jnp.dot(left, right, preferred_element_type=F32)

    def dot_rows(left, right):
        return lax.dot_general(left, right, (((1,), (1,)), ((), ())), preferred_element_type=F32)

    def twice(x, axis=1):
        return jnp.concatenate([x, x], axis=axis)

    def both(x, y, axis=1):
        return jnp.concatenate([x, y], axis=axis)

    def step(exact):
        for cols, k in ((top, wide), (low, size)):
            if exact:
                y = dot_rows(both(gh[:, :k], gl[:, :k]), twice(wb[cols, :k]))
                yh[:, cols], yl[:, cols] = halves(y)
            else:
                yh[:, cols] = dot_rows(gh[:, :k], wb[cols, :k]).astype(BF16)
        norm = jnp.zeros((1, 1), F32)
        strips = []
        for part, k in ((top, wide), (low, size)):
            if exact:
                m = dot(twice(wb[part, :k]), both(yh[:k, :k], yl[:k, :k], 0))
            else:
                m = dot(wb[part, :k], yh[:k, :k])
            corner = m[:, k - wide :] * half_mask[...] - half_eye[...]
            p = corner if k == wide else both(m[:, :wide], corner)
            ph[part, :k] = p.astype(BF16)
            strips.append(p)
            if exact:
                norm = norm + jnp.sum(p * p, keepdims=True)
        for p, part, k in zip(strips, (top, low), (wide, size)):
            corner = p[:, k - wide :] - dot(ph[part, part], ph[part, part])
            if exact:
                corner = corner - dot_rows(ph[part, :k], ph[part, :k]) * half_mask[...]
            dh[part, part] = corner.astype(BF16)
            if k == size:
                side = dot(ph[low, :], ph[:, top])
                if exact:
                    side = side + dot_rows(ph[low, top], ph[top, top])
                dh[low, top] = (p[:, :wide] - side).astype(BF16)
        for part in (top, low):
            w[part, part] = wb[part, part].astype(F32) - dot(dh[part, part], wb[part, part])
        w[low, top] = wb[low, top].astype(F32) - dot(dh[low, :], wb[:, top])
        return jnp.sum(norm)

    def rounded():
        for part, k in ((top, wide), (low, size)):
            wb[part, :k] = w[part, :k].astype(BF16)

    step(False)

    def not_done(state):
        count, norm = state
        return jnp.logical_and(count < rounds, jnp.logical_not(norm < SMALL))

    def again(state):
        rounded()
        return state[0] + 1, step(True)

    _, norm = lax.while_loop(not_done, again, (jnp.int32(0), jnp.float32(1.0)))
    found = norm < SMALL

    @pl.when(found)
    def _():
        for part, k in ((top, wide), (low, size)):
            wb[part, :k], dl[part, :k] = halves(w[part, :k])
        copies = []

        def send(source, target):
            copies.append(pltpu.make_async_copy(source, target, out_sem.at[len(copies)]))
            copies[-1].start()

        own_rows = jnp.concatenate([part[...] for part in rows], axis=0)
        count = own_rows.shape[0] // 2
        for n in range(2):
            here = pl.ds(n * count, count)
            sh, sl = halves(own_rows[n * count : (n + 1) * count])
            for cols, k in ((low, size), (top, wide)):
                out = against((sh[:, :k], sl[:, :k]), (wb[cols, :k], dl[cols, :k]))
                basis[here, cols] = out * scale
                send(basis.at[here, cols], basis_out.at[here, cols])
            if n == 1:
                for part, k in ((top, wide), (low, size)):
                    upper = times(
                        (wb[part, :k], dl[part, :k]), (gh[:k, k - wide :], gl[:k, k - wide :])
                    )
                    corner = jnp.where(r <= c, upper[:, :wide], 0.0)
                    upper = both(corner, upper[:, wide:]) if k == wide else corner
                    triangle[part, k - wide :] = upper * (1.0 / scale)
                triangle[low, top] = jnp.zeros((wide, wide), F32)
                send(triangle, triangle_out)
        for copy in copies:
            copy.wait()

    @pl.when(jnp.logical_not(found))
    def _():
        eliminate(gram, triangle, w)
        triangle[...] = triangle[...] * (1.0 / scale)
        first = 0
        for part in rows:

            def strip(n, carry, part=part, first=first):
                at = pl.ds(pl.multiple_of(n * BLOCK, BLOCK), BLOCK)
                out = exact_dot(part[at, :], w[...], (((1,), (1,)), ((), ())))
                here = pl.multiple_of(first + n * BLOCK, BLOCK)
                basis[pl.ds(here, BLOCK), :] = out * scale
                return carry

            lax.fori_loop(0, part.shape[0] // BLOCK, strip, 0)
            first += part.shape[0]
        copies = [
            pltpu.make_async_copy(triangle, triangle_out, out_sem.at[0]),
            pltpu.make_async_copy(basis, basis_out, out_sem.at[1]),
        ]
        for copy in copies:
            copy.start()
        for copy in copies:
            copy.wait()


def exact_dot(left, right, dims):
    return lax.dot_general(
        left, right, dims, precision=lax.Precision.HIGHEST, preferred_element_type=F32
    )


def eliminate(gram, upper, inverse):
    size = gram.shape[0]
    columns = lax.broadcasted_iota(jnp.int32, (BLOCK, size), 1)
    lines = lax.broadcasted_iota(jnp.int32, (BLOCK, size), 0)
    r, c = square_index()
    line = r[:, :1]
    for n in range(size // BLOCK):
        here = slice(n * BLOCK, (n + 1) * BLOCK)
        left = gram[here, :]
        right = jnp.where(columns == lines + n * BLOCK, 1.0, 0.0)
        if n:
            above = upper[: n * BLOCK, here]
            over = (((0,), (0,)), ((), ()))
            left = left - exact_dot(above, upper[: n * BLOCK, :], over)
            right = right - exact_dot(above, inverse[: n * BLOCK, :], over)
        upper[here, :] = left
        inverse[here, :] = right

        def row(j, carry, n=n, here=here):
            at = pl.ds(n * BLOCK + j, 1)
            corner = upper[here, here]
            column = jnp.sum(jnp.where(c == j, corner, 0.0), axis=1, keepdims=True)
            pivot = jnp.sum(jnp.where(line == j, column, 0.0), axis=0, keepdims=True)
            root = lax.rsqrt(pivot)
            left = upper[at, :] * root
            right = inverse[at, :] * root
            factor_of = jnp.where(line > j, column * root, 0.0)
            upper[here, :] = upper[here, :] - factor_of * left
            inverse[here, :] = inverse[here, :] - factor_of * right
            upper[at, :] = left
            inverse[at, :] = right
            return carry

        lax.fori_loop(0, BLOCK, row, 0)
        upper[here, :] = jnp.where(columns >= lines + n * BLOCK, upper[here, :], 0.0)


def factor(pieces, rows, scale):
    width = rows[0].shape[1]
    square = (width, width)
    local = sum(part.shape[0] for part in rows)
    number = gram_rows(width // BLOCK)[3]
    return pl.pallas_call(
        functools.partial(factor_kernel, len(rows), scale, 6),
        out_shape=[
            pltpu.HBM((local, width), F32),
            pltpu.HBM(square, F32),
        ],
        in_specs=[VMEM] * (8 + len(rows)),
        out_specs=[HBM, HBM],
        scratch_shapes=[
            pltpu.VMEM((number, BLOCK), F32),
            pltpu.VMEM(square, F32),
            pltpu.VMEM((width // 2, width // 2), F32),
            pltpu.VMEM((width // 2, width // 2), F32),
            pltpu.VMEM(square, F32),
            pltpu.VMEM((local, width), F32),
            pltpu.VMEM(square, F32),
            pltpu.SemaphoreType.DMA((5,)),
        ]
        + [pltpu.VMEM(square, BF16)] * 8,
        compiler_params=params(24 << 20),
    )(*pieces, *rows)


def body(tile_values, tile_places, tile_counts, sketch):
    tiles = tile_values[0, 0]
    size = tiles.shape[1]
    width = sketch.shape[1]
    row_devices = lax.axis_size("row")
    col_devices = lax.axis_size("col")
    local_rows = sketch.shape[0] // row_devices
    tile_rows = local_rows * col_devices // size
    panels = sketch.reshape(-1, size, width)
    places = tile_places[0, 0]
    scale = math.sqrt(local_rows * row_devices * col_devices)
    per_owner = tile_rows // col_devices
    cuts = sorted({0, per_owner // 6, per_owner * 5 // 6, per_owner})
    chunks = list(zip(cuts, cuts[1:]))
    early = chunks[:-1] or chunks
    late = chunks[len(early) :]

    def products(spans):
        out = tile_products(tile_counts, places, tiles, panels, tile_rows, tuple(spans))
        return out[: len(spans)], out[len(spans) :]

    def across_cores(send, keep):
        own = []
        for n in range(len(send)):
            if n == 1:
                *send[1:], core = lax.optimization_barrier((*send[1:], core))
            core = swapped(send[n], 0, 1)
            own.append(keep[n] + core)
        return own

    send, keep = products([(1, head, end) for head, end in early])
    own = across_cores(list(send), keep)
    across = [swapped(x, 0, 2) for x in own]
    places, own = lax.optimization_barrier((places, own))
    send, keep = products([(1, *chunk) for chunk in late] + [(0, *chunk) for chunk in chunks])
    send, keep, across[0] = lax.optimization_barrier((send, keep, across[0]))
    across += [swapped(x, 0, 2) for x in across_cores(list(send[: len(late)]), keep[: len(late)])]
    send, keep = send[len(late) :], keep[len(late) :]
    chunks = len(chunks)
    rows, grams = [], []
    for n in range(chunks):
        out = gram_chunk(keep[n], swapped(send[n], 0, 1), across[n], grams, n == chunks - 1)
        rows.append(out[0])
        grams.append(out[1])
    mine, theirs = gram_sum(*out[1:])
    basis, triangle = factor(mine + theirs, rows, scale)
    return basis, triangle


def solution(mesh):
    in_specs = (
        P("row", "col", None, None, None),
        P("row", "col", None, None),
        P("row", "col"),
        P("col", None),
    )
    out_specs = (P(("row", "col"), None), P())
    return jax.shard_map(body, mesh=mesh, in_specs=in_specs, out_specs=out_specs, check_vma=False)
```

```python
import functools
import math

import jax
import jax.numpy as jnp
from jax import lax
from jax.experimental import pallas as pl
from jax.experimental.pallas import tpu as pltpu
from jax.sharding import PartitionSpec as P

BF16 = jnp.bfloat16
F32 = jnp.float32
PAIR = 2
TURN = 20
PARTS = 2
BLOCK = 128
SMALL = 0.01
SMEM = pl.BlockSpec(memory_space=pltpu.SMEM)
VMEM = pl.BlockSpec(memory_space=pltpu.VMEM)
HBM = pl.BlockSpec(memory_space=pltpu.HBM)

def in_hbm(x):
    return pltpu.with_memory_space_constraint(x, pltpu.HBM)


def params(size):
    return pltpu.CompilerParams(vmem_limit_bytes=size)


def halves(x):
    high = x.astype(BF16)
    return high, (x - high.astype(F32)).astype(BF16)


def tile_kernel(resident, spans, stride, counts, places, tiles, panels, *refs):
    outs, refs = refs[: 2 * len(spans)], refs[2 * len(spans) :]
    tile_buf, panel_buf, place_of, key, first_of, key_of, acc, load_sem, panel_sem = refs[:9]
    fill, entry = refs[9:-1], refs[-1]
    slots = tiles.shape[0]
    blocks = acc.shape[0]
    per_owner = key.shape[0] // lax.axis_size("col")
    panel_loads = [pltpu.make_async_copy(panels, panel_buf, panel_sem.at[0])] if resident else []
    cuts = [-(-slots * n // PARTS) for n in range(PARTS + 1)]
    tile_loads = [
        pltpu.make_async_copy(
            tiles.at[pl.ds(a, b - a)], tile_buf.at[pl.ds(a, b - a)], load_sem.at[1 + n]
        )
        for n, (a, b) in enumerate(zip(cuts, cuts[1:]))
    ]
    place_load = pltpu.make_async_copy(places, place_of, load_sem.at[0])
    for load in [place_load] + panel_loads + tile_loads:
        load.start()
    own = lax.axis_index("col")

    heads = {}
    for n, (flip, head, end) in enumerate(spans):
        for inside in range(head, end):
            heads[flip, inside] = sum(e - h for _, h, e in spans[:n]) + inside - head
    for owner in range(key.shape[0] // per_owner):
        base = jnp.where((owner & 1) == (own & 1), blocks // 2, 0)
        flipped = (owner >> 1) != (own >> 1)
        for inside in range(per_owner):
            name = [base + heads[f, inside] if (f, inside) in heads else blocks for f in (0, 1)]
            key[owner * per_owner + inside] = jnp.where(flipped, name[1], name[0])
    base = [n * (blocks * stride + cuts[1]) for n in range(PARTS + 1)]
    for n in range(PARTS):
        for k in range(blocks + 1):
            fill[n][k] = base[n] + k * stride
    place_load.wait()
    live = counts[0, 0]
    unroll = math.gcd(cuts[1], 6)

    def put(g, carry):
        for i in range(unroll):
            mine = [cut + g * unroll + i for cut in cuts[:-1]]
            if slots % PARTS:
                mine = [jnp.minimum(t, slots - 1) for t in mine]
            names = [key[place_of[0, t]] for t in mine]
            lists = [
                jnp.where(cut + g * unroll + i < live, name, blocks)
                for cut, name in zip(cuts, names)
            ]
            spots = [fill[n][k] for n, k in enumerate(lists)]
            for n in range(PARTS):
                fill[n][lists[n]] = spots[n] + 1
                entry[spots[n]] = mine[n]
        return carry

    lax.fori_loop(0, (jnp.minimum(live, cuts[1]) + unroll - 1) // unroll, put, 0)

    for i in range(PAIR):
        entry[base[-1] + i] = slots
    number, bounds = 0, [0]
    for n in range(PARTS):
        for k in range(blocks):
            head = base[n] + k * stride
            end = fill[n][k]
            for i in range(PAIR - 1):
                entry[end + i] = slots

            def add_pair(j, at, head=head, k=k):
                first_of[at + j] = head + j * PAIR
                key_of[at + j] = k
                return at

            pairs = (end - head + PAIR - 1) // PAIR
            lax.fori_loop(0, pairs, add_pair, number)
            number += pairs
        bounds.append(number // TURN)
    for i in range(TURN - 1):
        first_of[number + i] = base[-1]
        key_of[number + i] = 0
    bounds[-1] = (number + TURN - 1) // TURN
    acc[...] = jnp.zeros_like(acc)
    tile_buf[slots] = jnp.zeros_like(tile_buf[slots])
    for load in panel_loads:
        load.wait()

    def turn(g, carry):
        firsts = [first_of[g * TURN + i] for i in range(TURN)]
        slot = [[entry[at + j] for j in range(PAIR)] for at in firsts]
        column = [[place_of[1, jnp.minimum(t, slots - 1)] for t in pair] for pair in slot]
        if not resident:
            copies = [
                pltpu.make_async_copy(
                    panels.at[column[i][j]],
                    panel_buf.at[i * PAIR + j],
                    panel_sem.at[i * PAIR + j],
                )
                for i in range(TURN)
                for j in range(PAIR)
            ]
            for copy in copies:
                copy.start()
            for copy in copies:
                copy.wait()
        for i in range(TURN):
            left = jnp.concatenate([tile_buf[slot[i][j]] for j in range(PAIR)], axis=1)
            right = jnp.concatenate(
                [panel_buf[column[i][j] if resident else i * PAIR + j] for j in range(PAIR)],
                axis=0,
            )
            acc[key_of[g * TURN + i]] += jnp.dot(left, right, preferred_element_type=F32)
        return carry

    for n, load in enumerate(tile_loads):
        load.wait()
        lax.fori_loop(bounds[n], bounds[n + 1], turn, 0)
    first = 0
    for out in outs:
        out[...] = acc[first : first + out.shape[0]]
        first += out.shape[0]


def tile_products(counts, places, tiles, panels, tile_rows, spans):
    slots, size, _ = tiles.shape
    width = panels.shape[2]
    sizes = [end - head for _, head, end in spans] * 2
    blocks = sum(sizes)
    part = -(-slots // PARTS)
    stride = (min(part, panels.shape[0]) // PAIR + 1) * PAIR
    pairs = PARTS * blocks * stride // PAIR + TURN
    resident = panels.size * 2 <= 16 << 20
    panel_shape = (panels.shape[0] if resident else PAIR * TURN, size, width)
    return pl.pallas_call(
        functools.partial(tile_kernel, resident, spans, stride),
        out_shape=[jax.ShapeDtypeStruct((n, size, width), F32) for n in sizes],
        in_specs=[SMEM, HBM, HBM, HBM],
        out_specs=[VMEM] * len(sizes),
        scratch_shapes=[
            pltpu.VMEM((slots + 1, size, size), BF16),
            pltpu.VMEM(panel_shape, BF16),
            pltpu.SMEM((2, slots), jnp.int32),
            pltpu.SMEM((tile_rows,), jnp.int32),
            pltpu.SMEM((pairs,), jnp.int32),
            pltpu.SMEM((pairs,), jnp.int32),
            pltpu.VMEM((blocks, size, width), F32),
            pltpu.SemaphoreType.DMA((1 + PARTS,)),
            pltpu.SemaphoreType.DMA((1 if resident else PAIR * TURN,)),
        ]
        + [pltpu.SMEM((blocks + 1,), jnp.int32)] * PARTS
        + [pltpu.SMEM((PARTS * (blocks * stride + part) + PAIR,), jnp.int32)],
        compiler_params=params(50 << 20),
    )(counts, in_hbm(places), tiles, panels)


def gram_rows(order):
    under = [(i, j) for i in range(order) for j in range(i)]
    heads = {block: n * BLOCK for n, block in enumerate(under)}
    first = len(under) * BLOCK
    pairs = []
    for i in range(0, order, 2):
        pairs.append((i, i + 1, first, 0))
        first += BLOCK
    pairs = [(i, j, head, first + n) for n, (i, j, head, _) in enumerate(pairs)]
    return heads, pairs, first, -(-(first + len(pairs)) // 64) * 64


def square_index():
    return (
        lax.broadcasted_iota(jnp.int32, (BLOCK, BLOCK), 0),
        lax.broadcasted_iota(jnp.int32, (BLOCK, BLOCK), 1),
    )


def gram_kernel(last, *refs):
    if last:
        keep, core, across, *earlier, rows, own, send, acc = refs
    else:
        keep, core, across, rows, acc = refs
    total = (keep[...] + core[...]) + across[...]
    total = total.reshape(rows.shape)
    rows[...] = total
    high, low = halves(total)
    left = jnp.concatenate([high, high, low], axis=0)
    right = jnp.concatenate([high, low, high], axis=0)
    order = rows.shape[1] // BLOCK
    heads, pairs, slab, number = gram_rows(order)
    diagonal = {}
    for i in range(order):
        strip = lax.dot_general(
            left[:, i * BLOCK : (i + 1) * BLOCK],
            right[:, : (i + 1) * BLOCK],
            (((0,), (0,)), ((), ())),
            preferred_element_type=F32,
        )
        for j in range(i):
            acc[pl.ds(heads[i, j], BLOCK)] = strip[:, j * BLOCK : (j + 1) * BLOCK]
        diagonal[i] = strip[:, i * BLOCK :]
    acc[pl.ds(slab, number - slab)] = jnp.zeros((number - slab, BLOCK), F32)
    r, c = square_index()
    for i, j, head, line in pairs:
        acc[pl.ds(head, BLOCK)] = jnp.where(r >= c, diagonal[i], diagonal[j])
        acc[pl.ds(line, 1)] = jnp.sum(jnp.where(r == c, diagonal[j], 0.0), axis=0, keepdims=True)
    if last:
        for gram in earlier:
            acc[...] += gram[...]
    if last:
        core_bit, me = place()
        size = own.shape[1]
        half = acc.shape[0] // 2
        for d in range(own.shape[0]):
            at = (me ^ d) * size
            own[d] = acc[pl.ds(pl.multiple_of(core_bit * half + at, 8), size)]
            send[d] = acc[pl.ds(pl.multiple_of((1 - core_bit) * half + at, 8), size)]


def place():
    row, col = lax.axis_index("row"), lax.axis_index("col")
    return col & 1, (row & 1) | (col & 2)


def gram_chunk(keep, core, across, earlier, last):
    width = keep.shape[2]
    rows = keep.shape[0] * keep.shape[1]
    number = gram_rows(width // BLOCK)[3]
    whole = jax.ShapeDtypeStruct((number, BLOCK), F32)
    pieces = jax.ShapeDtypeStruct((4, number // 8, BLOCK), F32)
    row_shape = jax.ShapeDtypeStruct((rows, width), F32)
    args = [keep, core, across] + (list(earlier) if last else [])
    outs = [row_shape] + ([pieces, pieces] if last else [whole])
    return pl.pallas_call(
        functools.partial(gram_kernel, last),
        out_shape=outs,
        in_specs=[VMEM] * len(args),
        out_specs=[VMEM] * len(outs),
        scratch_shapes=[pltpu.VMEM(whole.shape, F32)] if last else [],
        compiler_params=params(16 << 20),
    )(*args)


def swapped(x, row_flip, col_flip):
    rows, cols = lax.axis_size("row"), lax.axis_size("col")
    if not row_flip:
        return lax.ppermute(x, "col", [(c, c ^ col_flip) for c in range(cols)])
    if not col_flip:
        return lax.ppermute(x, "row", [(r, r ^ row_flip) for r in range(rows)])
    route = [
        (r * cols + c, (r ^ row_flip) * cols + (c ^ col_flip))
        for r in range(rows)
        for c in range(cols)
    ]
    return lax.ppermute(x, ("row", "col"), route)


FLIPS = ((1, 0), (0, 2), (1, 2))


def gram_sum(own, send):
    theirs = swapped(send, 0, 1)
    part = [own[d] + theirs[d] for d in range(4)]
    got = [swapped(x, *flip) for x, flip in zip(part[1:], FLIPS)]
    piece = (part[0] + got[0]) + (got[1] + got[2])
    bits = lax.axis_size("row").bit_length() - 1
    bit = 1
    while bit < bits:
        if bit + 1 < bits:
            a, b = 1 << bit, 2 << bit
            got = [swapped(piece, flip, 0) for flip in (a, b, a | b)]
            piece = (piece + got[0]) + (got[1] + got[2])
            bit += 2
        else:
            piece = piece + swapped(piece, 1 << bit, 0)
            bit += 1
    mine = [piece] + [swapped(piece, *flip) for flip in FLIPS]
    return mine, [swapped(x, 0, 1) for x in mine]


def against(left, right_rows):
    lh, ll = left
    rh, rl = right_rows
    return lax.dot_general(
        jnp.concatenate([lh, lh, ll], axis=1),
        jnp.concatenate([rh, rl, rh], axis=1),
        (((1,), (1,)), ((), ())),
        preferred_element_type=F32,
    )


def times(left, right):
    lh, ll = left
    rh, rl = right
    return jnp.dot(
        jnp.concatenate([lh, lh, ll], axis=1),
        jnp.concatenate([rh, rl, rh], axis=0),
        preferred_element_type=F32,
    )


def factor_kernel(chunks, scale, rounds, *refs):
    pieces, rows = refs[:8], refs[8 : 8 + chunks]
    basis_out, triangle_out = refs[8 + chunks : 10 + chunks]
    blocks, gram, half_mask, half_eye, w, basis, triangle, out_sem = refs[10 + chunks : 18 + chunks]
    wb, gh, gl, yh, yl, ph, dh, dl = refs[18 + chunks :]
    size = gram.shape[0]
    order = size // BLOCK
    core_bit, me = place()
    half = blocks.shape[0] // 2
    for n, piece in enumerate(pieces):
        at = (core_bit ^ (n // 4)) * half + (me ^ (n % 4)) * piece.shape[0]
        blocks[pl.ds(pl.multiple_of(at, 8), piece.shape[0])] = piece[...]
    at = [slice(i * BLOCK, (i + 1) * BLOCK) for i in range(order)]

    r, c = square_index()
    row_scale, col_scale = [], []
    heads, pairs, _, _ = gram_rows(order)
    lower = {}
    for i, j, head, line in pairs:
        packed = blocks[pl.ds(head, BLOCK)]
        turned = packed.T
        lower[i, i] = jnp.where(r >= c, packed, turned)
        lower[j, j] = jnp.where(
            r < c, packed, jnp.where(r == c, blocks[pl.ds(line, 1)], turned)
        )
    for i in range(order):
        diagonal = jnp.where(r == c, lower[i, i], 0.0)
        row_scale.append(lax.rsqrt(jnp.sum(diagonal, axis=1, keepdims=True)))
        col_scale.append(lax.rsqrt(jnp.sum(diagonal, axis=0, keepdims=True)))
    for i, j in [(i, j) for i in range(order) for j in range(i + 1)]:
        block = lower[i, i] if i == j else blocks[pl.ds(heads[i, j], BLOCK)]
        first = -(block * row_scale[i] * col_scale[j])
        if i == j:
            first = jnp.where(r > c, first, jnp.where(r == c, 1.0, 0.0))
        wb[at[i], at[j]] = (first * col_scale[j]).astype(BF16)
        for p, q, x in [(i, j, block)] + ([(j, i, block.T)] if i != j else []):
            gram[at[p], at[q]] = x
            gh[at[p], at[q]], gl[at[p], at[q]] = halves(x)
        if i != j:
            wb[at[j], at[i]] = jnp.zeros((BLOCK, BLOCK), BF16)

    wide = size // 2
    top, low = slice(0, wide), slice(wide, size)
    r = lax.broadcasted_iota(jnp.int32, (wide, wide), 0)
    c = lax.broadcasted_iota(jnp.int32, (wide, wide), 1)
    half_mask[...] = jnp.where(r > c, 1.0, jnp.where(r == c, 0.5, 0.0))
    half_eye[...] = jnp.where(r == c, 0.5, 0.0)
    ph[top, low] = jnp.zeros((wide, wide), BF16)

    def dot(left, right):
        return jnp.dot(left, right, preferred_element_type=F32)

    def dot_rows(left, right):
        return lax.dot_general(left, right, (((1,), (1,)), ((), ())), preferred_element_type=F32)

    def twice(x, axis=1):
        return jnp.concatenate([x, x], axis=axis)

    def both(x, y, axis=1):
        return jnp.concatenate([x, y], axis=axis)

    def step(exact):
        for cols, k in ((top, wide), (low, size)):
            if exact:
                y = dot_rows(both(gh[:, :k], gl[:, :k]), twice(wb[cols, :k]))
                yh[:, cols], yl[:, cols] = halves(y)
            else:
                yh[:, cols] = dot_rows(gh[:, :k], wb[cols, :k]).astype(BF16)
        norm = jnp.zeros((1, 1), F32)
        strips = []
        for part, k in ((top, wide), (low, size)):
            if exact:
                m = dot(twice(wb[part, :k]), both(yh[:k, :k], yl[:k, :k], 0))
            else:
                m = dot(wb[part, :k], yh[:k, :k])
            corner = m[:, k - wide :] * half_mask[...] - half_eye[...]
            p = corner if k == wide else both(m[:, :wide], corner)
            ph[part, :k] = p.astype(BF16)
            strips.append(p)
            if exact:
                norm = norm + jnp.sum(p * p, keepdims=True)
        for p, part, k in zip(strips, (top, low), (wide, size)):
            corner = dot_rows(ph[part, :k], ph[part, :k]) * half_mask[...]
            corner = p[:, k - wide :] - dot(ph[part, part], ph[part, part]) - corner
            dh[part, part] = corner.astype(BF16)
            if k == size:
                side = dot(ph[low, :], ph[:, top]) + dot_rows(ph[low, top], ph[top, top])
                dh[low, top] = (p[:, :wide] - side).astype(BF16)
        for part in (top, low):
            w[part, part] = wb[part, part].astype(F32) - dot(dh[part, part], wb[part, part])
        w[low, top] = wb[low, top].astype(F32) - dot(dh[low, :], wb[:, top])
        return jnp.sum(norm)

    def rounded():
        for part, k in ((top, wide), (low, size)):
            wb[part, :k] = w[part, :k].astype(BF16)

    step(False)

    def not_done(state):
        count, norm = state
        return jnp.logical_and(count < rounds, jnp.logical_not(norm < SMALL))

    def again(state):
        rounded()
        return state[0] + 1, step(True)

    _, norm = lax.while_loop(not_done, again, (jnp.int32(0), jnp.float32(1.0)))
    found = norm < SMALL

    @pl.when(found)
    def _():
        for part, k in ((top, wide), (low, size)):
            wb[part, :k], dl[part, :k] = halves(w[part, :k])
        copies = []

        def send(source, target):
            copies.append(pltpu.make_async_copy(source, target, out_sem.at[len(copies)]))
            copies[-1].start()

        own_rows = jnp.concatenate([part[...] for part in rows], axis=0)
        strips = 3 if own_rows.shape[0] % (3 * BLOCK) == 0 else 2
        count = own_rows.shape[0] // strips
        for n in range(strips):
            here = pl.ds(n * count, count)
            sh, sl = halves(own_rows[n * count : (n + 1) * count])
            for cols, k in ((low, size), (top, wide)):
                out = against((sh[:, :k], sl[:, :k]), (wb[cols, :k], dl[cols, :k]))
                basis[here, cols] = out * scale
                send(basis.at[here, cols], basis_out.at[here, cols])
            if n == 1:
                for part, k in ((top, wide), (low, size)):
                    upper = times(
                        (wb[part, :k], dl[part, :k]), (gh[:k, k - wide :], gl[:k, k - wide :])
                    )
                    corner = jnp.where(r <= c, upper[:, :wide], 0.0)
                    upper = both(corner, upper[:, wide:]) if k == wide else corner
                    triangle[part, k - wide :] = upper * (1.0 / scale)
                triangle[low, top] = jnp.zeros((wide, wide), F32)
                send(triangle, triangle_out)
        for copy in copies:
            copy.wait()

    @pl.when(jnp.logical_not(found))
    def _():
        eliminate(gram, triangle, w)
        triangle[...] = triangle[...] * (1.0 / scale)
        first = 0
        for part in rows:

            def strip(n, carry, part=part, first=first):
                at = pl.ds(pl.multiple_of(n * BLOCK, BLOCK), BLOCK)
                out = exact_dot(part[at, :], w[...], (((1,), (1,)), ((), ())))
                here = pl.multiple_of(first + n * BLOCK, BLOCK)
                basis[pl.ds(here, BLOCK), :] = out * scale
                return carry

            lax.fori_loop(0, part.shape[0] // BLOCK, strip, 0)
            first += part.shape[0]
        copies = [
            pltpu.make_async_copy(triangle, triangle_out, out_sem.at[0]),
            pltpu.make_async_copy(basis, basis_out, out_sem.at[1]),
        ]
        for copy in copies:
            copy.start()
        for copy in copies:
            copy.wait()


def exact_dot(left, right, dims):
    return lax.dot_general(
        left, right, dims, precision=lax.Precision.HIGHEST, preferred_element_type=F32
    )


def eliminate(gram, upper, inverse):
    size = gram.shape[0]
    columns = lax.broadcasted_iota(jnp.int32, (BLOCK, size), 1)
    lines = lax.broadcasted_iota(jnp.int32, (BLOCK, size), 0)
    r, c = square_index()
    line = r[:, :1]
    for n in range(size // BLOCK):
        here = slice(n * BLOCK, (n + 1) * BLOCK)
        left = gram[here, :]
        right = jnp.where(columns == lines + n * BLOCK, 1.0, 0.0)
        if n:
            above = upper[: n * BLOCK, here]
            over = (((0,), (0,)), ((), ()))
            left = left - exact_dot(above, upper[: n * BLOCK, :], over)
            right = right - exact_dot(above, inverse[: n * BLOCK, :], over)
        upper[here, :] = left
        inverse[here, :] = right

        def row(j, carry, n=n, here=here):
            at = pl.ds(n * BLOCK + j, 1)
            corner = upper[here, here]
            column = jnp.sum(jnp.where(c == j, corner, 0.0), axis=1, keepdims=True)
            pivot = jnp.sum(jnp.where(line == j, column, 0.0), axis=0, keepdims=True)
            root = lax.rsqrt(pivot)
            left = upper[at, :] * root
            right = inverse[at, :] * root
            factor_of = jnp.where(line > j, column * root, 0.0)
            upper[here, :] = upper[here, :] - factor_of * left
            inverse[here, :] = inverse[here, :] - factor_of * right
            upper[at, :] = left
            inverse[at, :] = right
            return carry

        lax.fori_loop(0, BLOCK, row, 0)
        upper[here, :] = jnp.where(columns >= lines + n * BLOCK, upper[here, :], 0.0)


def factor(pieces, rows, scale):
    width = rows[0].shape[1]
    square = (width, width)
    local = sum(part.shape[0] for part in rows)
    number = gram_rows(width // BLOCK)[3]
    return pl.pallas_call(
        functools.partial(factor_kernel, len(rows), scale, 6),
        out_shape=[
            pltpu.HBM((local, width), F32),
            pltpu.HBM(square, F32),
        ],
        in_specs=[VMEM] * (8 + len(rows)),
        out_specs=[HBM, HBM],
        scratch_shapes=[
            pltpu.VMEM((number, BLOCK), F32),
            pltpu.VMEM(square, F32),
            pltpu.VMEM((width // 2, width // 2), F32),
            pltpu.VMEM((width // 2, width // 2), F32),
            pltpu.VMEM(square, F32),
            pltpu.VMEM((local, width), F32),
            pltpu.VMEM(square, F32),
            pltpu.SemaphoreType.DMA((7,)),
        ]
        + [pltpu.VMEM(square, BF16)] * 8,
        compiler_params=params(24 << 20),
    )(*pieces, *rows)


def body(tile_values, tile_places, tile_counts, sketch):
    tiles = tile_values[0, 0]
    size = tiles.shape[1]
    width = sketch.shape[1]
    row_devices = lax.axis_size("row")
    col_devices = lax.axis_size("col")
    local_rows = sketch.shape[0] // row_devices
    tile_rows = local_rows * col_devices // size
    panels = sketch.reshape(-1, size, width)
    places = tile_places[0, 0]
    scale = math.sqrt(local_rows * row_devices * col_devices)
    per_owner = tile_rows // col_devices
    cuts = sorted({0, per_owner // 6, per_owner * 5 // 6, per_owner})
    chunks = list(zip(cuts, cuts[1:]))
    early = chunks[:-1] or chunks
    late = chunks[len(early) :]

    def products(spans):
        out = tile_products(tile_counts, places, tiles, panels, tile_rows, tuple(spans))
        return out[: len(spans)], out[len(spans) :]

    def across_cores(send, keep):
        own = []
        for n in range(len(send)):
            if n == 1:
                *send[1:], core = lax.optimization_barrier((*send[1:], core))
            core = swapped(send[n], 0, 1)
            own.append(keep[n] + core)
        return own

    send, keep = products([(1, head, end) for head, end in early])
    own = across_cores(list(send), keep)
    across = [swapped(x, 0, 2) for x in own]
    places, own = lax.optimization_barrier((places, own))
    send, keep = products([(1, *chunk) for chunk in late] + [(0, *chunk) for chunk in chunks])
    send, keep, across[0] = lax.optimization_barrier((send, keep, across[0]))
    across += [swapped(x, 0, 2) for x in across_cores(list(send[: len(late)]), keep[: len(late)])]
    send, keep = send[len(late) :], keep[len(late) :]
    chunks = len(chunks)
    rows, grams = [], []
    for n in range(chunks):
        out = gram_chunk(keep[n], swapped(send[n], 0, 1), across[n], grams, n == chunks - 1)
        rows.append(out[0])
        grams.append(out[1])
    mine, theirs = gram_sum(*out[1:])
    basis, triangle = factor(mine + theirs, rows, scale)
    return basis, triangle


def solution(mesh):
    in_specs = (
        P("row", "col", None, None, None),
        P("row", "col", None, None),
        P("row", "col"),
        P("col", None),
    )
    out_specs = (P(("row", "col"), None), P())
    return jax.shard_map(body, mesh=mesh, in_specs=in_specs, out_specs=out_specs, check_vma=False)
```
